32 devices in a mesh: dp: 4 (over y, x), fsdp: 8 (over z, core).
Axes of the slice: x: 2, y: 2, z: 4, core: 2. Of those that a mesh axis runs over, the one named last changes fastest.
Arguments:
- x_big: bfloat16 [128, 14, 14, 384], P(('dp', 'fsdp')), may hold values from -6 to 6
- x_small: bfloat16 [384, 6, 6, 384], P(('dp', 'fsdp')), may hold values from -6 to 6
- cot_big: bfloat16 [128, 14, 14, 384], P(('dp', 'fsdp')), may hold values from -6 to 6
- cot_small: bfloat16 [384, 6, 6, 384], P(('dp', 'fsdp')), may hold values from -6 to 6
- counts: int32 [4, 8, 2], P('dp', 'fsdp'), may hold values from 1 to 12, as said below
- params: float32 [384, 4708], P('fsdp'), may hold values from -2 to 3
- first: float32 [384, 4708], P('fsdp')
- second: float32 [384, 4708], P('fsdp')
Outputs:
- out_big: bfloat16 [128, 14, 14, 384], P(('dp', 'fsdp'))
- out_small: bfloat16 [384, 6, 6, 384], P(('dp', 'fsdp'))
- grad_big: bfloat16 [128, 14, 14, 384], P(('dp', 'fsdp'))
- grad_small: bfloat16 [384, 6, 6, 384], P(('dp', 'fsdp'))
- new_params: float32 [384, 4708], P('fsdp')
- new_first: float32 [384, 4708], P('fsdp')
- new_second: float32 [384, 4708], P('fsdp')
- grad_norm: float32 [], replicated
The draws below stay inside these ranges and needn't reach their ends.
Inputs may be any that keep to these rules, and one draw needn't show every extreme that they name: counts[d, f, 0] is at most 4; live crops fill a device's first slots; some device has all its slots live.
All inputs are finite; a program needn't handle non-finite values.
Results may differ from the reference program's by a relative error of at most 0.023.
Values may be sent and summed in bfloat16 or wider, within the bound.
No kernel may reach another device: no remote copies, remote signals or barrier semaphores. Data moves between devices by JAX's collectives and lax.ppermute only.
A program may use at most 128 MiB of HBM per device.

```python
import math
import jax
import jax.numpy as jnp
from jax import lax

DIM = 384
FFN = 1536
H_BIG = 14
H_SMALL = 6
STEP = 10
B_BIG = 4
B_SMALL = 12
IMAGES_BIG = 128
IMAGES_SMALL = 384
PACKED = 4708
N_DP = 4
N_FSDP = 8


def moment_scale():
    base_size = 1.0 / math.sqrt(DIM * PACKED)
    matrix_cols = 4 * DIM + 4 + 2 * FFN
    return base_size * jnp.concatenate([jnp.ones((matrix_cols,), jnp.float32), jnp.full((PACKED - matrix_cols,), 4.0, jnp.float32)])


def draw_params(key, part):
    key = jax.random.fold_in(key, 11)
    key_mats, key_gain_one, key_gain_two, key_bias, key_up = jax.random.split(key, 5)
    span_cols = 4 * DIM + 4 + 2 * FFN + 83
    base_vals = jax.random.truncated_normal(key_mats, -4.0, 4.0, (DIM, span_cols), jnp.float32)
    spread = jnp.concatenate([jnp.full((4 * DIM + 4 + FFN,), DIM ** (-0.5), jnp.float32), jnp.full((FFN,), FFN ** (-0.5), jnp.float32), jnp.full((9,), 1.0 / 3.0, jnp.float32), jnp.full((25,), 0.2, jnp.float32), jnp.full((49,), 1.0 / 7.0, jnp.float32)])
    rising = 0.5 + 1.5 * jnp.arange(DIM, dtype=jnp.float32) / (DIM - 1)
    gain_one = rising * jax.random.uniform(key_gain_one, (DIM,), jnp.float32, 0.8, 1.2)
    gain_two = rising * jax.random.uniform(key_gain_two, (DIM,), jnp.float32, 0.8, 1.2)
    shifts = 0.3 * jax.random.truncated_normal(key_bias, -4.0, 4.0, (DIM, 7), jnp.float32)
    vectors = jnp.stack([gain_one, shifts[:, 0], shifts[:, 1], shifts[:, 2], shifts[:, 3], shifts[:, 4], gain_two, shifts[:, 5], shifts[:, 6]], axis=1)
    up_bias = 0.3 * jax.random.truncated_normal(key_up, -4.0, 4.0, (DIM, FFN // DIM), jnp.float32)
    return jnp.concatenate([base_vals * spread, vectors, up_bias], axis=1)


def draw_first(key, part):
    key = jax.random.fold_in(key, 12)
    base_vals = jax.random.truncated_normal(key, -4.0, 4.0, (DIM, PACKED), jnp.float32)
    return 0.11 * moment_scale() * base_vals


def draw_second(key, part):
    key = jax.random.fold_in(key, 13)
    factor = jnp.exp(jax.random.uniform(key, (DIM, PACKED), jnp.float32, math.log(0.5), math.log(8.0)))
    scale_row = moment_scale()
    return 0.001 / 0.999 * scale_row * scale_row * factor


def draw_counts(key, part):
    key = jax.random.fold_in(key, 14)
    position = jnp.arange(N_FSDP, dtype=jnp.int32)
    capacity = jnp.array([B_BIG, B_SMALL], jnp.int32)
    floor_vals = jnp.maximum(capacity // 3, 1)
    target = floor_vals[None, :] + (capacity - floor_vals)[None, :] * position[:, None] // max(N_FSDP - 1, 1)
    jitter = jax.random.randint(key, (N_DP, N_FSDP, 2), -1, 2)
    result = jnp.clip(target[None, :, :] + jitter, 1, capacity[None, None, :])
    result = result.at[0, N_FSDP - 1].set(capacity)
    return result.astype(jnp.int32)


def block_scale(stream_key, shape, shards, least, top_value):
    def one(axis_at, shards_of):
        draws = jax.random.uniform(jax.random.fold_in(jax.random.fold_in(stream_key, 6), axis_at), (shards_of,), jnp.float32, least / len(shards), top_value / len(shards))
        return jnp.repeat(jnp.exp(draws), shape[axis_at] // shards_of).reshape((-1,) + (1,) * (len(shape) - axis_at - 1))

    loudness = one(*shards[0])
    for cut in shards[1:]:
        loudness = loudness * one(*cut)
    return loudness


def bell_draw(key, shape, deviation, bound, shards=(), held_as=jnp.bfloat16):
    drawn = jax.random.normal(key, shape, jnp.float32) * deviation
    if len(shards) > 0:
        drawn = block_scale(key, shape, shards, -0.22, 0.18) * drawn
    return jnp.clip(drawn, min=-bound, max=bound).astype(held_as)


def setup_inputs(seed: int = 0) -> dict:
    keys = jax.random.split(jax.random.key(seed), 9)
    x_big = bell_draw(keys[0], (IMAGES_BIG, H_BIG, H_BIG, DIM), 1.0, 6.0, ((0, 32),))
    x_small = bell_draw(keys[1], (IMAGES_SMALL, H_SMALL, H_SMALL, DIM), 1.0, 6.0, ((0, 32),))
    cot_big = bell_draw(keys[2], (IMAGES_BIG, H_BIG, H_BIG, DIM), 1.0, 6.0, ((0, 32),))
    cot_small = bell_draw(keys[3], (IMAGES_SMALL, H_SMALL, H_SMALL, DIM), 1.0, 6.0, ((0, 32),))
    counts = draw_counts(jax.random.fold_in(keys[8], 71), 0)
    params = draw_params(jax.random.fold_in(keys[8], 71), 0)
    first = draw_first(jax.random.fold_in(keys[8], 71), 0)
    second = draw_second(jax.random.fold_in(keys[8], 71), 0)
    return dict(x_big=x_big, x_small=x_small, cot_big=cot_big, cot_small=cot_small, counts=counts, params=params, first=first, second=second)


@jax.custom_vjp
def low(v):
    return lax.optimization_barrier(v.astype(jnp.bfloat16)).astype(jnp.float32)

@jax.custom_vjp
def low_back(v):
    return v

def low_keep(v):
    return (low(v), None)

def low_pass(kept, grad):
    return (grad,)

def back_keep(v):
    return (v, None)

def back_low(kept, grad):
    return (low(grad),)
low.defvjp(low_keep, low_pass)
low_back.defvjp(back_keep, back_low)
CLIP_NORM = 1.0
BETA_ONE = 0.9
BETA_TWO = 0.999
LEARN_RATE = 0.05
DECAY_RATE = 0.05
ADAM_EPS = 1e-08
KERNEL_SIDES = (3, 5, 7)

def column_starts(model_width, hidden_units):
    mod_start = 2 * model_width + 4
    out_start = mod_start + model_width
    up_start = out_start + model_width
    down_start = up_start + hidden_units
    taps_start = down_start + hidden_units
    vec_start = taps_start + 83
    bias_start = vec_start + 9
    packed_end = bias_start + hidden_units // model_width
    return (mod_start, out_start, up_start, down_start, taps_start, vec_start, bias_start, packed_end)

def layer_norm(values, gain_vec, shift_vec):
    center = values - lax.optimization_barrier(jnp.mean(values, axis=-1, keepdims=True))
    spread = lax.optimization_barrier(jnp.mean(center * center, axis=-1, keepdims=True))
    return center * lax.rsqrt(spread + 1e-05) * gain_vec + shift_vec

def depthwise(field_in, kernel, kernel_side):
    margin = kernel_side // 2
    channels = field_in.shape[-1]
    filters = kernel.T.reshape(kernel_side, kernel_side, 1, channels)
    return lax.conv_general_dilated(field_in, filters, (1, 1), ((margin, margin), (margin, margin)), dimension_numbers=('NHWC', 'HWIO', 'NHWC'), feature_group_count=channels, precision=lax.Precision.HIGHEST)

def modulate(context, gate_vals, kernels):
    total = jnp.zeros_like(context)
    tap_offset = 0
    for level_index, kernel_side in enumerate(KERNEL_SIDES):
        context = jax.nn.gelu(depthwise(context, kernels[:, tap_offset:tap_offset + kernel_side * kernel_side], kernel_side), approximate=False)
        tap_offset = tap_offset + kernel_side * kernel_side
        total = total + context * gate_vals[..., level_index:level_index + 1]
    summary = jax.nn.gelu(lax.optimization_barrier(jnp.mean(context, axis=(1, 2), keepdims=True)), approximate=False)
    return total + summary * gate_vals[..., 3:4]

def mixing(context, gate_vals, kernels, big_shape, small_shape):
    model_width = context.shape[1]
    rows_big = big_shape[0] * big_shape[1] * big_shape[2]
    part_big = modulate(context[:rows_big].reshape(big_shape), gate_vals[:rows_big].reshape(tuple(big_shape[:3]) + (4,)), kernels)
    part_small = modulate(context[rows_big:].reshape(small_shape), gate_vals[rows_big:].reshape(tuple(small_shape[:3]) + (4,)), kernels)
    return jnp.concatenate([part_big.reshape(-1, model_width), part_small.reshape(-1, model_width)], axis=0)

def matmul(left, right):
    return jnp.dot(left, right, precision=lax.Precision.HIGHEST, preferred_element_type=jnp.float32)

def matmul_t(left, right):
    return lax.dot_general(left, right, (((1,), (1,)), ((), ())), precision=lax.Precision.HIGHEST, preferred_element_type=jnp.float32)

def block_forward(big, small, params):
    weights = low(params)
    model_width = big.shape[-1]
    hidden_units = FFN
    mod_start, out_start, up_start, down_start, taps_start, vec_start, bias_start, packed_end = column_starts(model_width, hidden_units)
    vectors = weights[:, vec_start:vec_start + 9]
    tokens = jnp.concatenate([big.reshape(-1, model_width), small.reshape(-1, model_width)], axis=0)
    normed = low(layer_norm(tokens, vectors[:, 0], vectors[:, 1]))
    in_bias = jnp.concatenate([vectors[:, 2], vectors[:, 3], jnp.zeros((4,), jnp.float32)])
    projected = low_back(matmul(normed, weights[:, :mod_start])) + in_bias
    queries = projected[:, :model_width]
    context = projected[:, model_width:2 * model_width]
    gate_vals = projected[:, 2 * model_width:]
    mixed = low(mixing(context, gate_vals, weights[:, taps_start:vec_start], big.shape, small.shape))
    modulator = low_back(matmul(mixed, weights[:, mod_start:out_start])) + vectors[:, 4]
    product = low(queries * modulator)
    resid = tokens + low_back(matmul(product, weights[:, out_start:up_start])) + vectors[:, 5]
    normed_two = low(layer_norm(resid, vectors[:, 6], vectors[:, 7]))
    up_bias = weights[:, bias_start:packed_end].reshape(hidden_units)
    pre_act = low_back(matmul(normed_two, weights[:, up_start:down_start])) + up_bias
    activated = low(jax.nn.gelu(pre_act, approximate=False))
    return resid + low_back(matmul_t(activated, weights[:, down_start:taps_start])) + vectors[:, 8]

def adam_update(params, grads, first, second, scale):
    clipped = grads * scale
    first_new = BETA_ONE * first + (1.0 - BETA_ONE) * clipped
    second_new = BETA_TWO * second + (1.0 - BETA_TWO) * clipped * clipped
    first_hat = first_new / (1.0 - BETA_ONE ** STEP)
    second_hat = second_new / (1.0 - BETA_TWO ** STEP)
    params_new = params - LEARN_RATE * (first_hat / (jnp.sqrt(second_hat) + ADAM_EPS) + DECAY_RATE * params)
    return (params_new, first_new, second_new)

def reference(x_big, x_small, cot_big, cot_small, counts, params, first, second):
    devices = N_DP * N_FSDP
    big_all = x_big.astype(jnp.float32).reshape((devices, B_BIG) + x_big.shape[1:])
    small_all = x_small.astype(jnp.float32).reshape((devices, B_SMALL) + x_small.shape[1:])
    cot_big_all = cot_big.astype(jnp.float32).reshape((devices, B_BIG) + cot_big.shape[1:])
    cot_small_all = cot_small.astype(jnp.float32).reshape((devices, B_SMALL) + cot_small.shape[1:])
    count_rows = counts.reshape(devices, 2)
    rows_big = B_BIG * H_BIG * H_BIG

    def device_step(total, item):
        big, small, cot_one, cot_two, count_pair = item
        live_big = (jnp.arange(B_BIG) < count_pair[0]).astype(jnp.float32)
        live_small = (jnp.arange(B_SMALL) < count_pair[1]).astype(jnp.float32)
        output, pull = jax.vjp(block_forward, big, small, params)
        weighted = jnp.concatenate([(cot_one * live_big[:, None, None, None]).reshape(-1, DIM), (cot_two * live_small[:, None, None, None]).reshape(-1, DIM)], axis=0)
        grad_one, grad_two, grad_params = pull(weighted)
        result = (output[:rows_big].reshape(big.shape).astype(jnp.bfloat16), output[rows_big:].reshape(small.shape).astype(jnp.bfloat16), grad_one.astype(jnp.bfloat16), grad_two.astype(jnp.bfloat16))
        return (total + grad_params, result)
    grads, stacked = lax.scan(device_step, jnp.zeros(params.shape, jnp.float32), (big_all, small_all, cot_big_all, cot_small_all, count_rows))
    out_big = stacked[0].reshape(x_big.shape)
    out_small = stacked[1].reshape(x_small.shape)
    grad_big = stacked[2].reshape(x_big.shape)
    grad_small = stacked[3].reshape(x_small.shape)
    grad_norm = jnp.sqrt(jnp.sum(grads * grads))
    scale = jnp.minimum(1.0, CLIP_NORM / (grad_norm + 1e-06))
    new_params, new_first, new_second = adam_update(params, grads, first, second, scale)
    return (out_big, out_small, grad_big, grad_small, new_params, new_first, new_second, grad_norm)
```

```python
from functools import partial

import jax
import jax.numpy as jnp
import numpy as np
from jax import lax
from jax.experimental import pallas as pl
from jax.experimental.pallas import tpu as pltpu
from jax.sharding import PartitionSpec as P

FFN = 1536
STEP = 10
CLIP_NORM = 1.0
BETA_ONE = 0.9
BETA_TWO = 0.999
LEARN_RATE = 0.05
DECAY_RATE = 0.05
ADAM_EPS = 1e-08
KERNEL_SIDES = (3, 5, 7)
F32 = jnp.float32
BF16 = jnp.bfloat16
VMEM_BYTES = 58 * 2**20

SLOT = 16


def up_to(value, step):
    return -(-value // step) * step


class Plan:
    def __init__(self, big_shape, small_shape):
        self.n_big, self.side_big = big_shape[0], big_shape[1]
        self.n_small, self.side_small = small_shape[0], small_shape[1]
        self.width = big_shape[3]
        self.pix_big = self.side_big**2
        self.pix_small = self.side_small**2
        self.rows_big = up_to(self.pix_big, SLOT)
        self.group = 4
        while (self.group * self.pix_small) % SLOT:
            self.group += 1
        self.n_groups = self.n_small // self.group
        assert self.n_groups * self.group == self.n_small
        self.rows_small = self.group * self.pix_small
        self.small_at = self.n_big * self.rows_big
        self.used = self.small_at + self.n_groups * self.rows_small
        self.rows = up_to(self.used, 128)
        self.n_images = self.n_big + self.n_small
        self.image_rows = up_to(self.n_images, SLOT)


def half_spectrum(size):
    reps = []
    for u in range(size):
        for v in range(size):
            other = ((-u) % size, (-v) % size)
            if (u, v) <= other:
                reps.append((u, v, 1.0 if (u, v) == other else 2.0))
    return np.array(reps)


def transform_pair(side, kernel_side, copies):
    margin = kernel_side // 2
    size = side + margin
    reps = half_spectrum(size)
    count = len(reps)
    freq = 2 * np.pi * reps[:, :2] / size
    grid = np.array([(i, j) for i in range(side) for j in range(side)], float)
    lags = np.array([(i - margin, j - margin) for i in range(kernel_side) for j in range(kernel_side)], float)
    phase = freq @ grid.T
    lag_phase = freq @ lags.T
    weight = reps[:, 2:3] / size**2
    pix = side * side
    half = up_to(copies * count, SLOT)
    rows = up_to(copies * pix, SLOT)
    forward = np.zeros((2 * half, rows))
    inverse = np.zeros((rows, 2 * half))
    taps = np.zeros((2 * half, kernel_side**2))
    back = np.zeros((kernel_side**2, 2 * half))
    for one in range(copies):
        low, col = one * count, one * pix
        forward[low : low + count, col : col + pix] = np.cos(phase)
        forward[half + low : half + low + count, col : col + pix] = -np.sin(phase)
        inverse[col : col + pix, low : low + count] = (weight * np.cos(phase)).T
        inverse[col : col + pix, half + low : half + low + count] = -(weight * np.sin(phase)).T
        taps[low : low + count] = np.cos(lag_phase)
        taps[half + low : half + low + count] = np.sin(lag_phase)
        back[:, low : low + count] = (weight * np.cos(lag_phase)).T
        back[:, half + low : half + low + count] = -(weight * np.sin(lag_phase)).T
    return forward, inverse, taps, back


TABLE = 128
GATES_AT = 0
TAPS_AT = 4
VECS_AT = 87
BIAS_AT = 96


def low_np(values):
    return jnp.asarray(values, F32).astype(BF16)


def high_and_rest(values):
    high = values.astype(np.float32).astype(jnp.bfloat16)
    rest = (values - high.astype(np.float64)).astype(np.float32).astype(jnp.bfloat16)
    return jnp.asarray(high), jnp.asarray(rest)


def constants(plan):
    consts = {}
    tap_at = TAPS_AT
    for level, kernel_side in enumerate(KERNEL_SIDES):
        for kind, side, copies in (("b", plan.side_big, 1), ("s", plan.side_small, plan.group)):
            forward, inverse, taps, back = transform_pair(side, kernel_side, copies)
            wide = np.zeros((taps.shape[0], TABLE))
            wide[:, tap_at : tap_at + kernel_side**2] = taps
            tall = np.zeros((TABLE, taps.shape[0]))
            tall[tap_at : tap_at + kernel_side**2] = back
            consts["f" + kind + str(level)] = low_np(forward)
            consts["g" + kind + str(level)] = low_np(inverse)
            high, rest = high_and_rest(wide)
            consts["k" + kind + str(level)] = jnp.concatenate([high, rest], axis=1)
            consts["t" + kind + str(level)] = low_np(tall)
        tap_at += kernel_side**2
    pick = np.zeros((plan.image_rows, plan.rows))
    for one in range(plan.n_big):
        pick[one, one * plan.rows_big : one * plan.rows_big + plan.pix_big] = 1.0
    for one in range(plan.n_small):
        at = plan.small_at + one * plan.pix_small
        pick[plan.n_big + one, at : at + plan.pix_small] = 1.0
    consts["pick"] = low_np(pick)
    consts["spread"] = low_np(pick.T)
    consts["eye"] = low_np(np.eye(TABLE))
    lanes = np.zeros((FFN, plan.width))
    lanes[np.arange(FFN), np.arange(FFN) // (FFN // plan.width)] = 1.0
    consts["lanes"] = low_np(lanes)
    return consts


def dot(left, right):
    return jnp.dot(left, right, preferred_element_type=F32)


def dot_nt(left, right):
    return lax.dot_general(left, right, (((1,), (1,)), ((), ())), preferred_element_type=F32)


def dot_tn(left, right):
    return lax.dot_general(left, right, (((0,), (0,)), ((), ())), preferred_element_type=F32)


def each_rows(count, tile, body):
    def step(index, carry):
        body(pl.ds(pl.multiple_of(index * tile, tile), tile))
        return carry

    lax.fori_loop(0, count // tile, step, 0)


def gelu_and_slope(values):
    chance = 0.5 + 0.5 * lax.erf(values * 0.7071067811865476)
    bell = jnp.exp(values * values * -0.5) * 0.3989422804014327
    return values * chance, chance + values * bell


def call(body, outs, names, scratch, args, cost):
    def kernel(*refs):
        body(dict(zip(names, refs)))

    return pl.pallas_call(
        kernel,
        out_shape=[jax.ShapeDtypeStruct(shape, dtype) for shape, dtype in outs],
        scratch_shapes=[pltpu.VMEM(shape, dtype) for shape, dtype in scratch],
        compiler_params=pltpu.CompilerParams(vmem_limit_bytes=VMEM_BYTES),
        cost_estimate=pl.CostEstimate(flops=cost, bytes_accessed=cost // 200, transcendentals=0),
    )(*args)


def run(body, inputs, outputs, scratch, cost=10**9):
    names = list(inputs) + list(outputs) + list(scratch)
    results = call(body, list(outputs.values()), names, list(scratch.values()), list(inputs.values()), cost)
    return dict(zip(outputs, results))


def units(plan):
    for one in range(plan.n_big):
        yield "b", slice(one * plan.rows_big, (one + 1) * plan.rows_big)
    for one in range(plan.n_groups):
        at = plan.small_at + one * plan.rows_small
        yield "s", slice(at, at + plan.rows_small)


def spectra_of_taps(plan, refs, table):
    for level in range(3):
        for kind in "bs":
            name = "k" + kind + str(level)
            refs["h" + kind + str(level)][...] = dot_nt(refs[name][:, :TABLE], table) + dot_nt(
                refs[name][:, TABLE:], table
            )


def image_scale(plan):
    row = lax.broadcasted_iota(jnp.int32, (plan.image_rows, 1), 0)
    return jnp.where(row < plan.n_big, 1.0 / plan.pix_big, 1.0 / plan.pix_small).astype(F32)


def forward_mix(plan, refs):
    rows, width = plan.rows, plan.width
    table = refs["wa"][:, 2 * width :]
    refs["vec"][...] = dot_nt(refs["eye"][...], table)
    hidden = FFN
    ratio = hidden // width
    spread = dot_nt(refs["vec"][BIAS_AT : BIAS_AT + 16, :].astype(BF16), refs["lanes"][...])
    row = lax.broadcasted_iota(jnp.int32, (16, hidden), 0)
    lane = lax.broadcasted_iota(jnp.int32, (16, hidden), 1)
    picked = jnp.where(lax.rem(lane, ratio) == row, spread, 0.0)
    refs["upb"][...] = jnp.broadcast_to(jnp.sum(picked, axis=0, keepdims=True), (8, hidden))
    spectra_of_taps(plan, refs, table)
    gain = refs["vec"][VECS_AT : VECS_AT + 1, :]
    shift = refs["vec"][VECS_AT + 1 : VECS_AT + 2, :]

    def norm_rows(at):
        values = refs["x"][at, :].astype(F32)
        center = values - jnp.mean(values, axis=-1, keepdims=True)
        scale = lax.rsqrt(jnp.mean(center * center, axis=-1, keepdims=True) + 1e-05)
        refs["normed"][at, :] = (center * scale * gain + shift).astype(BF16)

    each_rows(rows, 64, norm_rows)
    for step in range(rows // 256):
        at = slice(step * 256, step * 256 + 256)
        part = dot(refs["normed"][at, :], refs["wa"][...])
        refs["q"][at, :] = (part[:, :width] + refs["vec"][VECS_AT + 2 : VECS_AT + 3, :]).astype(BF16)
        refs["c"][0, at, :] = (part[:, width : 2 * width] + refs["vec"][VECS_AT + 3 : VECS_AT + 4, :]).astype(BF16)
        refs["gate"][at, :] = part[:, 2 * width :]
    refs["c"][1:, plan.used :, :] = jnp.zeros((3, rows - plan.used, width), BF16)
    refs["gp"][:, plan.used :, :] = jnp.zeros((3, rows - plan.used, width), BF16)
    for level in range(3):
        for kind, at in units(plan):
            count = refs["f" + kind + str(level)].shape[0]
            half = count // 2
            refs["wave"][:count, :] = dot(refs["f" + kind + str(level)][...], refs["c"][level, at, :])
            taps = refs["h" + kind + str(level)]
            for low in range(0, half, 16):
                re, im = slice(low, low + 16), slice(half + low, half + low + 16)
                wave_re, wave_im = refs["wave"][re, :], refs["wave"][im, :]
                tap_re, tap_im = taps[re, :], taps[im, :]
                refs["wave_low"][re, :] = (wave_re * tap_re - wave_im * tap_im).astype(BF16)
                refs["wave_low"][im, :] = (wave_re * tap_im + wave_im * tap_re).astype(BF16)
            length = at.stop - at.start
            refs["field"][:length, :] = dot(refs["g" + kind + str(level)][...], refs["wave_low"][:count, :])
            for low in range(0, length, 16):
                into = slice(at.start + low, at.start + low + 16)
                value, slope = gelu_and_slope(refs["field"][low : low + 16, :])
                refs["c"][level + 1, into, :] = value.astype(BF16)
                refs["gp"][level, into, :] = slope.astype(BF16)
    mean = dot(refs["pick"][...], refs["c"][3]) * image_scale(plan)
    summary, slope = gelu_and_slope(mean)
    refs["sum"][0] = summary
    refs["sum"][1] = slope
    summary_low = summary.astype(BF16)

    def mix_rows(at):
        gate = refs["gate"][at, :]
        total = dot(refs["spread"][at, :], summary_low) * gate[:, 3:4]
        for level in range(3):
            total += refs["c"][level + 1, at, :].astype(F32) * gate[:, level : level + 1]
        refs["mixed"][at, :] = total.astype(BF16)

    each_rows(rows, 64, mix_rows)


def mix_scratch(plan, consts):
    scratch = {}
    for level in range(3):
        for kind in "bs":
            scratch["h" + kind + str(level)] = ((consts["f" + kind + str(level)].shape[0], plan.width), F32)
    return scratch


def mix_forward(plan, consts, x_rows, wa):
    rows, width = plan.rows, plan.width
    waves = max(consts["f" + kind + str(level)].shape[0] for level in range(3) for kind in "bs")
    keys = [k + kind + str(level) for level in range(3) for kind in "bs" for k in "fgk"]
    inputs = dict(x=x_rows, wa=wa, **{k: consts[k] for k in keys + ["pick", "spread", "eye", "lanes"]})
    outputs = dict(
        normed=((rows, width), BF16),
        q=((rows, width), BF16),
        c=((4, rows, width), BF16),
        gp=((3, rows, width), BF16),
        mixed=((rows, width), BF16),
        gate=((rows, TABLE), F32),
        vec=((TABLE, width), F32),
        upb=((8, FFN), F32),
        sum=((2, plan.image_rows, width), F32),
    )
    scratch = dict(
        wave=((waves, width), F32),
        wave_low=((waves, width), BF16),
        field=((max(plan.rows_big, plan.rows_small), width), F32),
        **mix_scratch(plan, consts),
    )
    return run(partial(forward_mix, plan), inputs, outputs, scratch)


def middle(plan, refs):
    rows, width, hidden = plan.rows, plan.width, FFN
    vec = lambda index: refs["vec"][VECS_AT + index : VECS_AT + index + 1, :]
    for step in range(rows // 256):
        at = slice(step * 256, step * 256 + 256)
        modulator = dot(refs["mixed"][at, :], refs["wm"][...]) + vec(4)
        refs["mod"][at, :] = modulator
        refs["prod"][at, :] = (refs["q"][at, :].astype(F32) * modulator).astype(BF16)
    for step in range(rows // 256):
        at = slice(step * 256, step * 256 + 256)
        refs["resid"][at, :] = refs["x"][at, :].astype(F32) + dot(refs["prod"][at, :], refs["wo"][...]) + vec(5)

    def norm_rows(at):
        values = refs["resid"][at, :]
        center = values - jnp.mean(values, axis=-1, keepdims=True)
        scale = lax.rsqrt(jnp.mean(center * center, axis=-1, keepdims=True) + 1e-05)
        unit = center * scale
        refs["unit"][at, :] = unit
        refs["scale"][at, :] = jnp.broadcast_to(scale, (scale.shape[0], TABLE))
        refs["n2"][at, :] = (unit * vec(6) + vec(7)).astype(BF16)

    each_rows(rows, 64, norm_rows)
    for low in range(0, hidden, 256):
        lanes = slice(low, low + 256)
        refs["pa"][...] = dot(refs["n2"][...], refs["wu"][:, lanes]) + refs["upb"][0:1, lanes]
        refs["ga"][...] = dot(refs["wl"][...], refs["wd"][:, lanes])

        def act_rows(index, total):
            at = pl.ds(pl.multiple_of(index * 32, 32), 32)
            value, slope = gelu_and_slope(refs["pa"][at, :])
            grad = refs["ga"][at, :] * slope
            refs["act"][at, lanes] = value.astype(BF16)
            refs["pre"][at, lanes] = grad.astype(BF16)
            return total + grad[0:8] + grad[8:16] + grad[16:24] + grad[24:32]

        total = lax.fori_loop(0, rows // 32, act_rows, jnp.zeros((8, 256), F32))
        refs["gub"][0:1, lanes] = jnp.sum(total, axis=0, keepdims=True)
    for step in range(rows // 256):
        at = slice(step * 256, step * 256 + 256)
        refs["out"][at, :] = (
            refs["resid"][at, :] + dot_nt(refs["act"][at, :], refs["wd"][...]) + vec(8)
        ).astype(BF16)
        refs["gn"][at, :] = dot_nt(refs["pre"][at, :], refs["wu"][...])
    for low in range(0, hidden, 256):
        lanes = slice(low, low + 256)
        refs["gu"][:, lanes] = dot_tn(refs["n2"][...], refs["pre"][:, lanes]).astype(BF16)
        refs["gd"][:, lanes] = dot_tn(refs["wl"][...], refs["act"][:, lanes]).astype(BF16)

    def fold(values):
        total = values[0:8]
        for low in range(8, values.shape[0], 8):
            total = total + values[low : low + 8]
        return total

    zero = jnp.zeros((8, width), F32)

    def norm_back(index, totals):
        at = pl.ds(pl.multiple_of(index * 32, 32), 32)
        grad = refs["gn"][at, :]
        unit = refs["unit"][at, :]
        weighted = refs["wl"][at, :].astype(F32)
        grad_unit = grad * unit
        gained = grad * vec(6)
        mean_one = jnp.mean(gained, axis=-1, keepdims=True)
        mean_two = jnp.mean(gained * unit, axis=-1, keepdims=True)
        result = weighted + refs["scale"][at, 0:1] * (gained - mean_one - unit * mean_two)
        refs["gres"][at, :] = result
        refs["glow"][at, :] = result.astype(BF16)
        return (
            totals[0] + fold(grad_unit),
            totals[1] + fold(grad),
            totals[2] + fold(result),
            totals[3] + fold(weighted),
        )

    totals = lax.fori_loop(0, rows // 32, norm_back, (zero,) * 4)
    refs["gv"][...] = jnp.zeros(refs["gv"].shape, F32)
    for at, total in zip((6, 7, 5, 8), totals):
        refs["gv"][at : at + 1, :] = jnp.sum(total, axis=0, keepdims=True)
    for step in range(rows // 256):
        at = slice(step * 256, step * 256 + 256)
        refs["gn"][at, :] = dot_nt(refs["glow"][at, :], refs["wo"][...])

    def product_back(index, totals):
        at = pl.ds(pl.multiple_of(index * 32, 32), 32)
        grad = refs["gn"][at, :]
        grad_query = grad * refs["mod"][at, :]
        grad_mod = grad * refs["q"][at, :].astype(F32)
        refs["gq"][at, :] = grad_query.astype(BF16)
        refs["gmod"][at, :] = grad_mod.astype(BF16)
        return totals[0] + fold(grad_query), totals[1] + fold(grad_mod)

    totals = lax.fori_loop(0, rows // 32, product_back, (zero,) * 2)
    for at, total in zip((2, 4), totals):
        refs["gv"][at : at + 1, :] = jnp.sum(total, axis=0, keepdims=True)
    for step in range(rows // 256):
        at = slice(step * 256, step * 256 + 256)
        refs["gmix"][at, :] = dot_nt(refs["gmod"][at, :], refs["wm"][...]).astype(BF16)
    refs["go"][...] = dot_tn(refs["prod"][...], refs["glow"][...]).astype(BF16)
    refs["gm"][...] = dot_tn(refs["mixed"][...], refs["gmod"][...]).astype(BF16)
    refs["gqw"][...] = dot_tn(refs["normed"][...], refs["gq"][...]).astype(BF16)
    ratio = hidden // width
    row = lax.broadcasted_iota(jnp.int32, (16, hidden), 0)
    lane = lax.broadcasted_iota(jnp.int32, (16, hidden), 1)
    picked = jnp.where(lax.rem(lane, ratio) == row, refs["gub"][0:1, :], 0.0).astype(BF16)
    refs["gv"][16:32, :] = dot(picked, refs["lanes"][...])


def middle_pass(plan, consts, x_rows, wl, first, weights):
    rows, width, hidden = plan.rows, plan.width, FFN
    inputs = dict(
        x=x_rows,
        wl=wl,
        **{k: first[k] for k in ("normed", "q", "mixed", "vec", "upb")},
        **weights,
        lanes=consts["lanes"],
    )
    token = ((rows, width), BF16)
    outputs = dict(
        out=token,
        gu=((width, hidden), BF16),
        gd=((width, hidden), BF16),
        go=((width, width), BF16),
        gm=((width, width), BF16),
        gqw=((width, width), BF16),
        gq=token,
        gmix=token,
        gres=((rows, width), F32),
        gv=((32, width), F32),
    )
    wide = ((rows, hidden), BF16)
    field = ((rows, width), F32)
    scratch = dict(
        mod=field,
        prod=token,
        resid=field,
        unit=field,
        scale=((rows, TABLE), F32),
        n2=token,
        pa=((rows, 256), F32),
        ga=((rows, 256), F32),
        act=wide,
        pre=wide,
        gub=((8, hidden), F32),
        gn=field,
        glow=token,
        gmod=token,
    )
    return run(partial(middle, plan), inputs, outputs, scratch)


def backward_mix(plan, refs):
    rows, width = plan.rows, plan.width
    table = refs["wa"][:, 2 * width :]
    spectra_of_taps(plan, refs, table)
    scale = image_scale(plan)
    summary_low = refs["sum"][0].astype(BF16)
    lane = lax.broadcasted_iota(jnp.int32, (1, TABLE), 1)

    def gate_rows(at):
        gate = refs["gate"][at, :]
        grad = refs["gmix"][at, :].astype(F32)
        spread = dot(refs["spread"][at, :], summary_low)
        result = jnp.where(lane == 3, jnp.sum(grad * spread, axis=-1, keepdims=True), 0.0)
        for level in range(3):
            part = jnp.sum(grad * refs["c"][level + 1, at, :].astype(F32), axis=-1, keepdims=True)
            result = jnp.where(lane == level, part, result)
        refs["ggate"][at, :] = result.astype(BF16)
        refs["gc"][at, :] = grad * gate[:, 2:3]
        refs["tmp"][at, :] = (grad * gate[:, 3:4]).astype(BF16)

    each_rows(rows, 64, gate_rows)
    grad_summary = dot(refs["pick"][...], refs["tmp"][...]) * refs["sum"][1] * scale
    grad_summary_low = grad_summary.astype(BF16)
    taps_total = jnp.zeros((TABLE, width), F32)
    for level in (2, 1, 0):

        def pre_rows(at):
            grad = refs["gc"][at, :]
            if level == 2:
                grad = grad + dot(refs["spread"][at, :], grad_summary_low)
            refs["tmp"][at, :] = (grad * refs["gp"][level, at, :].astype(F32)).astype(BF16)

        each_rows(rows, 64, pre_rows)
        seen = set()
        for kind, at in units(plan):
            name = kind + str(level)
            count = refs["f" + name].shape[0]
            half = count // 2
            refs["wave"][:count, :] = dot(refs["f" + name][...], refs["c"][level, at, :])
            refs["gwave"][:count, :] = dot(refs["f" + name][...], refs["tmp"][at, :])
            taps = refs["h" + name]
            cross = refs["x" + kind]
            for low in range(0, half, 16):
                re, im = slice(low, low + 16), slice(half + low, half + low + 16)
                wave_re, wave_im = refs["wave"][re, :], refs["wave"][im, :]
                grad_re, grad_im = refs["gwave"][re, :], refs["gwave"][im, :]
                tap_re, tap_im = taps[re, :], taps[im, :]
                refs["wave_low"][re, :] = (grad_re * tap_re + grad_im * tap_im).astype(BF16)
                refs["wave_low"][im, :] = (grad_im * tap_re - grad_re * tap_im).astype(BF16)
                cross_re = grad_re * wave_re + grad_im * wave_im
                cross_im = grad_re * wave_im - grad_im * wave_re
                if kind in seen:
                    cross_re = cross_re + cross[re, :]
                    cross_im = cross_im + cross[im, :]
                cross[re, :] = cross_re
                cross[im, :] = cross_im
            seen.add(kind)
            length = at.stop - at.start
            back = dot(refs["g" + name][...], refs["wave_low"][:count, :])
            if level:
                for low in range(0, length, 16):
                    into = slice(at.start + low, at.start + low + 16)
                    direct = refs["gmix"][into, :].astype(F32) * refs["gate"][into, level - 1 : level]
                    refs["gc"][into, :] = back[low : low + 16] + direct
            else:
                refs["gc"][at, :] = back
        for kind in "bs":
            name = kind + str(level)
            count = refs["f" + name].shape[0]
            taps_total = taps_total + dot(refs["t" + name][...], refs["x" + kind][:count, :].astype(BF16))
    refs["gtab"][...] = taps_total
    refs["gc"][plan.used :, :] = jnp.zeros((rows - plan.used, width), F32)

    def fold(values):
        total = values[0:8]
        for low in range(8, values.shape[0], 8):
            total = total + values[low : low + 8]
        return total

    zero = jnp.zeros((8, width), F32)

    def low_rows(index, total):
        at = pl.ds(pl.multiple_of(index * 32, 32), 32)
        grad = refs["gc"][at, :]
        refs["tmp"][at, :] = grad.astype(BF16)
        return total + fold(grad)

    context_total = lax.fori_loop(0, rows // 32, low_rows, zero)
    gain = refs["vec"][VECS_AT : VECS_AT + 1, :]
    for step in range(rows // 256):
        at = slice(step * 256, step * 256 + 256)
        refs["gc"][at, :] = (
            dot_nt(refs["gq"][at, :], refs["wa"][:, :width])
            + dot_nt(refs["tmp"][at, :], refs["wa"][:, width : 2 * width])
            + dot_nt(refs["ggate"][at, :], table)
        )

    def norm_back(index, totals):
        at = pl.ds(pl.multiple_of(index * 32, 32), 32)
        values = refs["x"][at, :].astype(F32)
        center = values - jnp.mean(values, axis=-1, keepdims=True)
        scale_row = lax.rsqrt(jnp.mean(center * center, axis=-1, keepdims=True) + 1e-05)
        unit = center * scale_row
        grad = refs["gc"][at, :]
        gained = grad * gain
        mean_one = jnp.mean(gained, axis=-1, keepdims=True)
        mean_two = jnp.mean(gained * unit, axis=-1, keepdims=True)
        result = refs["gres"][at, :] + scale_row * (gained - mean_one - unit * mean_two)
        refs["gx"][at, :] = result.astype(BF16)
        return totals[0] + fold(grad * unit), totals[1] + fold(grad)

    totals = lax.fori_loop(0, rows // 32, norm_back, (zero,) * 2)
    refs["gtab"][VECS_AT : VECS_AT + 9, :] = refs["gv"][0:9, :]
    refs["gtab"][VECS_AT : VECS_AT + 1, :] = jnp.sum(totals[0], axis=0, keepdims=True)
    refs["gtab"][VECS_AT + 1 : VECS_AT + 2, :] = jnp.sum(totals[1], axis=0, keepdims=True)
    refs["gtab"][VECS_AT + 3 : VECS_AT + 4, :] = jnp.sum(context_total, axis=0, keepdims=True)
    refs["gtab"][BIAS_AT : BIAS_AT + 4, :] = refs["gv"][16:20, :]
    refs["gct"][:, :width] = dot_tn(refs["normed"][...], refs["tmp"][...]).astype(BF16)
    refs["gct"][:, width:] = (
        dot_tn(refs["normed"][...], refs["ggate"][...])
        + dot_tn(refs["gtab"][...].astype(BF16), refs["eye"][...])
    ).astype(BF16)


def mix_backward(plan, consts, x_rows, wa, first, mid):
    rows, width = plan.rows, plan.width
    waves = max(consts["f" + kind + str(level)].shape[0] for level in range(3) for kind in "bs")
    keys = [k + kind + str(level) for level in range(3) for kind in "bs" for k in "fgkt"]
    inputs = dict(
        x=x_rows,
        wa=wa,
        **{k: first[k] for k in ("normed", "c", "gp", "gate", "vec", "sum")},
        **{k: mid[k] for k in ("gq", "gmix", "gres", "gv")},
        **{k: consts[k] for k in keys + ["pick", "spread", "eye"]},
    )
    outputs = dict(gx=((rows, width), BF16), gct=((width, width + TABLE), BF16))
    scratch = dict(
        wave=((waves, width), F32),
        gwave=((waves, width), F32),
        wave_low=((waves, width), BF16),
        xb=((waves, width), F32),
        xs=((waves, width), F32),
        gc=((rows, width), F32),
        tmp=((rows, width), BF16),
        ggate=((rows, TABLE), BF16),
        gtab=((TABLE, width), F32),
        **mix_scratch(plan, consts),
    )
    return run(partial(backward_mix, plan), inputs, outputs, scratch)


def adam_update(params, grads, first, second, scale):
    clipped = grads * scale
    first_new = BETA_ONE * first + (1.0 - BETA_ONE) * clipped
    second_new = BETA_TWO * second + (1.0 - BETA_TWO) * clipped * clipped
    first_hat = first_new / (1.0 - BETA_ONE**STEP)
    second_hat = second_new / (1.0 - BETA_TWO**STEP)
    params_new = params - LEARN_RATE * (
        first_hat / (jnp.sqrt(second_hat) + ADAM_EPS) + DECAY_RATE * params
    )
    return (params_new, first_new, second_new)


def to_rows(plan, big, small):
    width = plan.width
    padded = jnp.pad(
        big.reshape(plan.n_big, plan.pix_big, width), ((0, 0), (0, plan.rows_big - plan.pix_big), (0, 0))
    )
    return jnp.concatenate(
        [
            padded.reshape(plan.small_at, width),
            small.reshape(-1, width),
            jnp.zeros((plan.rows - plan.used, width), big.dtype),
        ],
        axis=0,
    )


def from_rows(plan, table, big_shape, small_shape):
    big = table[: plan.small_at].reshape(plan.n_big, plan.rows_big, plan.width)[:, : plan.pix_big]
    return big.reshape(big_shape), table[plan.small_at : plan.used].reshape(small_shape)


def local(x_big, x_small, cot_big, cot_small, counts, params, first, second):
    width = x_big.shape[-1]
    hidden = FFN
    plan = Plan(x_big.shape, x_small.shape)
    consts = constants(plan)
    mod_at = 2 * width + 4
    out_at = mod_at + width
    up_at = out_at + width
    down_at = up_at + hidden
    tail_at = down_at + hidden
    shard = params.astype(BF16)
    tail = params.shape[1] - tail_at
    shard_a = jnp.concatenate(
        [shard[:, :mod_at], shard[:, tail_at:], jnp.zeros((shard.shape[0], TABLE - 4 - tail), BF16)], axis=1
    )
    shard_b = shard[:, mod_at:tail_at]
    wa = lax.all_gather(shard_a, "fsdp", axis=0, tiled=True)
    wb = lax.all_gather(shard_b, "fsdp", axis=0, tiled=True)
    weights = dict(
        wm=wb[:, :width], wo=wb[:, width : 2 * width], wu=wb[:, 2 * width : 2 * width + hidden], wd=wb[:, 2 * width + hidden :]
    )
    count_pair = counts.reshape(2)
    live_big = (jnp.arange(x_big.shape[0]) < count_pair[0]).astype(BF16)
    live_small = (jnp.arange(x_small.shape[0]) < count_pair[1]).astype(BF16)
    x_rows = to_rows(plan, x_big, x_small)
    wl = to_rows(plan, cot_big * live_big[:, None, None, None], cot_small * live_small[:, None, None, None])
    one = mix_forward(plan, consts, x_rows, wa)
    mid = middle_pass(plan, consts, x_rows, wl, one, weights)
    out_big, out_small = from_rows(plan, mid["out"], x_big.shape, x_small.shape)
    end = mix_backward(plan, consts, x_rows, wa, one, mid)
    grad_big, grad_small = from_rows(plan, end["gx"], x_big.shape, x_small.shape)
    grads = jnp.concatenate([mid["gqw"], end["gct"], mid["gm"], mid["go"], mid["gu"], mid["gd"]], axis=1)
    part = lax.psum_scatter(grads, "fsdp", scatter_dimension=0, tiled=True)
    summed = lax.psum(part, "dp").astype(F32)
    base = 2 * width + TABLE
    table = jnp.concatenate(
        [
            summed[:, : 2 * width + 4],
            summed[:, base:],
            summed[:, 2 * width + 4 : 2 * width + 4 + tail],
        ],
        axis=1,
    )
    square_sum = lax.psum(jnp.sum(table * table), "fsdp")
    grad_norm = jnp.sqrt(square_sum)
    scale = jnp.minimum(1.0, CLIP_NORM / (grad_norm + 1e-06))
    new_params, new_first, new_second = adam_update(params, table, first, second, scale)
    return (out_big, out_small, grad_big, grad_small, new_params, new_first, new_second, grad_norm)


def solution(mesh):
    images = P(("dp", "fsdp"), None, None, None)
    rows = P("fsdp", None)
    in_specs = (images,) * 4 + (P("dp", "fsdp", None),) + (rows,) * 3
    out_specs = (images,) * 4 + (rows,) * 3 + (P(),)
    return jax.shard_map(local, mesh=mesh, in_specs=in_specs, out_specs=out_specs, check_vma=False)
```

```python
from functools import partial

import jax
import jax.numpy as jnp
import numpy as np
from jax import lax
from jax.experimental import pallas as pl
from jax.experimental.pallas import tpu as pltpu
from jax.sharding import PartitionSpec as P

FFN = 1536
STEP = 10
CLIP_NORM = 1.0
BETA_ONE = 0.9
BETA_TWO = 0.999
LEARN_RATE = 0.05
DECAY_RATE = 0.05
ADAM_EPS = 1e-08
KERNEL_SIDES = (3, 5, 7)
F32 = jnp.float32
BF16 = jnp.bfloat16
VMEM_BYTES = 58 * 2**20

SLOT = 16


def up_to(value, step):
    return -(-value // step) * step


class Plan:
    def __init__(self, big_shape, small_shape):
        self.n_big, self.side_big = big_shape[0], big_shape[1]
        self.n_small, self.side_small = small_shape[0], small_shape[1]
        self.width = big_shape[3]
        self.pix_big = self.side_big**2
        self.pix_small = self.side_small**2
        self.rows_big = up_to(self.pix_big, SLOT)
        self.group = 4
        while (self.group * self.pix_small) % SLOT:
            self.group += 1
        self.n_groups = self.n_small // self.group
        assert self.n_groups * self.group == self.n_small
        self.rows_small = self.group * self.pix_small
        self.small_at = self.n_big * self.rows_big
        self.used = self.small_at + self.n_groups * self.rows_small
        self.rows = up_to(self.used, 128)
        self.n_images = self.n_big + self.n_small
        self.image_rows = up_to(self.n_images, SLOT)


def half_spectrum(size):
    reps = []
    for u in range(size):
        for v in range(size):
            other = ((-u) % size, (-v) % size)
            if (u, v) <= other:
                reps.append((u, v, 1.0 if (u, v) == other else 2.0))
    return np.array(reps)


def transform_pair(side, kernel_side, copies):
    margin = kernel_side // 2
    size = side + margin
    reps = half_spectrum(size)
    count = len(reps)
    freq = 2 * np.pi * reps[:, :2] / size
    grid = np.array([(i, j) for i in range(side) for j in range(side)], float)
    lags = np.array([(i - margin, j - margin) for i in range(kernel_side) for j in range(kernel_side)], float)
    phase = freq @ grid.T
    lag_phase = freq @ lags.T
    weight = reps[:, 2:3] / size**2
    pix = side * side
    half = up_to(copies * count, SLOT)
    rows = up_to(copies * pix, SLOT)
    forward = np.zeros((2 * half, rows))
    inverse = np.zeros((rows, 2 * half))
    taps = np.zeros((2 * half, kernel_side**2))
    back = np.zeros((kernel_side**2, 2 * half))
    for one in range(copies):
        low, col = one * count, one * pix
        forward[low : low + count, col : col + pix] = np.cos(phase)
        forward[half + low : half + low + count, col : col + pix] = -np.sin(phase)
        inverse[col : col + pix, low : low + count] = (weight * np.cos(phase)).T
        inverse[col : col + pix, half + low : half + low + count] = -(weight * np.sin(phase)).T
        taps[low : low + count] = np.cos(lag_phase)
        taps[half + low : half + low + count] = np.sin(lag_phase)
        back[:, low : low + count] = (weight * np.cos(lag_phase)).T
        back[:, half + low : half + low + count] = -(weight * np.sin(lag_phase)).T
    return forward, inverse, taps, back


TABLE = 128
GATES_AT = 0
TAPS_AT = 4
VECS_AT = 87
BIAS_AT = 96


def low_np(values):
    return jnp.asarray(values, F32).astype(BF16)


def high_and_rest(values):
    high = values.astype(np.float32).astype(jnp.bfloat16)
    rest = (values - high.astype(np.float64)).astype(np.float32).astype(jnp.bfloat16)
    return jnp.asarray(high), jnp.asarray(rest)


def constants(plan):
    consts = {}
    tap_at = TAPS_AT
    for level, kernel_side in enumerate(KERNEL_SIDES):
        for kind, side, copies in (("b", plan.side_big, 1), ("s", plan.side_small, plan.group)):
            forward, inverse, taps, back = transform_pair(side, kernel_side, copies)
            wide = np.zeros((taps.shape[0], TABLE))
            wide[:, tap_at : tap_at + kernel_side**2] = taps
            tall = np.zeros((TABLE, taps.shape[0]))
            tall[tap_at : tap_at + kernel_side**2] = back
            consts["f" + kind + str(level)] = low_np(forward)
            consts["g" + kind + str(level)] = low_np(inverse)
            high, rest = high_and_rest(wide)
            consts["k" + kind + str(level)] = jnp.concatenate([high, rest], axis=1)
            consts["t" + kind + str(level)] = low_np(tall)
        tap_at += kernel_side**2
    pick = np.zeros((plan.image_rows, plan.rows))
    for one in range(plan.n_big):
        pick[one, one * plan.rows_big : one * plan.rows_big + plan.pix_big] = 1.0
    for one in range(plan.n_small):
        at = plan.small_at + one * plan.pix_small
        pick[plan.n_big + one, at : at + plan.pix_small] = 1.0
    consts["pick"] = low_np(pick)
    consts["spread"] = low_np(pick.T)
    consts["eye"] = low_np(np.eye(TABLE))
    lanes = np.zeros((FFN, plan.width))
    lanes[np.arange(FFN), np.arange(FFN) // (FFN // plan.width)] = 1.0
    consts["lanes"] = low_np(lanes)
    return consts


def dot(left, right):
    return jnp.dot(left, right, preferred_element_type=F32)


def dot_nt(left, right):
    return lax.dot_general(left, right, (((1,), (1,)), ((), ())), preferred_element_type=F32)


def dot_tn(left, right):
    return lax.dot_general(left, right, (((0,), (0,)), ((), ())), preferred_element_type=F32)


def tiles(low, high, step):
    for at in range(low, high, step):
        yield slice(at, min(at + step, high))


def gelu_and_slope(values):
    chance = 0.5 + 0.5 * lax.erf(values * 0.7071067811865476)
    bell = jnp.exp(values * values * -0.5) * 0.3989422804014327
    return values * chance, chance + values * bell


class Refs(dict):
    def __getattr__(self, name):
        return self[name]

    def setup(self, fetched, sent):
        self.used = 0
        self.open = {}
        self.leaving = []
        self.sent = sent
        for name, (source, lanes) in fetched.items():
            far = self[source] if lanes is None else self[source].at[:, lanes]
            self.open[name] = self.copy(far, self[name])

    def copy(self, source, target):
        result = pltpu.make_async_copy(source, target, self["sems"].at[self.used])
        result.start()
        self.used += 1
        return result

    def need(self, *names):
        for name in names:
            if name in self.open:
                self.open.pop(name).wait()

    def send(self, name, at=None):
        far, near = self["far_" + name], self[name]
        if at is not None:
            far, near = far.at[at], near.at[at]
        self.leaving.append(self.copy(near, far))

    def finish(self):
        self.need(*list(self.open))
        for copy in self.leaving:
            copy.wait()


COPIES = 96


def run(body, inputs, outputs, scratch, fetched=None, sent=(), far=(), micros=20, limit=VMEM_BYTES):
    fetched = {name: (name, None) if entry is None else entry for name, entry in (fetched or {}).items()}
    sources = {source for source, _ in fetched.values()}
    buffers = {}
    for name, (source, lanes) in fetched.items():
        shape = inputs[source].shape
        if lanes is not None:
            shape = (shape[0], lanes.stop - lanes.start)
        buffers["near_" + name] = (shape, inputs[source].dtype)
    for name in sent:
        buffers["near_" + name] = outputs[name]
    names = ["in_" + name for name in inputs] + ["out_" + name for name in outputs] + list(scratch) + list(buffers)

    def kernel(*args):
        given = dict(zip(names + ["sems"], args))
        refs = Refs()
        for name in inputs:
            refs[name] = given["in_" + name]
        for name in outputs:
            refs["far_" + name if name in sent else name] = given["out_" + name]
        for name in list(scratch) + ["sems"]:
            refs[name] = given[name]
        entries = {}
        for name, (source, lanes) in fetched.items():
            refs["source_" + source] = given["in_" + source]
            entries[name] = ("source_" + source, lanes)
        for name in list(fetched) + list(sent):
            refs[name] = given["near_" + name]
        refs.setup(entries, sent)
        body(refs)
        refs.finish()

    def space(name, distant):
        return pl.BlockSpec(memory_space=pl.ANY if distant else pltpu.VMEM)

    results = pl.pallas_call(
        kernel,
        in_specs=[space(name, name in sources or name in far) for name in inputs],
        out_specs=[space(name, name in sent or name in far) for name in outputs],
        out_shape=[jax.ShapeDtypeStruct(shape, dtype) for shape, dtype in outputs.values()],
        scratch_shapes=[pltpu.VMEM(*entry) for entry in list(scratch.values()) + list(buffers.values())]
        + [pltpu.SemaphoreType.DMA((COPIES,))],
        compiler_params=pltpu.CompilerParams(vmem_limit_bytes=limit),
        cost_estimate=pl.CostEstimate(flops=micros * 10**9, bytes_accessed=micros * 10**6, transcendentals=0),
    )(*inputs.values())
    return dict(zip(outputs, results))


def units(plan):
    result = []
    for one in range(plan.n_big):
        result.append(("b", slice(one * plan.rows_big, (one + 1) * plan.rows_big), len(result)))
    for one in range(plan.n_groups):
        at = plan.small_at + one * plan.rows_small
        result.append(("s", slice(at, at + plan.rows_small), len(result)))
    return result


def wave_rows(plan, consts):
    result, total = {}, []
    for level in range(3):
        at = 0
        for kind, _, index in units(plan):
            count = consts["f" + kind + str(level)].shape[0]
            result[level, index] = slice(at, at + count)
            at += count
        total.append(at)
    return result, total


def spectrum_of_taps(refs, name, table):
    refs["h" + name][...] = dot_nt(refs["k" + name][:, :TABLE], table) + dot_nt(refs["k" + name][:, TABLE:], table)


def image_scale(plan):
    row = lax.broadcasted_iota(jnp.int32, (plan.image_rows, 1), 0)
    return jnp.where(row < plan.n_big, 1.0 / plan.pix_big, 1.0 / plan.pix_small).astype(F32)


def unit_rows(values):
    center = values - jnp.mean(values, axis=-1, keepdims=True)
    scale = lax.rsqrt(jnp.mean(center * center, axis=-1, keepdims=True) + 1e-05)
    return center * scale, scale


def fold(values):
    total = values[0:8]
    for low in range(8, values.shape[0], 8):
        total = total + values[low : low + 8]
    return total


def column_sum(values):
    return jnp.sum(values, axis=0, keepdims=True)


def forward_mix(plan, places, sizes, n_pieces, refs):
    rows, width, hidden = plan.rows, plan.width, FFN
    for copy in gather(refs, sizes, n_pieces, "wa"):
        copy.wait()
    refs.send("wa")
    refs.need("eye")
    inner = 2 * width + TABLE
    table = refs.wa[:, 2 * width : inner]
    refs.vec[...] = dot_nt(refs.eye[...], table)
    refs.need("x")
    gain = refs.vec[VECS_AT : VECS_AT + 1, :]
    shift = refs.vec[VECS_AT + 1 : VECS_AT + 2, :]
    for block in tiles(0, rows, 256):
        for at in tiles(block.start, block.stop, 32):
            unit, _ = unit_rows(refs.x[at, :].astype(F32))
            refs.normed[at, :] = (unit * gain + shift).astype(BF16)
        refs.send("normed", block)
        part = dot(refs.normed[block, :], refs.wa[:, :inner])
        refs.c[0, block, :] = (part[:, :width] + refs.vec[VECS_AT + 3 : VECS_AT + 4, :]).astype(BF16)
        refs.q[block, :] = (part[:, width : 2 * width] + refs.vec[VECS_AT + 2 : VECS_AT + 3, :]).astype(BF16)
        refs.gate[block, :] = part[:, 2 * width :]
    refs.send("gate")
    refs.send("q")
    refs.send("c", slice(0, 1))
    if rows > plan.used:
        refs.c[1:, plan.used :, :] = jnp.zeros((3, rows - plan.used, width), BF16)
        refs.gp[:, plan.used :, :] = jnp.zeros((3, rows - plan.used, width), BF16)
    for level in range(3):
        for kind in "bs":
            refs.need("f" + kind + str(level), "k" + kind + str(level), "g" + kind + str(level))
            spectrum_of_taps(refs, kind + str(level), table)
        for kind, at, index in units(plan):
            name = kind + str(level)
            count = refs["f" + name].shape[0]
            half = count // 2
            wave, low_wave = refs.wave.at[index], refs.wave_low.at[index]
            wave[:count, :] = dot(refs["f" + name][...], refs.c[level, at, :])
            saved = places[level, index].start
            taps = refs["h" + name]
            hat = refs["hat" + str(level)]
            for re in tiles(0, half, 16):
                im = slice(half + re.start, half + re.stop)
                wave_re, wave_im = wave[re, :], wave[im, :]
                tap_re, tap_im = taps[re, :], taps[im, :]
                hat[saved + re.start : saved + re.stop, :] = wave_re.astype(BF16)
                hat[saved + im.start : saved + im.stop, :] = wave_im.astype(BF16)
                low_wave[re, :] = (wave_re * tap_re - wave_im * tap_im).astype(BF16)
                low_wave[im, :] = (wave_re * tap_im + wave_im * tap_re).astype(BF16)
            refs.field[at, :] = dot(refs["g" + name][...], low_wave[:count, :])
            for into in tiles(at.start, at.stop, 16):
                value, slope = gelu_and_slope(refs.field[into, :])
                refs.c[level + 1, into, :] = value.astype(BF16)
                refs.gp[level, into, :] = slope.astype(BF16)
        refs.send("c", slice(level + 1, level + 2))
        refs.send("gp", slice(level, level + 1))
        refs.send("hat" + str(level))
    refs.need("pick", "spread")
    mean = dot(refs.pick[...], refs.c[3]) * image_scale(plan)
    summary, slope = gelu_and_slope(mean)
    refs.sum[0] = summary
    refs.sum[1] = slope
    summary_low = summary.astype(BF16)
    for block in tiles(0, rows, 256):
        refs.field[block, :] = dot(refs.spread[block, :], summary_low)
        for at in tiles(block.start, block.stop, 32):
            gate = refs.gate[at, :]
            total = refs.field[at, :] * gate[:, 3:4]
            for level in range(3):
                total += refs.c[level + 1, at, :].astype(F32) * gate[:, level : level + 1]
            refs.mixed[at, :] = total.astype(BF16)
        refs.send("mixed", block)
    refs.need("lanes")
    ratio = hidden // width
    spread = dot_nt(refs.vec[BIAS_AT : BIAS_AT + 16, :].astype(BF16), refs.lanes[...])
    row = lax.broadcasted_iota(jnp.int32, (16, hidden), 0)
    lane = lax.broadcasted_iota(jnp.int32, (16, hidden), 1)
    picked = jnp.where(lax.rem(lane, ratio) == row, spread, 0.0)
    refs.upb[...] = jnp.broadcast_to(jnp.sum(picked, axis=0, keepdims=True), (8, hidden))


def mix_scratch(plan, consts):
    scratch = {}
    for level in range(3):
        for kind in "bs":
            scratch["h" + kind + str(level)] = ((consts["f" + kind + str(level)].shape[0], plan.width), F32)
    return scratch


def most_waves(consts):
    return max(consts["f" + kind + str(level)].shape[0] for level in range(3) for kind in "bs")


def mix_forward(plan, consts, x_rows, pieces, sizes):
    rows, width = plan.rows, plan.width
    waves, n_units = most_waves(consts), len(units(plan))
    places, saved = wave_rows(plan, consts)
    keys = [k + kind + str(level) for level in range(3) for kind in "bs" for k in "fkg"]
    names = ["eye"] + keys + ["pick", "spread", "lanes"]
    inputs = dict(x=x_rows, **{k: consts[k] for k in names})
    apart = {"w" + str(step): piece for step, piece in enumerate(pieces)}
    inputs.update(apart)
    outputs = dict(
        wa=((width, 2 * width + 2 * TABLE), BF16),
        normed=((rows, width), BF16),
        q=((rows, width), BF16),
        c=((4, rows, width), BF16),
        gp=((3, rows, width), BF16),
        **{"hat" + str(level): ((saved[level], width), BF16) for level in range(3)},
        mixed=((rows, width), BF16),
        gate=((rows, TABLE), F32),
        vec=((TABLE, width), F32),
        upb=((8, FFN), F32),
        sum=((2, plan.image_rows, width), F32),
    )
    scratch = dict(
        wave=((n_units, waves, width), F32),
        wave_low=((n_units, waves, width), BF16),
        field=((rows, width), F32),
        **mix_scratch(plan, consts),
    )
    sent = ("normed", "q", "c", "gp", "hat0", "hat1", "hat2", "mixed", "gate")
    sent += ("wa",)
    body = partial(forward_mix, plan, places, sizes, len(pieces))
    return run(body, inputs, outputs, scratch, {k: None for k in ["x"] + names}, sent, list(apart), 20)


def gather(refs, sizes, n_pieces, target):
    n_dp, n_z, n_core = sizes
    if n_pieces == 1:
        return [refs.copy(refs["w0"], refs[target])]
    copies = []
    me, my_z, my_core = (lax.axis_index(name) for name in ("dp", "z", "core"))
    for step in range(n_pieces):
        piece = refs["w" + str(step)]
        _, height, part = piece.shape
        lanes = pl.ds(pl.multiple_of((me ^ (step // n_core)) * part, TABLE), part)
        for other in range(n_z):
            owner = (my_z ^ other) * n_core + (my_core ^ (step % n_core))
            rows = pl.ds(pl.multiple_of(owner * height, 16), height)
            copies.append(refs.copy(piece.at[other], refs[target].at[rows, lanes]))
    return copies


class Shares:
    def __init__(self, sizes, rows, columns, halves):
        self.n_dp, self.n_z, self.n_core = sizes
        self.height = rows // (self.n_z * self.n_core)
        self.part = up_to(columns, TABLE * self.n_dp) // self.n_dp
        self.empty = self.part * self.n_dp - columns
        self.halves = halves
        whole = (self.n_dp, self.n_z, self.n_core, self.height, self.part)
        self.shape = (self.n_core, self.n_dp, self.n_z, self.height, self.part) if halves else whole
        self.columns = columns

    def put(self, ref, low, values):
        done = 0
        while done < values.shape[1]:
            share, at = divmod(low + done, self.part)
            take = min(self.part - at, values.shape[1] - done)
            for owner in range(self.n_z * self.n_core):
                z, core = divmod(owner, self.n_core)
                place = (core, share, z) if self.halves else (share, z, core)
                ref[place + (slice(None), slice(at, at + take))] = values[
                    owner * self.height : (owner + 1) * self.height, done : done + take
                ]
            done += take

    def close(self, refs, stage, names):
        if self.empty:
            self.put(stage, self.columns, jnp.zeros((self.height * self.n_z * self.n_core, self.empty), BF16))
        core = lax.axis_index("core")
        for source, name in ((1 - core, names[1]), (core, names[0])):
            refs.leaving.append(refs.copy(stage.at[source], refs[name]))


class Plain:
    def __init__(self, rows, columns):
        self.shape = (rows, columns)

    def put(self, ref, low, values):
        ref[:, low : low + values.shape[1]] = values

    def close(self, refs, stage, names):
        refs.leaving.append(refs.copy(stage, refs[names[0]]))


def middle(plan, shares, sizes, n_pieces, refs):
    rows, width, hidden = plan.rows, plan.width, FFN
    vec = lambda index: refs.vec[VECS_AT + index : VECS_AT + index + 1, :]
    zero = jnp.zeros((8, width), F32)
    totals = [zero] * 4
    blocks = list(tiles(0, rows, 256))
    wm, wo = refs.wb.at[:, :width], refs.wb.at[:, width : 2 * width]
    wu, wd = refs.wb.at[:, 2 * width : 2 * width + hidden], refs.wb.at[:, 2 * width + hidden : 2 * width + 2 * hidden]
    arriving = gather(refs, sizes, n_pieces, "wb")
    refs.need("mixed", "q")
    for copy in arriving:
        copy.wait()
    refs.leaving.append(refs.copy(refs.wb.at[:, : 2 * width], refs.wmo))
    for block in blocks:
        modulator = dot(refs.mixed[block, :], wm[...]) + vec(4)
        refs.mod[block, :] = modulator.astype(BF16)
        refs.prod[block, :] = (refs.q[block, :].astype(F32) * modulator).astype(BF16)
        refs.send("mod", block)
        refs.send("prod", block)
    refs.need("x")
    for block in blocks:
        refs.resid[block, :] = dot(refs.prod[block, :], wo[...])
        for at in tiles(block.start, block.stop, 32):
            resid = refs.resid[at, :] + refs.x[at, :].astype(F32) + vec(5)
            refs.resid[at, :] = resid
            unit, scale = unit_rows(resid)
            refs.unit[at, :] = unit
            refs.scale[at, :] = jnp.broadcast_to(scale, (scale.shape[0], TABLE))
            refs.n2[at, :] = (unit * vec(6) + vec(7)).astype(BF16)
    refs.need("wl")
    for block in blocks:
        for index, lanes in enumerate(tiles(0, hidden, 256)):
            pre, grad_act = refs.pa.at[index % 3], refs.ga.at[index % 3]
            pre[...] = dot(refs.n2[block, :], wu[:, lanes])
            grad_act[...] = dot(refs.wl[block, :], wd[:, lanes])
            bias = refs.upb[0:1, lanes]
            total = jnp.zeros((8, 256), F32) if block.start == 0 else refs.gub[:, lanes]
            for low in tiles(0, 256, 16):
                at = slice(block.start + low.start, block.start + low.stop)
                value, slope = gelu_and_slope(pre[low, :] + bias)
                grad = grad_act[low, :] * slope
                refs.act[at, lanes] = value.astype(BF16)
                refs.pre[at, lanes] = grad.astype(BF16)
                total = total + fold(grad)
            refs.gub[:, lanes] = total
        refs.gn[block, :] = dot_nt(refs.pre[block, :], wu[...])
        refs.out[block, :] = (
            refs.resid[block, :] + dot_nt(refs.act[block, :], wd[...]) + vec(8)
        ).astype(BF16)
        refs.send("out", block)
    for lanes in tiles(0, hidden, 256):
        shares.put(refs.stage, lanes.start, dot_tn(refs.n2[...], refs.pre[:, lanes]).astype(BF16))
        shares.put(refs.stage, hidden + lanes.start, dot_tn(refs.wl[...], refs.act[:, lanes]).astype(BF16))
    shares.close(refs, refs.stage, ("keep", "give"))
    for block in blocks:
        for at in tiles(block.start, block.stop, 32):
            grad = refs.gn[at, :]
            unit = refs.unit[at, :]
            weighted = refs.wl[at, :].astype(F32)
            gained = grad * vec(6)
            mean_one = jnp.mean(gained, axis=-1, keepdims=True)
            mean_two = jnp.mean(gained * unit, axis=-1, keepdims=True)
            result = weighted + refs.scale[at, 0:1] * (gained - mean_one - unit * mean_two)
            refs.gres[at, :] = result
            refs.glow[at, :] = result.astype(BF16)
            totals = [old + fold(new) for old, new in zip(totals, (grad * unit, grad, result, weighted))]
        refs.send("gres", block)
        refs.send("glow", block)
    refs.gv[...] = jnp.zeros(refs.gv.shape, F32)
    for at, total in zip((6, 7, 5, 8), totals):
        refs.gv[at : at + 1, :] = column_sum(total)
    ratio = hidden // width
    row = lax.broadcasted_iota(jnp.int32, (16, hidden), 0)
    lane = lax.broadcasted_iota(jnp.int32, (16, hidden), 1)
    picked = jnp.where(lax.rem(lane, ratio) == row, column_sum(refs.gub[...]), 0.0).astype(BF16)
    refs.need("lanes")
    refs.gv[16:32, :] = dot(picked, refs.lanes[...])


def kept(shares):
    if isinstance(shares, Plain):
        return dict(keep=(shares.shape, BF16))
    return dict(keep=(shares.shape[1:], BF16), give=(shares.shape[1:], BF16))


def middle_pass(plan, consts, shares, x_rows, wl, first, pieces, sizes):
    rows, width, hidden = plan.rows, plan.width, FFN
    near = dict(mixed=first["mixed"], q=first["q"], x=x_rows, wl=wl, lanes=consts["lanes"])
    apart = {"w" + str(step): piece for step, piece in enumerate(pieces)}
    inputs = dict(near, vec=first["vec"], upb=first["upb"], **apart)
    token, field = ((rows, width), BF16), ((rows, width), F32)
    outputs = dict(kept(shares), out=token, mod=token, prod=token, glow=token, gres=field)
    outputs.update(wmo=((width, 2 * width), BF16), gv=((32, width), F32))
    wide = ((rows, hidden), BF16)
    scratch = dict(
        resid=field,
        unit=field,
        scale=((rows, TABLE), F32),
        n2=token,
        pa=((3, 256, 256), F32),
        ga=((3, 256, 256), F32),
        act=wide,
        pre=wide,
        gub=((8, hidden), F32),
        gn=field,
        stage=(shares.shape, BF16),
        wb=((width, 2 * width + 2 * hidden + 2 * TABLE), BF16),
    )
    body = partial(middle, plan, shares, sizes, len(pieces))
    far = ["keep", "give", "wmo"] + list(apart)
    sent = ("out", "mod", "prod", "glow", "gres")
    return run(body, inputs, outputs, scratch, {k: None for k in near}, sent, far, 23)


def product_back(plan, shares, refs):
    rows, width = plan.rows, plan.width
    totals = [jnp.zeros((8, width), F32)] * 2
    refs.need("glow", "wmo", "mod", "q")
    wm, wo = refs.wmo.at[:, :width], refs.wmo.at[:, width:]
    for block in tiles(0, rows, 256):
        refs.gn[block, :] = dot_nt(refs.glow[block, :], wo[...])
        for at in tiles(block.start, block.stop, 32):
            grad = refs.gn[at, :]
            grad_query = grad * refs.mod[at, :].astype(F32)
            grad_mod = grad * refs.q[at, :].astype(F32)
            refs.gq[at, :] = grad_query.astype(BF16)
            refs.gmod[at, :] = grad_mod.astype(BF16)
            totals = [totals[0] + fold(grad_query), totals[1] + fold(grad_mod)]
        refs.send("gq", block)
        refs.gmix[block, :] = dot_nt(refs.gmod[block, :], wm[...]).astype(BF16)
        refs.send("gmix", block)
    refs.need("prod", "normed", "mixed")
    shares.put(refs.stage, 2 * width, dot_tn(refs.prod[...], refs.glow[...]).astype(BF16))
    shares.put(refs.stage, 0, dot_tn(refs.normed[...], refs.gq[...]).astype(BF16))
    shares.put(refs.stage, width, dot_tn(refs.mixed[...], refs.gmod[...]).astype(BF16))
    shares.close(refs, refs.stage, ("keep", "give"))
    refs.gv2[...] = jnp.zeros(refs.gv2.shape, F32)
    for at, total in zip((2, 4), totals):
        refs.gv2[at : at + 1, :] = column_sum(total)


def product_pass(plan, shares, first, mid):
    rows, width = plan.rows, plan.width
    inputs = {k: mid[k] for k in ("glow", "wmo", "mod")}
    inputs.update(q=first["q"], prod=mid["prod"], normed=first["normed"], mixed=first["mixed"])
    token = ((rows, width), BF16)
    outputs = dict(kept(shares), gq=token, gmix=token, gv2=((8, width), F32))
    scratch = dict(gn=((rows, width), F32), gmod=token, stage=(shares.shape, BF16))
    fetched = {k: None for k in inputs}
    return run(partial(product_back, plan, shares), inputs, outputs, scratch, fetched, ("gq", "gmix"), ("keep", "give"), 9)


def backward_mix(plan, places, refs):
    rows, width = plan.rows, plan.width
    refs.need("table")
    table = refs.table[...]
    scale = image_scale(plan)
    summary_low = refs.sum[0].astype(BF16)
    lane = lax.broadcasted_iota(jnp.int32, (1, TABLE), 1)
    refs.need("gmix", "gate", "spread", "c")
    for block in tiles(0, rows, 256):
        refs.gc[block, :] = dot(refs.spread[block, :], summary_low)
        for at in tiles(block.start, block.stop, 32):
            grad = refs.gmix[at, :].astype(F32)
            result = jnp.where(lane == 3, jnp.sum(grad * refs.gc[at, :], axis=-1, keepdims=True), 0.0)
            for level in range(3):
                part = jnp.sum(grad * refs.c[level + 1, at, :].astype(F32), axis=-1, keepdims=True)
                result = jnp.where(lane == level, part, result)
            refs.ggate[at, :] = result.astype(BF16)
            refs.tmp[at, :] = (grad * refs.gate[at, 3:4]).astype(BF16)
    refs.need("pick")
    grad_summary = dot(refs.pick[...], refs.tmp[...]) * refs.sum[1] * scale
    grad_summary_low = grad_summary.astype(BF16)
    for block in tiles(0, rows, 256):
        refs.gc[block, :] = dot(refs.spread[block, :], grad_summary_low)
    taps_total = jnp.zeros((TABLE, width), F32)
    refs.need("gp")
    for level in (2, 1, 0):
        for kind in "bs":
            refs.need("f" + kind + str(level), "k" + kind + str(level), "g" + kind + str(level))
            spectrum_of_taps(refs, kind + str(level), table)
        refs.need("hat" + str(level))
        hat = refs["hat" + str(level)]
        seen = set()
        for kind, at, index in units(plan):
            name = kind + str(level)
            count = refs["f" + name].shape[0]
            half = count // 2
            for into in tiles(at.start, at.stop, 16):
                direct = refs.gmix[into, :].astype(F32) * refs.gate[into, level : level + 1]
                grad = refs.gc[into, :] + direct
                refs.tmp[into, :] = (grad * refs.gp[level, into, :].astype(F32)).astype(BF16)
            wave, low_wave = refs.wave.at[index], refs.wave_low.at[index]
            wave[:count, :] = dot(refs["f" + name][...], refs.tmp[at, :])
            saved = places[level, index].start
            taps = refs["h" + name]
            cross = refs["x" + kind]
            for re in tiles(0, half, 16):
                im = slice(half + re.start, half + re.stop)
                wave_re = hat[saved + re.start : saved + re.stop, :].astype(F32)
                wave_im = hat[saved + im.start : saved + im.stop, :].astype(F32)
                grad_re, grad_im = wave[re, :], wave[im, :]
                tap_re, tap_im = taps[re, :], taps[im, :]
                low_wave[re, :] = (grad_re * tap_re + grad_im * tap_im).astype(BF16)
                low_wave[im, :] = (grad_im * tap_re - grad_re * tap_im).astype(BF16)
                cross_re = grad_re * wave_re + grad_im * wave_im
                cross_im = grad_re * wave_im - grad_im * wave_re
                if kind in seen:
                    cross_re = cross_re + cross[re, :]
                    cross_im = cross_im + cross[im, :]
                cross[re, :] = cross_re
                cross[im, :] = cross_im
            seen.add(kind)
            refs.gc[at, :] = dot(refs["g" + name][...], low_wave[:count, :])
        for kind in "bs":
            name = kind + str(level)
            count = refs["f" + name].shape[0]
            refs.need("t" + name)
            taps_total = taps_total + dot(refs["t" + name][...], refs["x" + kind][:count, :].astype(BF16))
    refs.gtab[...] = taps_total
    if rows > plan.used:
        refs.gc[plan.used :, :] = jnp.zeros((rows - plan.used, width), F32)
    context_total = jnp.zeros((8, width), F32)
    for block in tiles(0, rows, 256):
        for at in tiles(block.start, block.stop, 32):
            grad = refs.gc[at, :]
            refs.glow[at, :] = grad.astype(BF16)
            context_total = context_total + fold(grad)
        refs.send("glow", block)
    refs.gtab[VECS_AT + 3 : VECS_AT + 4, :] = column_sum(context_total)


def input_back(plan, shares, refs):
    rows, width = plan.rows, plan.width
    refs.need("normed", "glow", "ggate")
    shares.put(refs.g3, 0, dot_tn(refs.normed[...], refs.glow[...]).astype(BF16))
    gates = dot_tn(refs.normed[...], refs.ggate[...])
    zero = jnp.zeros((8, width), F32)
    gain_total, shift_total = zero, zero
    refs.need("wa", "gq", "x", "gres")
    gain = refs.vec[VECS_AT : VECS_AT + 1, :]
    for block in tiles(0, rows, 256):
        refs.gc[block, :] = (
            dot_nt(refs.gq[block, :], refs.wa[:, width : 2 * width])
            + dot_nt(refs.glow[block, :], refs.wa[:, :width])
            + dot_nt(refs.ggate[block, :], refs.wa[:, 2 * width :])
        )
        for at in tiles(block.start, block.stop, 32):
            unit, scale_row = unit_rows(refs.x[at, :].astype(F32))
            grad = refs.gc[at, :]
            gained = grad * gain
            mean_one = jnp.mean(gained, axis=-1, keepdims=True)
            mean_two = jnp.mean(gained * unit, axis=-1, keepdims=True)
            result = refs.gres[at, :] + scale_row * (gained - mean_one - unit * mean_two)
            refs.gx[at, :] = result.astype(BF16)
            gain_total = gain_total + fold(grad * unit)
            shift_total = shift_total + fold(grad)
        refs.send("gx", block)
    refs.gtab[...] = refs.taps[...]
    refs.gtab[VECS_AT + 4 : VECS_AT + 9, :] = refs.gv[4:9, :]
    refs.gtab[VECS_AT + 2 : VECS_AT + 3, :] = refs.gv2[2:3, :]
    refs.gtab[VECS_AT + 4 : VECS_AT + 5, :] = refs.gv2[4:5, :]
    refs.gtab[VECS_AT : VECS_AT + 1, :] = column_sum(gain_total)
    refs.gtab[VECS_AT + 1 : VECS_AT + 2, :] = column_sum(shift_total)
    refs.gtab[BIAS_AT : BIAS_AT + 4, :] = refs.gv[16:20, :]
    refs.need("eye")
    small = gates + dot_tn(refs.gtab[...].astype(BF16), refs.eye[...])
    shares.put(refs.g3, width, small.astype(BF16))


def mix_backward(plan, consts, first, back):
    rows, width = plan.rows, plan.width
    waves, n_units = most_waves(consts), len(units(plan))
    places, _ = wave_rows(plan, consts)
    keys = [k + kind + str(level) for level in (2, 1, 0) for k in "kfgt" for kind in "bs"]
    hats = {"hat" + str(level): first["hat" + str(level)] for level in range(3)}
    inputs = dict({k: first[k] for k in ("wa", "gate", "c", "gp", "sum")}, gmix=back["gmix"], **hats)
    inputs.update({k: consts[k] for k in keys + ["pick", "spread"]})
    fetched = dict(table=("wa", slice(2 * width, 2 * width + TABLE)), gmix=None, gate=None, spread=None, c=None)
    fetched.update(pick=None, gp=None)
    for level in (2, 1, 0):
        for name in keys:
            if name.endswith(str(level)):
                fetched[name] = None
        fetched["hat" + str(level)] = None
    outputs = dict(glow=((rows, width), BF16), ggate=((rows, TABLE), BF16), gtab=((TABLE, width), F32))
    scratch = dict(
        wave=((n_units, waves, width), F32),
        wave_low=((n_units, waves, width), BF16),
        xb=((waves, width), F32),
        xs=((waves, width), F32),
        gc=((rows, width), F32),
        tmp=((rows, width), BF16),
        **mix_scratch(plan, consts),
    )
    return run(partial(backward_mix, plan, places), inputs, outputs, scratch, fetched, ("glow",), micros=18)


def input_pass(plan, consts, shares, x_rows, first, mid, back, mix):
    rows, width = plan.rows, plan.width
    near = dict(normed=first["normed"], glow=mix["glow"], ggate=mix["ggate"], wa=first["wa"], gq=back["gq"], x=x_rows)
    near.update(gres=mid["gres"], eye=consts["eye"])
    inputs = dict(near, taps=mix["gtab"], vec=first["vec"], gv=mid["gv"], gv2=back["gv2"])
    outputs = dict(g3=(shares.shape, BF16), gx=((rows, width), BF16))
    scratch = dict(gc=((rows, width), F32), gtab=((TABLE, width), F32))
    fetched = {k: None for k in near}
    fetched["wa"] = ("wa", slice(0, 2 * width + TABLE))
    return run(partial(input_back, plan, shares), inputs, outputs, scratch, fetched, ("gx",), micros=8)


def adam_rows(params, grads, first, second, scale):
    clipped = grads * scale
    first_new = BETA_ONE * first + (1.0 - BETA_ONE) * clipped
    second_new = BETA_TWO * second + (1.0 - BETA_TWO) * clipped * clipped
    first_hat = first_new * (1.0 / (1.0 - BETA_ONE**STEP))
    second_hat = second_new * (1.0 / (1.0 - BETA_TWO**STEP))
    params_new = params - LEARN_RATE * (first_hat / (jnp.sqrt(second_hat) + ADAM_EPS) + DECAY_RATE * params)
    return (params_new, first_new, second_new)


def to_rows(plan, big, small):
    width = plan.width
    padded = jnp.pad(
        big.reshape(plan.n_big, plan.pix_big, width), ((0, 0), (0, plan.rows_big - plan.pix_big), (0, 0))
    )
    return jnp.concatenate(
        [
            padded.reshape(plan.small_at, width),
            small.reshape(-1, width),
            jnp.zeros((plan.rows - plan.used, width), big.dtype),
        ],
        axis=0,
    )


def from_rows(plan, table, big_shape, small_shape):
    big = table[: plan.small_at].reshape(plan.n_big, plan.rows_big, plan.width)[:, : plan.pix_big]
    return big.reshape(big_shape), table[plan.small_at : plan.used].reshape(small_shape)


def whole_sums(plan, sizes, tail, late, early, late_columns):
    fsdp = ("z", "core")
    width, hidden = plan.width, FFN
    rows = late.shape[0]
    table = jnp.concatenate([late[:, :late_columns]] + early, axis=1)
    if sizes[1] * sizes[2] > 1:
        table = lax.psum_scatter(table, fsdp, scatter_dimension=0, tiled=True)
    table = lax.psum(table, "dp").astype(F32)
    ups, rest = late_columns, late_columns + 2 * hidden
    grads = jnp.concatenate(
        [
            table[:, rest : rest + width],
            table[:, : width + 4],
            table[:, rest + width :],
            table[:, ups:rest],
            table[:, width + 4 : width + 4 + tail],
        ],
        axis=1,
    )
    return grads, lax.psum(jnp.sum(grads * grads), fsdp)


def late_sums(refs):
    late = refs.both[0].astype(F32)
    for index in range(1, refs.both.shape[0]):
        late = late + refs.both[index].astype(F32)
    late = late.astype(BF16)
    refs.late[...] = late
    square = jnp.sum(jnp.square(refs.early[...].astype(F32))) + jnp.sum(jnp.square(late.astype(F32)))
    refs.wide[...] = jnp.full(refs.wide.shape, square, F32)


def optimizer(plan, sizes, parts, tail, refs):
    n_dp = sizes[0]
    part1, part2, part3 = parts
    width, hidden = plan.width, FFN
    me = lax.axis_index("dp")
    split = part1 + part2
    for step in range(n_dp):
        at = pl.ds(me ^ step, 1)
        refs.by_dp[at, :, :split] = refs["o" + str(step)][...].astype(F32)[None]
        refs.by_dp[at, :, split:] = refs["l" + str(step)][...].astype(F32)[None]
    blocks = [refs.by_dp[index] for index in range(n_dp)]
    cut = lambda low, high: jnp.concatenate([block[:, low:high] for block in blocks], axis=1)
    ups = cut(0, part1)
    mids = cut(part1, part1 + part2)
    lates = cut(part1 + part2, part1 + part2 + part3)
    table = lates[:, width : width + TABLE]
    refs.flat[:, :width] = mids[:, :width]
    refs.flat[:, width : 2 * width] = lates[:, :width]
    moved = jnp.concatenate([mids[:, width : 3 * width], ups, pltpu.roll(table, TABLE - 4, 1)], axis=1)
    refs.flat[:, 2 * width :] = pltpu.roll(moved, 4, 1)
    total = refs.wide[0]
    for index in range(1, refs.wide.shape[0]):
        total = total + refs.wide[index]
    norm = jnp.sqrt(total)
    refs.norm[...] = norm
    scale = jnp.minimum(1.0, CLIP_NORM / (norm[0:1, 0:1] + 1e-06))
    columns = refs.params.shape[1]
    for lanes in tiles(0, columns, 512):
        new = adam_rows(
            refs.params[:, lanes], refs.flat[:, lanes], refs.first[:, lanes], refs.second[:, lanes], scale
        )
        for name, value in zip(("new_params", "new_first", "new_second"), new):
            refs[name][:, lanes] = value


def local(sizes, x_big, x_small, cot_big, cot_small, counts, params, first, second):
    n_dp, n_z, n_core = sizes
    fsdp = ("z", "core")
    everywhere = ("dp",) + fsdp
    width = x_big.shape[-1]
    hidden = FFN
    plan = Plan(x_big.shape, x_small.shape)
    consts = constants(plan)
    height = params.shape[0]
    mod_at = 2 * width + 4
    tail_at = mod_at + 2 * width + 2 * hidden
    tail = params.shape[1] - tail_at
    power = all(size & (size - 1) == 0 for size in sizes)
    blocked = height % 16 == 0 and n_core == 2 and power and n_dp <= 4 and n_z <= 4

    def over(part, axis, step):
        return lax.ppermute(part, axis, [(index, index ^ step) for index in range(sizes[axis_of[axis]])])

    axis_of = dict(dp=0, z=1, core=2)
    shard = params.astype(BF16)
    empty = lambda columns: [jnp.zeros((height, columns), BF16)]
    shard_a = [shard[:, width : 2 * width], shard[:, :width], shard[:, 2 * width : mod_at], shard[:, tail_at:]]
    shard_a = jnp.concatenate(shard_a + empty(2 * TABLE - 4 - tail), axis=1)
    shard_b = jnp.concatenate([shard[:, mod_at:tail_at]] + empty(2 * TABLE), axis=1)
    if blocked:
        me, my_z = lax.axis_index("dp"), lax.axis_index("z")
        split_a, split_b = shard_a.shape[1] // n_dp, shard_b.shape[1] // n_dp
        mine = [lax.dynamic_slice_in_dim(table, me * size, size, 1) for table, size in ((shard_a, split_a), (shard_b, split_b))]
        mine = jnp.concatenate(mine, axis=1)
        all_z = jnp.stack([mine] + [over(mine, "z", step) for step in range(1, n_z)])

        def over_dp(part):
            return [part] + [over(part, "dp", step) for step in range(1, n_dp)]

        def with_core(parts):
            return [one for part in parts for one in (part, over(part, "core", 1))]

        pieces_a, pieces_b = with_core(over_dp(all_z[:, :, :split_a])), over_dp(all_z[:, :, split_a:])
    else:
        pieces_a, pieces_b = ([lax.all_gather(part, fsdp, axis=0, tiled=True)] for part in (shard_a, shard_b))
    count_pair = counts.reshape(2)
    live_big = (jnp.arange(x_big.shape[0]) < count_pair[0]).astype(BF16)
    live_small = (jnp.arange(x_small.shape[0]) < count_pair[1]).astype(BF16)
    x_rows = to_rows(plan, x_big, x_small)
    wl = to_rows(plan, cot_big * live_big[:, None, None, None], cot_small * live_small[:, None, None, None])
    if blocked:
        share1 = Shares(sizes, width, 2 * hidden, True)
        share2 = Shares(sizes, width, 3 * width, True)
        share3 = Shares(sizes, width, width + TABLE, False)
    else:
        share1, share2, share3 = Plain(width, 2 * hidden), Plain(width, 3 * width), Plain(width, width + TABLE)

    one = mix_forward(plan, consts, x_rows, pieces_a, sizes)
    if blocked:
        *pieces_b, one["mixed"] = lax.optimization_barrier((*pieces_b, one["mixed"]))
        pieces_b = with_core(pieces_b)
    mid = middle_pass(plan, consts, share1, x_rows, wl, one, pieces_b, sizes)
    if blocked:
        got1 = over(mid["give"], "core", 1)
    back = product_pass(plan, share2, one, mid)
    if blocked:
        got2 = over(back["give"], "core", 1)
        pick = lambda table, index: lax.dynamic_index_in_dim(table, index, 0, keepdims=False)

        def part_of(step):
            at = me ^ step
            halves = [pick(a, at) + pick(b, at) for a, b in ((mid["keep"], got1), (back["keep"], got2))]
            return jnp.concatenate(halves, axis=-1)

        by_dp = [part_of(0)] + [over(part_of(step), "dp", step) for step in range(1, n_dp)]
    mix = mix_backward(plan, consts, one, back)
    if blocked:
        *by_dp, mix["glow"] = lax.optimization_barrier((*by_dp, mix["glow"]))
        summed = sum(part.astype(F32) for part in by_dp).astype(BF16)
        by_z = [pick(summed, my_z)] + [over(pick(summed, my_z ^ step), "z", step) for step in range(1, n_z)]
    end = input_pass(plan, consts, share3, x_rows, one, mid, back, mix)
    out_big, out_small = from_rows(plan, mid["out"], x_big.shape, x_small.shape)
    grad_big, grad_small = from_rows(plan, end["gx"], x_big.shape, x_small.shape)
    images = (out_big, out_small, grad_big, grad_small)
    if not blocked:
        early = [mid["keep"], back["keep"]]
        grads, square = whole_sums(plan, sizes, tail, end["g3"], early, width + TABLE)
        grad_norm = jnp.sqrt(square)
        scale = jnp.minimum(1.0, CLIP_NORM / (grad_norm + 1e-06))
        return images + adam_rows(params, grads, first, second, scale) + (grad_norm,)
    count = n_dp * n_z * n_core
    *by_z, late = lax.optimization_barrier((*by_z, end["g3"]))
    both = lax.all_to_all(late.reshape(count, height, share3.part), everywhere, 0, 0)
    early = sum(part.astype(F32) for part in by_z).astype(BF16)
    owned = [early] + [over(early, "dp", step) for step in range(1, n_dp)]
    both, *rest = lax.optimization_barrier((both,) + images + tuple(owned))
    images, owned = tuple(rest[:4]), rest[4:]
    sums = run(
        late_sums,
        dict(both=both, early=owned[0]),
        dict(late=((height, share3.part), BF16), wide=((count, 8, TABLE), F32)),
        {},
        micros=2,
        limit=4 * 2**20,
    )
    wide = lax.all_to_all(sums["wide"], everywhere, 0, 0)
    late = [sums["late"]] + [over(sums["late"], "dp", step) for step in range(1, n_dp)]
    state = ((height, params.shape[1]), F32)
    inputs = dict({"o" + str(step): part for step, part in enumerate(owned)}, wide=wide)
    inputs.update({"l" + str(step): part for step, part in enumerate(late)})
    new = run(
        partial(optimizer, plan, sizes, (share1.part, share2.part, share3.part), tail),
        dict(inputs, params=params, first=first, second=second),
        dict(new_params=state, new_first=state, new_second=state, norm=((8, TABLE), F32)),
        dict(
            by_dp=((n_dp, height, share1.part + share2.part + share3.part), F32),
            flat=((height, up_to(params.shape[1], TABLE)), F32),
        ),
        micros=3,
        limit=16 * 2**20,
    )
    return images + (new["new_params"], new["new_first"], new["new_second"], new["norm"][0, 0])


def solution(mesh):
    n_dp, n_fsdp = mesh.shape["dp"], mesh.shape["fsdp"]
    n_core = 2 if n_fsdp % 2 == 0 else 1
    n_z = n_fsdp // n_core
    split = jax.sharding.Mesh(mesh.devices.reshape(n_dp, n_z, n_core), ("dp", "z", "core"))
    images = P(("dp", "z", "core"), None, None, None)
    rows = P(("z", "core"), None)
    in_specs = (images,) * 4 + (P("dp", ("z", "core"), None),) + (rows,) * 3
    out_specs = (images,) * 4 + (rows,) * 3 + (P(),)
    return jax.shard_map(
        partial(local, (n_dp, n_z, n_core)), mesh=split, in_specs=in_specs, out_specs=out_specs, check_vma=False
    )
```

```python
from functools import partial

import jax
import jax.numpy as jnp
import numpy as np
from jax import lax
from jax.experimental import pallas as pl
from jax.experimental.pallas import tpu as pltpu
from jax.sharding import PartitionSpec as P

FFN = 1536
STEP = 10
CLIP_NORM = 1.0
BETA_ONE = 0.9
BETA_TWO = 0.999
LEARN_RATE = 0.05
DECAY_RATE = 0.05
ADAM_EPS = 1e-08
KERNEL_SIDES = (3, 5, 7)
F32 = jnp.float32
BF16 = jnp.bfloat16
VMEM_BYTES = 58 * 2**20

SLOT = 16


def up_to(value, step):
    return -(-value // step) * step


class Plan:
    def __init__(self, big_shape, small_shape):
        self.n_big, self.side_big = big_shape[0], big_shape[1]
        self.n_small, self.side_small = small_shape[0], small_shape[1]
        self.width = big_shape[3]
        self.pix_big = self.side_big**2
        self.pix_small = self.side_small**2
        self.rows_big = up_to(self.pix_big, SLOT)
        self.group = max(size for size in (1, 2, 3) if self.n_small % size == 0)
        self.n_groups = self.n_small // self.group
        self.rows_small = up_to(self.group * self.pix_small, SLOT)
        self.small_at = self.n_big * self.rows_big
        self.used = self.small_at + self.n_groups * self.rows_small
        self.rows = up_to(self.used, 256)
        self.n_images = self.n_big + self.n_small
        self.image_rows = up_to(self.n_images, SLOT)


def half_spectrum(size):
    reps = []
    for u in range(size):
        for v in range(size):
            other = ((-u) % size, (-v) % size)
            if (u, v) <= other:
                reps.append((u, v, 1.0 if (u, v) == other else 2.0))
    return np.array(reps)


def transform_pair(side, kernel_side, copies):
    margin = kernel_side // 2
    size = side + margin
    reps = half_spectrum(size)
    count = len(reps)
    freq = 2 * np.pi * reps[:, :2] / size
    grid = np.array([(i, j) for i in range(side) for j in range(side)], float)
    lags = np.array([(i - margin, j - margin) for i in range(kernel_side) for j in range(kernel_side)], float)
    phase = freq @ grid.T
    lag_phase = freq @ lags.T
    weight = reps[:, 2:3] / size**2
    pix = side * side
    half = up_to(copies * count, SLOT)
    rows = up_to(copies * pix, SLOT)
    forward = np.zeros((2 * half, rows))
    inverse = np.zeros((rows, 2 * half))
    taps = np.zeros((2 * half, kernel_side**2))
    back = np.zeros((kernel_side**2, 2 * half))
    for one in range(copies):
        low, col = one * count, one * pix
        forward[low : low + count, col : col + pix] = np.cos(phase)
        forward[half + low : half + low + count, col : col + pix] = -np.sin(phase)
        inverse[col : col + pix, low : low + count] = (weight * np.cos(phase)).T
        inverse[col : col + pix, half + low : half + low + count] = -(weight * np.sin(phase)).T
        taps[low : low + count] = np.cos(lag_phase)
        taps[half + low : half + low + count] = np.sin(lag_phase)
        back[:, low : low + count] = (weight * np.cos(lag_phase)).T
        back[:, half + low : half + low + count] = -(weight * np.sin(lag_phase)).T
    return forward, inverse, taps, back


TABLE = 128
GATES_AT = 0
TAPS_AT = 4
VECS_AT = 87
BIAS_AT = 96


def low_np(values):
    return jnp.asarray(values, F32).astype(BF16)


def high_and_rest(values):
    high = values.astype(np.float32).astype(jnp.bfloat16)
    rest = (values - high.astype(np.float64)).astype(np.float32).astype(jnp.bfloat16)
    return jnp.asarray(high), jnp.asarray(rest)


def constants(plan):
    consts = {}
    tap_at = TAPS_AT
    for level, kernel_side in enumerate(KERNEL_SIDES):
        for kind, side, copies in (("b", plan.side_big, 1), ("s", plan.side_small, plan.group)):
            forward, inverse, taps, back = transform_pair(side, kernel_side, copies)
            wide = np.zeros((taps.shape[0], TABLE))
            wide[:, tap_at : tap_at + kernel_side**2] = taps
            tall = np.zeros((TABLE, taps.shape[0]))
            tall[tap_at : tap_at + kernel_side**2] = back
            consts["f" + kind + str(level)] = low_np(forward)
            consts["g" + kind + str(level)] = low_np(inverse)
            high, rest = high_and_rest(wide)
            consts["k" + kind + str(level)] = jnp.concatenate([high, rest], axis=1)
            consts["t" + kind + str(level)] = low_np(tall)
        tap_at += kernel_side**2
    pick = np.zeros((plan.image_rows, plan.rows))
    for one in range(plan.n_big):
        pick[one, one * plan.rows_big : one * plan.rows_big + plan.pix_big] = 1.0
    for one in range(plan.n_small):
        at = plan.small_at + one // plan.group * plan.rows_small + one % plan.group * plan.pix_small
        pick[plan.n_big + one, at : at + plan.pix_small] = 1.0
    consts["pick"] = low_np(pick)
    consts["spread"] = low_np(pick.T)
    consts["eye"] = low_np(np.eye(TABLE))
    lanes = np.zeros((FFN, plan.width))
    lanes[np.arange(FFN), np.arange(FFN) // (FFN // plan.width)] = 1.0
    consts["lanes"] = low_np(lanes)
    return consts


def dot(left, right):
    return jnp.dot(left, right, preferred_element_type=F32)


def dot_nt(left, right):
    return lax.dot_general(left, right, (((1,), (1,)), ((), ())), preferred_element_type=F32)


def dot_tn(left, right):
    return lax.dot_general(left, right, (((0,), (0,)), ((), ())), preferred_element_type=F32)


def tiles(low, high, step):
    for at in range(low, high, step):
        yield slice(at, min(at + step, high))


def gelu_and_slope(values):
    chance = 0.5 + 0.5 * lax.erf(values * 0.7071067811865476)
    bell = jnp.exp(values * values * -0.5) * 0.3989422804014327
    return values * chance, chance + values * bell


class Refs(dict):
    def __getattr__(self, name):
        return self[name]

    def setup(self, fetched, sent):
        self.used = 0
        self.open = {}
        self.leaving = []
        self.sent = sent
        self.waiting = dict(fetched)

    def copy(self, source, target):
        result = pltpu.make_async_copy(source, target, self["sems"].at[self.used])
        result.start()
        self.used += 1
        return result

    def begin(self, *names):
        for name in names or tuple(self.waiting):
            source, lanes = self.waiting.pop(name)
            far = self[source] if lanes is None else self[source].at[:, lanes]
            self.open[name] = self.copy(far, self[name])

    def need(self, *names):
        for name in names:
            if name in self.open:
                self.open.pop(name).wait()

    def send(self, name, at=None):
        far, near = self["far_" + name], self[name]
        if at is not None:
            far, near = far.at[at], near.at[at]
        self.leaving.append(self.copy(near, far))

    def finish(self):
        self.need(*list(self.open))
        for copy in self.leaving:
            copy.wait()


COPIES = 96


def run(body, inputs, outputs, scratch, fetched=None, sent=(), far=(), micros=20, limit=VMEM_BYTES):
    fetched = {name: (name, None) if entry is None else entry for name, entry in (fetched or {}).items()}
    sources = {source for source, _ in fetched.values()}
    buffers = {}
    for name, (source, lanes) in fetched.items():
        shape = inputs[source].shape
        if lanes is not None:
            shape = (shape[0], lanes.stop - lanes.start)
        buffers["near_" + name] = (shape, inputs[source].dtype)
    for name in sent:
        buffers["near_" + name] = outputs[name]
    names = ["in_" + name for name in inputs] + ["out_" + name for name in outputs] + list(scratch) + list(buffers)

    def kernel(*args):
        given = dict(zip(names + ["sems"], args))
        refs = Refs()
        for name in inputs:
            refs[name] = given["in_" + name]
        for name in outputs:
            refs["far_" + name if name in sent else name] = given["out_" + name]
        for name in list(scratch) + ["sems"]:
            refs[name] = given[name]
        entries = {}
        for name, (source, lanes) in fetched.items():
            refs["source_" + source] = given["in_" + source]
            entries[name] = ("source_" + source, lanes)
        for name in list(fetched) + list(sent):
            refs[name] = given["near_" + name]
        refs.setup(entries, sent)
        body(refs)
        refs.finish()

    def space(name, distant):
        return pl.BlockSpec(memory_space=pl.ANY if distant else pltpu.VMEM)

    results = pl.pallas_call(
        kernel,
        in_specs=[space(name, name in sources or name in far) for name in inputs],
        out_specs=[
            pl.BlockSpec(memory_space=pltpu.SMEM) if shape == (1, 1) else space(name, name in sent or name in far)
            for name, (shape, _) in outputs.items()
        ],
        out_shape=[jax.ShapeDtypeStruct(shape, dtype) for shape, dtype in outputs.values()],
        scratch_shapes=[pltpu.VMEM(*entry) for entry in list(scratch.values()) + list(buffers.values())]
        + [pltpu.SemaphoreType.DMA((COPIES,))],
        compiler_params=pltpu.CompilerParams(vmem_limit_bytes=limit),
        cost_estimate=pl.CostEstimate(flops=micros * 10**9, bytes_accessed=micros * 10**6, transcendentals=0),
    )(*inputs.values())
    return dict(zip(outputs, results))


def units(plan):
    result = []
    for one in range(plan.n_big):
        result.append(("b", slice(one * plan.rows_big, (one + 1) * plan.rows_big), len(result)))
    for one in range(plan.n_groups):
        at = plan.small_at + one * plan.rows_small
        result.append(("s", slice(at, at + plan.rows_small), len(result)))
    return result


def pairs(plan):
    result = []
    for kind in "bs":
        same = [unit for unit in units(plan) if unit[0] == kind]
        result += [same[low : low + 2] for low in range(0, len(same), 2)]
    return result


def side_by_side(values):
    return values[0] if len(values) == 1 else jnp.concatenate(values, axis=1)


def wave_rows(plan, consts):
    result, total = {}, []
    for level in range(3):
        at = 0
        for kind, _, index in units(plan):
            count = consts["f" + kind + str(level)].shape[0]
            result[level, index] = slice(at, at + count)
            at += count
        total.append(at)
    return result, total


def spectrum_of_taps(refs, name, table):
    refs["h" + name][...] = dot_nt(refs["k" + name][:, :TABLE], table) + dot_nt(refs["k" + name][:, TABLE:], table)


def image_scale(plan):
    row = lax.broadcasted_iota(jnp.int32, (plan.image_rows, 1), 0)
    return jnp.where(row < plan.n_big, 1.0 / plan.pix_big, 1.0 / plan.pix_small).astype(F32)


def unit_rows(values):
    center = values - jnp.mean(values, axis=-1, keepdims=True)
    scale = lax.rsqrt(jnp.mean(center * center, axis=-1, keepdims=True) + 1e-05)
    return center * scale, scale


def fold(values):
    total = values[0:8]
    for low in range(8, values.shape[0], 8):
        total = total + values[low : low + 8]
    return total


def column_sum(values):
    return jnp.sum(values, axis=0, keepdims=True)


def forward_mix(plan, places, sizes, n_pieces, refs):
    rows, width, hidden = plan.rows, plan.width, FFN
    arriving = gather(refs, sizes, n_pieces, "wa")
    refs.begin()
    for copy in arriving:
        copy.wait()
    refs.send("wa")
    refs.need("eye")
    table = refs.wa[:, width:]
    refs.vec[...] = dot_nt(refs.eye[...], table)
    refs.need("x")
    gain = refs.vec[VECS_AT : VECS_AT + 1, :]
    shift = refs.vec[VECS_AT + 1 : VECS_AT + 2, :]
    for block in tiles(0, rows, 256):
        for at in tiles(block.start, block.stop, 32):
            unit, _ = unit_rows(refs.x[at, :].astype(F32))
            refs.normed[at, :] = (unit * gain + shift).astype(BF16)
        refs.send("normed", block)
        part = dot(refs.normed[block, :], refs.wa[...])
        refs.context[block, :] = (part[:, :width] + refs.vec[VECS_AT + 3 : VECS_AT + 4, :]).astype(BF16)
        refs.gate[block, :] = part[:, width:]
    refs.send("gate")
    if rows > plan.used:
        refs.c[:, plan.used :, :] = jnp.zeros((3, rows - plan.used, width), BF16)
        refs.gp[:, plan.used :, :] = jnp.zeros((3, rows - plan.used, width), BF16)
    for level in range(3):
        for kind in "bs":
            refs.need("f" + kind + str(level), "k" + kind + str(level), "g" + kind + str(level))
            spectrum_of_taps(refs, kind + str(level), table)
        hat = refs["hat" + str(level)]
        field_in = refs.context if level == 0 else refs.c.at[level - 1]
        for pair in pairs(plan):
            name = pair[0][0] + str(level)
            count = refs["f" + name].shape[0]
            half = count // 2
            taps = refs["h" + name]
            both = dot(refs["f" + name][...], side_by_side([field_in[at, :] for _, at, _ in pair]))
            for place, (_, at, index) in enumerate(pair):
                wave, low_wave = refs.wave.at[index], refs.wave_low.at[index]
                wave[:count, :] = both[:, place * width : (place + 1) * width]
                saved = places[level, index].start
                for re in tiles(0, half, 16):
                    im = slice(half + re.start, half + re.stop)
                    wave_re, wave_im = wave[re, :], wave[im, :]
                    tap_re, tap_im = taps[re, :], taps[im, :]
                    hat[saved + re.start : saved + re.stop, :] = wave_re.astype(BF16)
                    hat[saved + im.start : saved + im.stop, :] = wave_im.astype(BF16)
                    low_wave[re, :] = (wave_re * tap_re - wave_im * tap_im).astype(BF16)
                    low_wave[im, :] = (wave_re * tap_im + wave_im * tap_re).astype(BF16)
            both = dot(refs["g" + name][...], side_by_side([refs.wave_low[index, :count, :] for _, _, index in pair]))
            for place, (_, at, index) in enumerate(pair):
                refs.field[at, :] = both[:, place * width : (place + 1) * width]
                for into in tiles(at.start, at.stop, 16):
                    value, slope = gelu_and_slope(refs.field[into, :])
                    refs.c[level, into, :] = value.astype(BF16)
                    refs.gp[level, into, :] = slope.astype(BF16)
        refs.send("c", slice(level, level + 1))
        refs.send("gp", slice(level, level + 1))
        refs.send("hat" + str(level))
    refs.need("pick", "spread")
    mean = dot(refs.pick[...], refs.c[2]) * image_scale(plan)
    summary, slope = gelu_and_slope(mean)
    refs.sum[0] = summary
    refs.sum[1] = slope
    summary_low = summary.astype(BF16)
    for block in tiles(0, rows, 256):
        refs.field[block, :] = dot(refs.spread[block, :], summary_low)
        for at in tiles(block.start, block.stop, 32):
            gate = refs.gate[at, :]
            total = refs.field[at, :] * gate[:, 3:4]
            for level in range(3):
                total += refs.c[level, at, :].astype(F32) * gate[:, level : level + 1]
            refs.mixed[at, :] = total.astype(BF16)
        refs.send("mixed", block)
    refs.need("lanes")
    ratio = hidden // width
    spread = dot_nt(refs.vec[BIAS_AT : BIAS_AT + 16, :].astype(BF16), refs.lanes[...])
    row = lax.broadcasted_iota(jnp.int32, (16, hidden), 0)
    lane = lax.broadcasted_iota(jnp.int32, (16, hidden), 1)
    picked = jnp.where(lax.rem(lane, ratio) == row, spread, 0.0)
    refs.upb[...] = jnp.broadcast_to(jnp.sum(picked, axis=0, keepdims=True), (8, hidden))


def mix_scratch(plan, consts):
    scratch = {}
    for level in range(3):
        for kind in "bs":
            scratch["h" + kind + str(level)] = ((consts["f" + kind + str(level)].shape[0], plan.width), F32)
    return scratch


def most_waves(consts):
    return max(consts["f" + kind + str(level)].shape[0] for level in range(3) for kind in "bs")


def mix_forward(plan, consts, x_rows, pieces, sizes):
    rows, width = plan.rows, plan.width
    waves, n_units = most_waves(consts), len(units(plan))
    places, saved = wave_rows(plan, consts)
    keys = [k + kind + str(level) for level in range(3) for kind in "bs" for k in "fkg"]
    names = ["eye"] + keys + ["pick", "spread", "lanes"]
    inputs = dict(x=x_rows, **{k: consts[k] for k in names})
    apart = {"w" + str(step): piece for step, piece in enumerate(pieces)}
    inputs.update(apart)
    outputs = dict(
        wa=((width, width + TABLE), BF16),
        normed=((rows, width), BF16),
        c=((3, rows, width), BF16),
        gp=((3, rows, width), BF16),
        **{"hat" + str(level): ((saved[level], width), BF16) for level in range(3)},
        mixed=((rows, width), BF16),
        gate=((rows, TABLE), F32),
        vec=((TABLE, width), F32),
        upb=((8, FFN), F32),
        sum=((2, plan.image_rows, width), F32),
    )
    scratch = dict(
        wave=((n_units, waves, width), F32),
        wave_low=((n_units, waves, width), BF16),
        field=((rows, width), F32),
        context=((rows, width), BF16),
        **mix_scratch(plan, consts),
    )
    sent = ("normed", "c", "gp", "hat0", "hat1", "hat2", "mixed", "gate")
    sent += ("wa",)
    body = partial(forward_mix, plan, places, sizes, len(pieces))
    return run(body, inputs, outputs, scratch, {k: None for k in ["x"] + names}, sent, list(apart), 20)


def gather(refs, sizes, n_pieces, target):
    n_dp, n_z, n_core = sizes
    if n_pieces == 1:
        return [refs.copy(refs["w0"], refs[target])]
    copies = []
    me, my_z, my_core = (lax.axis_index(name) for name in ("dp", "z", "core"))

    def place(piece, z, step, lanes):
        height = piece.shape[0]
        owner = (my_z ^ z) * n_core + (my_core ^ (step % n_core))
        copies.append(refs.copy(piece, refs[target].at[pl.ds(pl.multiple_of(owner * height, 16), height), lanes]))

    for step in range(n_pieces):
        piece = refs["w" + str(step)]
        if len(piece.shape) == 2:
            place(piece, step // n_core, step, slice(None))
            continue
        part = piece.shape[2]
        lanes = pl.ds(pl.multiple_of((me ^ (step // n_core)) * part, TABLE), part)
        for other in range(n_z):
            place(piece.at[other], other, step, lanes)
    return copies


class Shares:
    def __init__(self, sizes, rows, columns):
        self.n_dp, self.n_z, self.n_core = sizes
        self.height = rows // (self.n_z * self.n_core)
        self.part = up_to(columns, TABLE * self.n_dp) // self.n_dp
        self.empty = self.part * self.n_dp - columns
        self.shape = (self.n_core, self.n_dp, self.n_z, self.height, self.part)
        self.columns = columns

    def put(self, ref, low, values):
        done = 0
        while done < values.shape[1]:
            share, at = divmod(low + done, self.part)
            take = min(self.part - at, values.shape[1] - done)
            for owner in range(self.n_z * self.n_core):
                z, core = divmod(owner, self.n_core)
                ref[core, share, z, :, at : at + take] = values[
                    owner * self.height : (owner + 1) * self.height, done : done + take
                ]
            done += take

    def close(self, refs, stage, names):
        if self.empty:
            self.put(stage, self.columns, jnp.zeros((self.height * self.n_z * self.n_core, self.empty), BF16))
        core = lax.axis_index("core")
        for source, name in ((1 - core, names[1]), (core, names[0])):
            refs.leaving.append(refs.copy(stage.at[source], refs[name]))


class Plain:
    def __init__(self, rows, columns):
        self.shape = (rows, columns)

    def put(self, ref, low, values):
        ref[:, low : low + values.shape[1]] = values

    def close(self, refs, stage, names):
        refs.leaving.append(refs.copy(stage, refs[names[0]]))


def middle(plan, shares, sizes, n_pieces, refs):
    rows, width, hidden = plan.rows, plan.width, FFN
    vec = lambda index: refs.vec[VECS_AT + index : VECS_AT + index + 1, :]
    zero = jnp.zeros((8, width), F32)
    sums = {index: zero for index in (2, 4, 5, 6, 7, 8)}
    blocks = list(tiles(0, rows, 256))
    up_at = 3 * width
    down_at = up_at + hidden
    wq, wm, wo = (refs.wb.at[:, at * width : (at + 1) * width] for at in range(3))
    wu, wd = refs.wb.at[:, up_at:down_at], refs.wb.at[:, down_at : down_at + hidden]
    refs.begin("mixed", "normed")
    arriving = gather(refs, sizes, n_pieces, "wb")
    refs.begin()
    refs.need("mixed", "normed")
    for copy in arriving:
        copy.wait()
    refs.leaving.append(refs.copy(wq, refs.wq))

    def before(block):
        modulator = dot(refs.mixed[block, :], wm[...]) + vec(4)
        queries = dot(refs.normed[block, :], wq[...]) + vec(2)
        refs.mod[block, :] = modulator.astype(BF16)
        refs.q[block, :] = queries.astype(BF16)
        refs.prod[block, :] = (queries * modulator).astype(BF16)
        yield
        refs.need("x")
        refs.resid[block, :] = dot(refs.prod[block, :], wo[...])
        yield
        for part in tiles(block.start, block.stop, 64):
            for at in tiles(part.start, part.stop, 32):
                resid = refs.resid[at, :] + refs.x[at, :].astype(F32) + vec(5)
                refs.resid[at, :] = resid
                unit, scale = unit_rows(resid)
                refs.unit[at, :] = unit
                refs.scale[at, :] = jnp.broadcast_to(scale, (scale.shape[0], TABLE))
                refs.n2[at, :] = (unit * vec(6) + vec(7)).astype(BF16)
            yield

    def mlp(block):
        refs.need("wl")
        for index, lanes in enumerate(tiles(0, hidden, 256)):
            pre, grad_act = refs.pa.at[index % 3], refs.ga.at[index % 3]
            pre[...] = dot(refs.n2[block, :], wu[:, lanes])
            grad_act[...] = dot(refs.wl[block, :], wd[:, lanes])
            bias = refs.upb[0:1, lanes]
            total = jnp.zeros((8, 256), F32) if block.start == 0 else refs.gub[:, lanes]
            for low in tiles(0, 256, 16):
                at = slice(block.start + low.start, block.start + low.stop)
                value, slope = gelu_and_slope(pre[low, :] + bias)
                grad = grad_act[low, :] * slope
                refs.act[at, lanes] = value.astype(BF16)
                refs.pre[at, lanes] = grad.astype(BF16)
                total = total + fold(grad)
            refs.gub[:, lanes] = total
            yield

    def after(block):
        refs.gn[block, :] = dot_nt(refs.pre[block, :], wu[...])
        yield
        refs.out[block, :] = (refs.resid[block, :] + dot_nt(refs.act[block, :], wd[...]) + vec(8)).astype(BF16)
        refs.send("out", block)
        yield
        for part in tiles(block.start, block.stop, 128):
            for at in tiles(part.start, part.stop, 32):
                grad = refs.gn[at, :]
                unit = refs.unit[at, :]
                weighted = refs.wl[at, :].astype(F32)
                gained = grad * vec(6)
                mean_one = jnp.mean(gained, axis=-1, keepdims=True)
                mean_two = jnp.mean(gained * unit, axis=-1, keepdims=True)
                result = weighted + refs.scale[at, 0:1] * (gained - mean_one - unit * mean_two)
                refs.gres[at, :] = result
                refs.glow[at, :] = result.astype(BF16)
                for index, new in ((6, grad * unit), (7, grad), (5, result), (8, weighted)):
                    sums[index] = sums[index] + fold(new)
            yield
        refs.send("gres", block)
        refs.gn[block, :] = dot_nt(refs.glow[block, :], wo[...])
        yield
        for at in tiles(block.start, block.stop, 32):
            grad = refs.gn[at, :]
            grad_query = grad * refs.mod[at, :].astype(F32)
            grad_mod = grad * refs.q[at, :].astype(F32)
            refs.gq[at, :] = grad_query.astype(BF16)
            refs.gmod[at, :] = grad_mod.astype(BF16)
            for index, new in ((2, grad_query), (4, grad_mod)):
                sums[index] = sums[index] + fold(new)
        refs.send("gq", block)
        refs.gmix[block, :] = dot_nt(refs.gmod[block, :], wm[...]).astype(BF16)
        refs.send("gmix", block)
        yield

    def together(*steps):
        steps = list(steps)
        while steps:
            steps = [step for step in steps if next(step, refs) is not refs]

    together(before(blocks[0]))
    for index in range(len(blocks) + 1):
        steps = []
        if index < len(blocks):
            steps.append(mlp(blocks[index]))
        if index + 1 < len(blocks):
            steps.append(before(blocks[index + 1]))
        if index:
            steps.append(after(blocks[index - 1]))
        together(*steps)
    for lanes in tiles(0, hidden, 256):
        shares.put(refs.stage, lanes.start, dot_tn(refs.n2[...], refs.pre[:, lanes]).astype(BF16))
        shares.put(refs.stage, hidden + lanes.start, dot_tn(refs.wl[...], refs.act[:, lanes]).astype(BF16))
    at = 2 * hidden
    for left, right in ((refs.normed, refs.gq), (refs.mixed, refs.gmod), (refs.prod, refs.glow)):
        shares.put(refs.stage, at, dot_tn(left[...], right[...]).astype(BF16))
        at += width
    shares.close(refs, refs.stage, ("keep", "give"))
    refs.gv[...] = jnp.zeros(refs.gv.shape, F32)
    for index, total in sums.items():
        refs.gv[index : index + 1, :] = column_sum(total)
    ratio = hidden // width
    row = lax.broadcasted_iota(jnp.int32, (16, hidden), 0)
    lane = lax.broadcasted_iota(jnp.int32, (16, hidden), 1)
    picked = jnp.where(lax.rem(lane, ratio) == row, column_sum(refs.gub[...]), 0.0).astype(BF16)
    refs.need("lanes")
    refs.gv[16:32, :] = dot(picked, refs.lanes[...])


def kept(shares):
    if isinstance(shares, Plain):
        return dict(keep=(shares.shape, BF16))
    return dict(keep=(shares.shape[1:], BF16), give=(shares.shape[1:], BF16))


def middle_pass(plan, consts, shares, x_rows, wl, first, pieces, sizes):
    rows, width, hidden = plan.rows, plan.width, FFN
    near = dict(mixed=first["mixed"], normed=first["normed"], x=x_rows, wl=wl, lanes=consts["lanes"])
    apart = {"w" + str(step): piece for step, piece in enumerate(pieces)}
    inputs = dict(near, vec=first["vec"], upb=first["upb"], **apart)
    token, field, wide = ((rows, width), BF16), ((rows, width), F32), ((rows, hidden), BF16)
    outputs = dict(kept(shares), out=token, gq=token, gmix=token, gres=field)
    outputs.update(wq=((width, width), BF16), gv=((32, width), F32))
    scratch = dict(mod=token, q=token, prod=token, glow=token, gmod=token, n2=token)
    scratch.update(resid=field, unit=field, gn=field, act=wide, pre=wide)
    scratch.update(
        scale=((rows, TABLE), F32),
        pa=((3, 256, 256), F32),
        ga=((3, 256, 256), F32),
        gub=((8, hidden), F32),
        stage=(shares.shape, BF16),
        wb=((width, up_to(3 * width + 2 * hidden, TABLE * sizes[0])), BF16),
    )
    body = partial(middle, plan, shares, sizes, len(pieces))
    far = ["keep", "give", "wq"] + list(apart)
    return run(body, inputs, outputs, scratch, {k: None for k in near}, ("out", "gq", "gmix", "gres"), far, 26)


def backward_mix(plan, places, refs):
    rows, width = plan.rows, plan.width
    refs.begin()
    refs.need("gmix", "gate")
    for at in tiles(0, rows, 32):
        refs.tmp[at, :] = (refs.gmix[at, :].astype(F32) * refs.gate[at, 3:4]).astype(BF16)
    refs.need("pick", "spread", "table")
    table = refs.table[...]
    grad_summary = dot(refs.pick[...], refs.tmp[...]) * refs.sum[1] * image_scale(plan)
    grad_summary_low = grad_summary.astype(BF16)
    for block in tiles(0, rows, 256):
        refs.gc[block, :] = dot(refs.spread[block, :], grad_summary_low)
    summary_low = refs.sum[0].astype(BF16)
    lane = lax.broadcasted_iota(jnp.int32, (1, TABLE), 1)

    def gates(low, high):
        refs.need("c")
        for at in tiles(low, high, 32):
            grad = refs.gmix[at, :].astype(F32)
            spread = dot(refs.spread[at, :], summary_low)
            result = jnp.where(lane == 3, jnp.sum(grad * spread, axis=-1, keepdims=True), 0.0)
            for level in range(3):
                part = jnp.sum(grad * refs.c[level, at, :].astype(F32), axis=-1, keepdims=True)
                result = jnp.where(lane == level, part, result)
            refs.ggate[at, :] = result.astype(BF16)

    taps_total = jnp.zeros((TABLE, width), F32)
    refs.need("gp")
    for level in (2, 1, 0):
        for kind in "bs":
            refs.need("f" + kind + str(level), "k" + kind + str(level), "g" + kind + str(level))
            spectrum_of_taps(refs, kind + str(level), table)
        refs.need("hat" + str(level))
        hat = refs["hat" + str(level)]
        seen = set()
        for pair in pairs(plan):
            kind = pair[0][0]
            name = kind + str(level)
            count = refs["f" + name].shape[0]
            half = count // 2
            taps, cross = refs["h" + name], refs["x" + kind]
            for _, at, _ in pair:
                for into in tiles(at.start, at.stop, 16):
                    direct = refs.gmix[into, :].astype(F32) * refs.gate[into, level : level + 1]
                    grad = refs.gc[into, :] + direct
                    refs.tmp[into, :] = (grad * refs.gp[level, into, :].astype(F32)).astype(BF16)
            both = dot(refs["f" + name][...], side_by_side([refs.tmp[at, :] for _, at, _ in pair]))
            for place, (_, _, index) in enumerate(pair):
                refs.wave[index, :count, :] = both[:, place * width : (place + 1) * width]
            for re in tiles(0, half, 16):
                im = slice(half + re.start, half + re.stop)
                tap_re, tap_im = taps[re, :], taps[im, :]
                cross_re = cross_im = None
                for _, _, index in pair:
                    saved = places[level, index].start
                    wave_re = hat[saved + re.start : saved + re.stop, :].astype(F32)
                    wave_im = hat[saved + im.start : saved + im.stop, :].astype(F32)
                    grad_re, grad_im = refs.wave[index, re, :], refs.wave[index, im, :]
                    refs.wave_low[index, re, :] = (grad_re * tap_re + grad_im * tap_im).astype(BF16)
                    refs.wave_low[index, im, :] = (grad_im * tap_re - grad_re * tap_im).astype(BF16)
                    new_re = grad_re * wave_re + grad_im * wave_im
                    new_im = grad_re * wave_im - grad_im * wave_re
                    cross_re = new_re if cross_re is None else cross_re + new_re
                    cross_im = new_im if cross_im is None else cross_im + new_im
                if kind in seen:
                    cross_re = cross_re + cross[re, :]
                    cross_im = cross_im + cross[im, :]
                cross[re, :] = cross_re
                cross[im, :] = cross_im
            seen.add(kind)
            both = dot(refs["g" + name][...], side_by_side([refs.wave_low[index, :count, :] for _, _, index in pair]))
            for place, (_, at, _) in enumerate(pair):
                refs.gc[at, :] = both[:, place * width : (place + 1) * width]
        for kind in "bs":
            name = kind + str(level)
            count = refs["f" + name].shape[0]
            refs.need("t" + name)
            taps_total = taps_total + dot(refs["t" + name][...], refs["x" + kind][:count, :].astype(BF16))
        if level:
            half = rows // 64 * 32
            gates(*((0, half) if level == 2 else (half, rows)))
    refs.gtab[...] = taps_total
    if rows > plan.used:
        refs.gc[plan.used :, :] = jnp.zeros((rows - plan.used, width), F32)
    context_total = jnp.zeros((8, width), F32)
    for block in tiles(0, rows, 256):
        for at in tiles(block.start, block.stop, 32):
            grad = refs.gc[at, :]
            refs.glow[at, :] = grad.astype(BF16)
            context_total = context_total + fold(grad)
        refs.send("glow", block)
    refs.gtab[VECS_AT + 3 : VECS_AT + 4, :] = column_sum(context_total)


def input_back(plan, shares, refs):
    rows, width = plan.rows, plan.width
    refs.begin()
    refs.need("normed", "glow", "ggate")
    shares.put(refs.stage, 0, dot_tn(refs.normed[...], refs.glow[...]).astype(BF16))
    gates = dot_tn(refs.normed[...], refs.ggate[...])
    zero = jnp.zeros((8, width), F32)
    gain_total, shift_total = zero, zero
    refs.need("wa", "wq", "gq", "x", "gres")
    gain = refs.vec[VECS_AT : VECS_AT + 1, :]
    for block in tiles(0, rows, 256):
        refs.gc[block, :] = (
            dot_nt(refs.gq[block, :], refs.wq[...])
            + dot_nt(refs.glow[block, :], refs.wa[:, :width])
            + dot_nt(refs.ggate[block, :], refs.wa[:, width:])
        )
        for at in tiles(block.start, block.stop, 32):
            unit, scale_row = unit_rows(refs.x[at, :].astype(F32))
            grad = refs.gc[at, :]
            gained = grad * gain
            mean_one = jnp.mean(gained, axis=-1, keepdims=True)
            mean_two = jnp.mean(gained * unit, axis=-1, keepdims=True)
            result = refs.gres[at, :] + scale_row * (gained - mean_one - unit * mean_two)
            refs.gx[at, :] = result.astype(BF16)
            gain_total = gain_total + fold(grad * unit)
            shift_total = shift_total + fold(grad)
        refs.send("gx", block)
    refs.gtab[...] = refs.taps[...]
    refs.gtab[VECS_AT + 4 : VECS_AT + 9, :] = refs.gv[4:9, :]
    refs.gtab[VECS_AT + 2 : VECS_AT + 3, :] = refs.gv[2:3, :]
    refs.gtab[VECS_AT : VECS_AT + 1, :] = column_sum(gain_total)
    refs.gtab[VECS_AT + 1 : VECS_AT + 2, :] = column_sum(shift_total)
    refs.gtab[BIAS_AT : BIAS_AT + 4, :] = refs.gv[16:20, :]
    refs.need("eye")
    small = gates + dot_tn(refs.gtab[...].astype(BF16), refs.eye[...])
    shares.put(refs.stage, width, small.astype(BF16))
    shares.close(refs, refs.stage, ("keep", "give"))


def mix_backward(plan, consts, first, mid):
    rows, width = plan.rows, plan.width
    waves, n_units = most_waves(consts), len(units(plan))
    places, _ = wave_rows(plan, consts)
    keys = [k + kind + str(level) for level in (2, 1, 0) for k in "kfgt" for kind in "bs"]
    hats = {"hat" + str(level): first["hat" + str(level)] for level in range(3)}
    inputs = dict({k: first[k] for k in ("wa", "gate", "c", "gp", "sum")}, gmix=mid["gmix"], **hats)
    inputs.update({k: consts[k] for k in keys + ["pick", "spread"]})
    fetched = dict(gmix=None, gate=None, pick=None, spread=None, table=("wa", slice(width, width + TABLE)), gp=None)
    for level in (2, 1, 0):
        for name in keys:
            if name.endswith(str(level)):
                fetched[name] = None
        fetched["hat" + str(level)] = None
        fetched["c"] = None
    outputs = dict(glow=((rows, width), BF16), ggate=((rows, TABLE), BF16), gtab=((TABLE, width), F32))
    scratch = dict(
        wave=((n_units, waves, width), F32),
        wave_low=((n_units, waves, width), BF16),
        xb=((waves, width), F32),
        xs=((waves, width), F32),
        gc=((rows, width), F32),
        tmp=((rows, width), BF16),
        **mix_scratch(plan, consts),
    )
    return run(partial(backward_mix, plan, places), inputs, outputs, scratch, fetched, ("glow",), micros=18)


def input_pass(plan, consts, shares, x_rows, first, mid, mix):
    rows, width = plan.rows, plan.width
    near = dict(normed=first["normed"], glow=mix["glow"], ggate=mix["ggate"], wa=first["wa"], gq=mid["gq"], x=x_rows)
    near.update(gres=mid["gres"], eye=consts["eye"])
    near.update(wq=mid["wq"])
    inputs = dict(near, taps=mix["gtab"], vec=first["vec"], gv=mid["gv"])
    outputs = dict(kept(shares), gx=((rows, width), BF16))
    scratch = dict(gc=((rows, width), F32), gtab=((TABLE, width), F32), stage=(shares.shape, BF16))
    fetched = {k: None for k in near}
    return run(partial(input_back, plan, shares), inputs, outputs, scratch, fetched, ("gx",), ("keep", "give"), 8)


def adam_rows(params, grads, first, second, scale):
    clipped = grads * scale
    first_new = BETA_ONE * first + (1.0 - BETA_ONE) * clipped
    second_new = BETA_TWO * second + (1.0 - BETA_TWO) * clipped * clipped
    first_hat = first_new * (1.0 / (1.0 - BETA_ONE**STEP))
    second_hat = second_new * (1.0 / (1.0 - BETA_TWO**STEP))
    params_new = params - LEARN_RATE * (first_hat / (jnp.sqrt(second_hat) + ADAM_EPS) + DECAY_RATE * params)
    return (params_new, first_new, second_new)


def to_rows(plan, big, small):
    tables = []
    for images, count, pix, rows in (
        (big, plan.n_big, plan.pix_big, plan.rows_big),
        (small, plan.n_groups, plan.group * plan.pix_small, plan.rows_small),
    ):
        table = jnp.pad(images.reshape(count, pix, plan.width), ((0, 0), (0, rows - pix), (0, 0)))
        tables.append(table.reshape(count * rows, plan.width))
    if plan.rows > plan.used:
        tables.append(jnp.zeros((plan.rows - plan.used, plan.width), big.dtype))
    return jnp.concatenate(tables, axis=0)


def from_rows(plan, table, big_shape, small_shape):
    big = table[: plan.small_at].reshape(plan.n_big, plan.rows_big, plan.width)[:, : plan.pix_big]
    small = table[plan.small_at : plan.used].reshape(plan.n_groups, plan.rows_small, plan.width)
    return big.reshape(big_shape), small[:, : plan.group * plan.pix_small].reshape(small_shape)


def whole_sums(plan, sizes, tail, late, early, late_columns):
    fsdp = ("z", "core")
    width, hidden = plan.width, FFN
    rows = late.shape[0]
    table = jnp.concatenate([late[:, :late_columns], early], axis=1)
    if sizes[1] * sizes[2] > 1:
        table = lax.psum_scatter(table, fsdp, scatter_dimension=0, tiled=True)
    table = lax.psum(table, "dp").astype(F32)
    ups, rest = late_columns, late_columns + 2 * hidden
    grads = jnp.concatenate(
        [
            table[:, rest : rest + width],
            table[:, : width + 4],
            table[:, rest + width :],
            table[:, ups:rest],
            table[:, width + 4 : width + 4 + tail],
        ],
        axis=1,
    )
    return grads, lax.psum(jnp.sum(grads * grads), fsdp)


def late_sums(refs):
    late = refs.both[0].astype(F32)
    for index in range(1, refs.both.shape[0]):
        late = late + refs.both[index].astype(F32)
    late = late.astype(BF16)
    refs.late[...] = late
    square = jnp.sum(jnp.square(refs.early[...].astype(F32))) + jnp.sum(jnp.square(late.astype(F32)))
    refs.wide[...] = jnp.full(refs.wide.shape, square, F32)


def optimizer(plan, sizes, parts, tail, refs):
    n_dp = sizes[0]
    refs.begin()
    part1, part3 = parts
    width, hidden = plan.width, FFN
    me = lax.axis_index("dp")
    split = part1
    for step in range(n_dp):
        at = pl.ds(me ^ step, 1)
        refs.by_dp[at, :, :split] = refs["o" + str(step)][...].astype(F32)[None]
        refs.by_dp[at, :, split:] = refs["l" + str(step)][...].astype(F32)[None]
    blocks = [refs.by_dp[index] for index in range(n_dp)]
    cut = lambda low, high: jnp.concatenate([block[:, low:high] for block in blocks], axis=1)
    early = cut(0, part1)
    lates = cut(part1, part1 + part3)
    table = lates[:, width : width + TABLE]
    mids = 2 * hidden + width
    refs.flat[:, :width] = early[:, 2 * hidden : mids]
    refs.flat[:, width : 2 * width] = lates[:, :width]
    moved = [early[:, mids : mids + 2 * width], early[:, : 2 * hidden], pltpu.roll(table, TABLE - 4, 1)]
    moved = jnp.concatenate(moved, axis=1)
    refs.flat[:, 2 * width :] = pltpu.roll(moved, 4, 1)
    total = refs.wide[0]
    for index in range(1, refs.wide.shape[0]):
        total = total + refs.wide[index]
    norm = jnp.sqrt(total)
    refs.norm[0, 0] = norm[0, 0]
    scale = jnp.minimum(1.0, CLIP_NORM / (norm[0:1, 0:1] + 1e-06))
    columns = refs.params.shape[1]
    for lanes in tiles(0, columns, 512):
        new = adam_rows(
            refs.params[:, lanes], refs.flat[:, lanes], refs.first[:, lanes], refs.second[:, lanes], scale
        )
        for name, value in zip(("new_params", "new_first", "new_second"), new):
            refs[name][:, lanes] = value


def local(sizes, x_big, x_small, cot_big, cot_small, counts, params, first, second):
    n_dp, n_z, n_core = sizes
    fsdp = ("z", "core")
    everywhere = ("dp",) + fsdp
    width = x_big.shape[-1]
    hidden = FFN
    plan = Plan(x_big.shape, x_small.shape)
    consts = constants(plan)
    height = params.shape[0]
    mod_at = 2 * width + 4
    tail_at = mod_at + 2 * width + 2 * hidden
    tail = params.shape[1] - tail_at
    power = all(size & (size - 1) == 0 for size in sizes)
    blocked = height % 16 == 0 and n_core == 2 and power and n_dp <= 4 and n_z <= 4

    def over(part, axis, step):
        return lax.ppermute(part, axis, [(index, index ^ step) for index in range(sizes[axis_of[axis]])])

    axis_of = dict(dp=0, z=1, core=2)
    def rows_of_images(x_big, x_small, cot_big, cot_small, counts):
        count_pair = counts.reshape(2)
        live_big = (jnp.arange(x_big.shape[0]) < count_pair[0]).astype(BF16)
        live_small = (jnp.arange(x_small.shape[0]) < count_pair[1]).astype(BF16)
        x_rows = to_rows(plan, x_big, x_small)
        wl = to_rows(plan, cot_big * live_big[:, None, None, None], cot_small * live_small[:, None, None, None])
        return x_rows, wl

    given = (x_big, x_small, cot_big, cot_small, counts)
    shard = params.astype(BF16)
    empty = lambda columns: [jnp.zeros((height, columns), BF16)]
    shard_a = jnp.concatenate([shard[:, width:mod_at], shard[:, tail_at:]] + empty(TABLE - 4 - tail), axis=1)
    rest = 3 * width + 2 * hidden
    shard_b = [shard[:, :width], shard[:, mod_at:tail_at]] + empty(up_to(rest, TABLE * n_dp) - rest)
    shard_b = jnp.concatenate(shard_b, axis=1)
    if blocked:
        me, my_z = lax.axis_index("dp"), lax.axis_index("z")
        split_b = shard_b.shape[1] // n_dp
        mine_b = lax.dynamic_slice_in_dim(shard_b, me * split_b, split_b, 1)

        def over_z(part):
            return [part] + [over(part, "z", step) for step in range(1, n_z)]

        def over_dp(part):
            return [part] + [over(part, "dp", step) for step in range(1, n_dp)]

        def with_core(parts):
            return [one for part in parts for one in (part, over(part, "core", 1))]

        all_a = over_z(shard_a)
        near = min(1, n_z - 1)
        all_a[near], mine_b = lax.optimization_barrier((all_a[near], mine_b))
        all_b = over_z(mine_b)
        all_a[-1], *given = lax.optimization_barrier((all_a[-1], *given))
        x_rows, wl = rows_of_images(*given)
        *all_a, x_rows = lax.optimization_barrier((*all_a, x_rows))
        pieces_a = with_core(all_a)
        *all_b, wl = lax.optimization_barrier((*all_b, wl))
        stack_b = jnp.stack(all_b)
        x_rows, stack_b = lax.optimization_barrier((x_rows, stack_b))
        pieces_b = over_dp(stack_b)
    else:
        x_rows, wl = rows_of_images(*given)
        pieces_a, pieces_b = ([lax.all_gather(part, fsdp, axis=0, tiled=True)] for part in (shard_a, shard_b))
    if blocked:
        share1 = Shares(sizes, width, 3 * width + 2 * hidden)
        share3 = Shares(sizes, width, width + TABLE)
    else:
        share1, share3 = Plain(width, 3 * width + 2 * hidden), Plain(width, width + TABLE)

    one = mix_forward(plan, consts, x_rows, pieces_a, sizes)
    if blocked:
        *pieces_b, one["mixed"] = lax.optimization_barrier((*pieces_b, one["mixed"]))
        pieces_b = with_core(pieces_b)
    mid = middle_pass(plan, consts, share1, x_rows, wl, one, pieces_b, sizes)
    if blocked:
        got = over(mid["give"], "core", 1)
        pick = lambda table, index: lax.dynamic_index_in_dim(table, index, 0, keepdims=False)
        part_of = lambda step: pick(mid["keep"], me ^ step) + pick(got, me ^ step)
        by_dp = [part_of(0)] + [over(part_of(step), "dp", step) for step in range(1, n_dp)]
    mix = mix_backward(plan, consts, one, mid)
    if blocked:
        *by_dp, mix["glow"] = lax.optimization_barrier((*by_dp, mix["glow"]))
        summed = sum(part.astype(F32) for part in by_dp).astype(BF16)
        by_z = [pick(summed, my_z)] + [over(pick(summed, my_z ^ step), "z", step) for step in range(1, n_z)]
    end = input_pass(plan, consts, share3, x_rows, one, mid, mix)
    out_big, out_small = from_rows(plan, mid["out"], x_big.shape, x_small.shape)
    grad_big, grad_small = from_rows(plan, end["gx"], x_big.shape, x_small.shape)
    images = (out_big, out_small, grad_big, grad_small)
    if not blocked:
        grads, square = whole_sums(plan, sizes, tail, end["keep"], mid["keep"], width + TABLE)
        grad_norm = jnp.sqrt(square)
        scale = jnp.minimum(1.0, CLIP_NORM / (grad_norm + 1e-06))
        return images + adam_rows(params, grads, first, second, scale) + (grad_norm,)
    count = n_dp * n_z * n_core
    *by_z, last = lax.optimization_barrier((*by_z, end["give"]))
    last = end["keep"] + over(last, "core", 1)
    both = lax.all_to_all(last.reshape(n_dp * n_z, height, share3.part), ("dp", "z"), 0, 0)
    early = sum(part.astype(F32) for part in by_z).astype(BF16)
    owned = [early] + [over(early, "dp", step) for step in range(1, n_dp)]
    both, *rest = lax.optimization_barrier((both, *images[:2], *owned))
    images, owned = tuple(rest[:2]) + images[2:], rest[2:]
    sums = run(
        late_sums,
        dict(both=both, early=owned[0]),
        dict(late=((height, share3.part), BF16), wide=((count, 8, TABLE), F32)),
        {},
        micros=2,
        limit=4 * 2**20,
    )
    wide = lax.all_to_all(sums["wide"], everywhere, 0, 0)
    late = [sums["late"]] + [over(sums["late"], "dp", step) for step in range(1, n_dp)]
    wide, *images = lax.optimization_barrier((wide,) + images)
    images = tuple(images)
    state = ((height, params.shape[1]), F32)
    inputs = dict({"o" + str(step): part for step, part in enumerate(owned)}, wide=wide)
    inputs.update({"l" + str(step): part for step, part in enumerate(late)})
    new = run(
        partial(optimizer, plan, sizes, (share1.part, share3.part), tail),
        dict(inputs, params=params, first=first, second=second),
        dict(new_params=state, new_first=state, new_second=state, norm=((1, 1), F32)),
        dict(
            by_dp=((n_dp, height, share1.part + share3.part), F32),
            flat=((height, up_to(params.shape[1], TABLE)), F32),
        ),
        micros=3,
        limit=16 * 2**20,
    )
    return images + (new["new_params"], new["new_first"], new["new_second"], new["norm"].reshape(()))


def solution(mesh):
    n_dp, n_fsdp = mesh.shape["dp"], mesh.shape["fsdp"]
    n_core = 2 if n_fsdp % 2 == 0 else 1
    n_z = n_fsdp // n_core
    split = jax.sharding.Mesh(mesh.devices.reshape(n_dp, n_z, n_core), ("dp", "z", "core"))
    images = P(("dp", "z", "core"), None, None, None)
    rows = P(("z", "core"), None)
    in_specs = (images,) * 4 + (P("dp", ("z", "core"), None),) + (rows,) * 3
    out_specs = (images,) * 4 + (rows,) * 3 + (P(),)
    return jax.shard_map(
        partial(local, (n_dp, n_z, n_core)), mesh=split, in_specs=in_specs, out_specs=out_specs, check_vma=False
    )
```

```python
from functools import partial

import jax
import jax.numpy as jnp
import numpy as np
from jax import lax
from jax.experimental import pallas as pl
from jax.experimental.pallas import tpu as pltpu
from jax.sharding import PartitionSpec as P

FFN = 1536
STEP = 10
CLIP_NORM = 1.0
BETA_ONE = 0.9
BETA_TWO = 0.999
LEARN_RATE = 0.05
DECAY_RATE = 0.05
ADAM_EPS = 1e-08
KERNEL_SIDES = (3, 5, 7)
F32 = jnp.float32
BF16 = jnp.bfloat16
VMEM_BYTES = 58 * 2**20

SLOT = 16


def up_to(value, step):
    return -(-value // step) * step


class Plan:
    def __init__(self, big_shape, small_shape):
        self.n_big, self.side_big = big_shape[0], big_shape[1]
        self.n_small, self.side_small = small_shape[0], small_shape[1]
        self.width = big_shape[3]
        self.pix_big = self.side_big**2
        self.pix_small = self.side_small**2
        self.rows_big = up_to(self.pix_big, SLOT)
        self.group = max(size for size in (1, 2, 3) if self.n_small % size == 0)
        self.n_groups = self.n_small // self.group
        self.rows_small = up_to(self.group * self.pix_small, SLOT)
        self.small_at = self.n_big * self.rows_big
        self.used = self.small_at + self.n_groups * self.rows_small
        self.rows = up_to(self.used, 256)
        self.n_images = self.n_big + self.n_small
        self.image_rows = up_to(self.n_images, SLOT)


def half_spectrum(size):
    reps = []
    for u in range(size):
        for v in range(size):
            other = ((-u) % size, (-v) % size)
            if (u, v) <= other:
                reps.append((u, v, 1.0 if (u, v) == other else 2.0))
    return np.array(reps)


def transform_pair(side, kernel_side, copies):
    margin = kernel_side // 2
    size = side + margin
    reps = half_spectrum(size)
    count = len(reps)
    freq = 2 * np.pi * reps[:, :2] / size
    grid = np.array([(i, j) for i in range(side) for j in range(side)], float)
    lags = np.array([(i - margin, j - margin) for i in range(kernel_side) for j in range(kernel_side)], float)
    phase = freq @ grid.T
    lag_phase = freq @ lags.T
    weight = reps[:, 2:3] / size**2
    pix = side * side
    half = up_to(copies * count, SLOT)
    rows = up_to(copies * pix, SLOT)
    forward = np.zeros((2 * half, rows))
    inverse = np.zeros((rows, 2 * half))
    taps = np.zeros((2 * half, kernel_side**2))
    back = np.zeros((kernel_side**2, 2 * half))
    for one in range(copies):
        low, col = one * count, one * pix
        forward[low : low + count, col : col + pix] = np.cos(phase)
        forward[half + low : half + low + count, col : col + pix] = -np.sin(phase)
        inverse[col : col + pix, low : low + count] = (weight * np.cos(phase)).T
        inverse[col : col + pix, half + low : half + low + count] = -(weight * np.sin(phase)).T
        taps[low : low + count] = np.cos(lag_phase)
        taps[half + low : half + low + count] = np.sin(lag_phase)
        back[:, low : low + count] = (weight * np.cos(lag_phase)).T
        back[:, half + low : half + low + count] = -(weight * np.sin(lag_phase)).T
    return forward, inverse, taps, back


TABLE = 128
GATES_AT = 0
TAPS_AT = 4
VECS_AT = 87
BIAS_AT = 96


def low_np(values):
    return jnp.asarray(values, F32).astype(BF16)


def high_and_rest(values):
    high = values.astype(np.float32).astype(jnp.bfloat16)
    rest = (values - high.astype(np.float64)).astype(np.float32).astype(jnp.bfloat16)
    return jnp.asarray(high), jnp.asarray(rest)


def constants(plan):
    consts = {}
    tap_at = TAPS_AT
    for level, kernel_side in enumerate(KERNEL_SIDES):
        for kind, side, copies in (("b", plan.side_big, 1), ("s", plan.side_small, plan.group)):
            forward, inverse, taps, back = transform_pair(side, kernel_side, copies)
            wide = np.zeros((taps.shape[0], TABLE))
            wide[:, tap_at : tap_at + kernel_side**2] = taps
            tall = np.zeros((TABLE, taps.shape[0]))
            tall[tap_at : tap_at + kernel_side**2] = back
            consts["f" + kind + str(level)] = low_np(forward)
            consts["g" + kind + str(level)] = low_np(inverse)
            high, rest = high_and_rest(wide)
            consts["k" + kind + str(level)] = jnp.concatenate([high, rest], axis=1)
            consts["t" + kind + str(level)] = low_np(tall)
        tap_at += kernel_side**2
    pick = np.zeros((plan.image_rows, plan.rows))
    for one in range(plan.n_big):
        pick[one, one * plan.rows_big : one * plan.rows_big + plan.pix_big] = 1.0
    for one in range(plan.n_small):
        at = plan.small_at + one // plan.group * plan.rows_small + one % plan.group * plan.pix_small
        pick[plan.n_big + one, at : at + plan.pix_small] = 1.0
    consts["pick"] = low_np(pick)
    consts["spread"] = low_np(pick.T)
    consts["eye"] = low_np(np.eye(TABLE))
    lanes = np.zeros((FFN, plan.width))
    lanes[np.arange(FFN), np.arange(FFN) // (FFN // plan.width)] = 1.0
    consts["lanes"] = low_np(lanes)
    return consts


def dot(left, right):
    return jnp.dot(left, right, preferred_element_type=F32)


def dot_nt(left, right):
    return lax.dot_general(left, right, (((1,), (1,)), ((), ())), preferred_element_type=F32)


def dot_tn(left, right):
    return lax.dot_general(left, right, (((0,), (0,)), ((), ())), preferred_element_type=F32)


def tiles(low, high, step):
    for at in range(low, high, step):
        yield slice(at, min(at + step, high))


def gelu_and_slope(values):
    chance = 0.5 + 0.5 * lax.erf(values * 0.7071067811865476)
    bell = jnp.exp(values * values * -0.5) * 0.3989422804014327
    return values * chance, chance + values * bell


class Refs(dict):
    def __getattr__(self, name):
        return self[name]

    def setup(self, fetched, sent):
        self.used = 0
        self.open = {}
        self.leaving = []
        self.sent = sent
        self.waiting = dict(fetched)

    def copy(self, source, target):
        result = pltpu.make_async_copy(source, target, self["sems"].at[self.used])
        result.start()
        self.used += 1
        return result

    def begin(self, *names):
        for name in names or tuple(self.waiting):
            source, lanes = self.waiting.pop(name)
            far = self[source] if lanes is None else self[source].at[:, lanes]
            self.open[name] = self.copy(far, self[name])

    def need(self, *names):
        for name in names:
            if name in self.open:
                self.open.pop(name).wait()

    def send(self, name, at=None):
        far, near = self["far_" + name], self[name]
        if at is not None:
            far, near = far.at[at], near.at[at]
        self.leaving.append(self.copy(near, far))

    def finish(self):
        self.need(*list(self.open))
        for copy in self.leaving:
            copy.wait()


COPIES = 96


def run(body, inputs, outputs, scratch, fetched=None, sent=(), far=(), micros=20, limit=VMEM_BYTES):
    fetched = {name: (name, None) if entry is None else entry for name, entry in (fetched or {}).items()}
    sources = {source for source, _ in fetched.values()}
    buffers = {}
    for name, (source, lanes) in fetched.items():
        shape = inputs[source].shape
        if lanes is not None:
            shape = (shape[0], lanes.stop - lanes.start)
        buffers["near_" + name] = (shape, inputs[source].dtype)
    for name in sent:
        buffers["near_" + name] = outputs[name]
    names = ["in_" + name for name in inputs] + ["out_" + name for name in outputs] + list(scratch) + list(buffers)

    def kernel(*args):
        given = dict(zip(names + ["sems"], args))
        refs = Refs()
        for name in inputs:
            refs[name] = given["in_" + name]
        for name in outputs:
            refs["far_" + name if name in sent else name] = given["out_" + name]
        for name in list(scratch) + ["sems"]:
            refs[name] = given[name]
        entries = {}
        for name, (source, lanes) in fetched.items():
            refs["source_" + source] = given["in_" + source]
            entries[name] = ("source_" + source, lanes)
        for name in list(fetched) + list(sent):
            refs[name] = given["near_" + name]
        refs.setup(entries, sent)
        body(refs)
        refs.finish()

    def space(name, distant):
        return pl.BlockSpec(memory_space=pl.ANY if distant else pltpu.VMEM)

    results = pl.pallas_call(
        kernel,
        in_specs=[space(name, name in sources or name in far) for name in inputs],
        out_specs=[
            pl.BlockSpec(memory_space=pltpu.SMEM) if shape == (1, 1) else space(name, name in sent or name in far)
            for name, (shape, _) in outputs.items()
        ],
        out_shape=[jax.ShapeDtypeStruct(shape, dtype) for shape, dtype in outputs.values()],
        scratch_shapes=[pltpu.VMEM(*entry) for entry in list(scratch.values()) + list(buffers.values())]
        + [pltpu.SemaphoreType.DMA((COPIES,))],
        compiler_params=pltpu.CompilerParams(vmem_limit_bytes=limit),
        cost_estimate=pl.CostEstimate(flops=micros * 10**9, bytes_accessed=micros * 10**6, transcendentals=0),
    )(*inputs.values())
    return dict(zip(outputs, results))


def units(plan):
    result = []
    for one in range(plan.n_big):
        result.append(("b", slice(one * plan.rows_big, (one + 1) * plan.rows_big), len(result)))
    for one in range(plan.n_groups):
        at = plan.small_at + one * plan.rows_small
        result.append(("s", slice(at, at + plan.rows_small), len(result)))
    return result


def pairs(plan):
    result = []
    for kind in "bs":
        same = [unit for unit in units(plan) if unit[0] == kind]
        result += [same[low : low + 2] for low in range(0, len(same), 2)]
    return result


def side_by_side(values):
    return values[0] if len(values) == 1 else jnp.concatenate(values, axis=1)


def wave_rows(plan, consts):
    result, total = {}, []
    for level in range(3):
        at = 0
        for kind, _, index in units(plan):
            count = consts["f" + kind + str(level)].shape[0]
            result[level, index] = slice(at, at + count)
            at += count
        total.append(at)
    return result, total


def spectrum_of_taps(refs, name, table):
    refs["h" + name][...] = dot_nt(refs["k" + name][:, :TABLE], table) + dot_nt(refs["k" + name][:, TABLE:], table)


def image_scale(plan):
    row = lax.broadcasted_iota(jnp.int32, (plan.image_rows, 1), 0)
    return jnp.where(row < plan.n_big, 1.0 / plan.pix_big, 1.0 / plan.pix_small).astype(F32)


def unit_rows(values):
    center = values - jnp.mean(values, axis=-1, keepdims=True)
    scale = lax.rsqrt(jnp.mean(center * center, axis=-1, keepdims=True) + 1e-05)
    return center * scale, scale


def fold(values):
    total = values[0:8]
    for low in range(8, values.shape[0], 8):
        total = total + values[low : low + 8]
    return total


def column_sum(values):
    return jnp.sum(values, axis=0, keepdims=True)


def forward_mix(plan, places, sizes, n_pieces, refs):
    rows, width, hidden = plan.rows, plan.width, FFN
    arriving = gather(refs, sizes, n_pieces, "wa")
    refs.begin()
    for copy in arriving:
        copy.wait()
    refs.send("wa")
    refs.need("eye")
    table = refs.wa[:, width:]
    refs.vec[...] = dot_nt(refs.eye[...], table)
    refs.need("x")
    gain = refs.vec[VECS_AT : VECS_AT + 1, :]
    shift = refs.vec[VECS_AT + 1 : VECS_AT + 2, :]
    for block in tiles(0, rows, 256):
        for at in tiles(block.start, block.stop, 32):
            unit, _ = unit_rows(refs.x[at, :].astype(F32))
            refs.unit[at, :] = unit.astype(BF16)
            refs.normed[at, :] = (unit * gain + shift).astype(BF16)
        refs.send("normed", block)
        refs.send("unit", block)
        part = dot(refs.normed[block, :], refs.wa[...])
        refs.context[block, :] = (part[:, :width] + refs.vec[VECS_AT + 3 : VECS_AT + 4, :]).astype(BF16)
        refs.gate[block, :] = part[:, width:]
    refs.send("gate")
    if rows > plan.used:
        refs.c[:, plan.used :, :] = jnp.zeros((3, rows - plan.used, width), BF16)
        refs.gp[:, plan.used :, :] = jnp.zeros((3, rows - plan.used, width), BF16)
    for level in range(3):
        for kind in "bs":
            refs.need("f" + kind + str(level), "k" + kind + str(level), "g" + kind + str(level))
            spectrum_of_taps(refs, kind + str(level), table)
        hat = refs["hat" + str(level)]
        field_in = refs.context if level == 0 else refs.c.at[level - 1]
        for pair in pairs(plan):
            name = pair[0][0] + str(level)
            count = refs["f" + name].shape[0]
            half = count // 2
            taps = refs["h" + name]
            both = dot(refs["f" + name][...], side_by_side([field_in[at, :] for _, at, _ in pair]))
            for place, (_, at, index) in enumerate(pair):
                wave, low_wave = refs.wave.at[index], refs.wave_low.at[index]
                wave[:count, :] = both[:, place * width : (place + 1) * width]
                saved = places[level, index].start
                for re in tiles(0, half, 16):
                    im = slice(half + re.start, half + re.stop)
                    wave_re, wave_im = wave[re, :], wave[im, :]
                    tap_re, tap_im = taps[re, :], taps[im, :]
                    hat[saved + re.start : saved + re.stop, :] = wave_re.astype(BF16)
                    hat[saved + im.start : saved + im.stop, :] = wave_im.astype(BF16)
                    low_wave[re, :] = (wave_re * tap_re - wave_im * tap_im).astype(BF16)
                    low_wave[im, :] = (wave_re * tap_im + wave_im * tap_re).astype(BF16)
            both = dot(refs["g" + name][...], side_by_side([refs.wave_low[index, :count, :] for _, _, index in pair]))
            for place, (_, at, index) in enumerate(pair):
                refs.field[at, :] = both[:, place * width : (place + 1) * width]
                for into in tiles(at.start, at.stop, 16):
                    value, slope = gelu_and_slope(refs.field[into, :])
                    refs.c[level, into, :] = value.astype(BF16)
                    refs.gp[level, into, :] = slope.astype(BF16)
        refs.send("c", slice(level, level + 1))
        refs.send("gp", slice(level, level + 1))
        refs.send("hat" + str(level))
    refs.need("pick", "spread")
    mean = dot(refs.pick[...], refs.c[2]) * image_scale(plan)
    summary, slope = gelu_and_slope(mean)
    refs.sum[0] = summary
    refs.sum[1] = slope
    summary_low = summary.astype(BF16)
    for block in tiles(0, rows, 256):
        refs.field[block, :] = dot(refs.spread[block, :], summary_low)
        for at in tiles(block.start, block.stop, 32):
            gate = refs.gate[at, :]
            total = refs.field[at, :] * gate[:, 3:4]
            for level in range(3):
                total += refs.c[level, at, :].astype(F32) * gate[:, level : level + 1]
            refs.mixed[at, :] = total.astype(BF16)
        refs.send("mixed", block)
    refs.need("lanes")
    ratio = hidden // width
    spread = dot_nt(refs.vec[BIAS_AT : BIAS_AT + 16, :].astype(BF16), refs.lanes[...])
    row = lax.broadcasted_iota(jnp.int32, (16, hidden), 0)
    lane = lax.broadcasted_iota(jnp.int32, (16, hidden), 1)
    picked = jnp.where(lax.rem(lane, ratio) == row, spread, 0.0)
    refs.upb[...] = jnp.broadcast_to(jnp.sum(picked, axis=0, keepdims=True), (8, hidden))


def mix_scratch(plan, consts):
    scratch = {}
    for level in range(3):
        for kind in "bs":
            scratch["h" + kind + str(level)] = ((consts["f" + kind + str(level)].shape[0], plan.width), F32)
    return scratch


def most_waves(consts):
    return max(consts["f" + kind + str(level)].shape[0] for level in range(3) for kind in "bs")


def mix_forward(plan, consts, x_rows, pieces, sizes):
    rows, width = plan.rows, plan.width
    waves, n_units = most_waves(consts), len(units(plan))
    places, saved = wave_rows(plan, consts)
    keys = [k + kind + str(level) for level in range(3) for kind in "bs" for k in "fkg"]
    names = ["eye"] + keys + ["pick", "spread", "lanes"]
    inputs = dict(x=x_rows, **{k: consts[k] for k in names})
    apart = {"w" + str(step): piece for step, piece in enumerate(pieces)}
    inputs.update(apart)
    outputs = dict(
        wa=((width, width + TABLE), BF16),
        normed=((rows, width), BF16),
        unit=((rows, width), BF16),
        c=((3, rows, width), BF16),
        gp=((3, rows, width), BF16),
        **{"hat" + str(level): ((saved[level], width), BF16) for level in range(3)},
        mixed=((rows, width), BF16),
        gate=((rows, TABLE), F32),
        vec=((TABLE, width), F32),
        upb=((8, FFN), F32),
        sum=((2, plan.image_rows, width), F32),
    )
    scratch = dict(
        wave=((n_units, waves, width), F32),
        wave_low=((n_units, waves, width), BF16),
        field=((rows, width), F32),
        context=((rows, width), BF16),
        **mix_scratch(plan, consts),
    )
    sent = ("normed", "unit", "c", "gp", "hat0", "hat1", "hat2", "mixed", "gate")
    sent += ("wa",)
    body = partial(forward_mix, plan, places, sizes, len(pieces))
    return run(body, inputs, outputs, scratch, {k: None for k in ["x"] + names}, sent, list(apart), 2)


def gather(refs, sizes, n_pieces, target):
    n_dp, n_z, n_core = sizes
    if n_pieces == 1:
        return [refs.copy(refs["w0"], refs[target])]
    copies = []
    me, my_z, my_core = (lax.axis_index(name) for name in ("dp", "z", "core"))

    def place(piece, z, step, lanes):
        height = piece.shape[0]
        owner = (my_z ^ z) * n_core + (my_core ^ (step % n_core))
        copies.append(refs.copy(piece, refs[target].at[pl.ds(pl.multiple_of(owner * height, 16), height), lanes]))

    for step in range(n_pieces):
        piece = refs["w" + str(step)]
        if len(piece.shape) == 2:
            place(piece, step // n_core, step, slice(None))
            continue
        part = piece.shape[2]
        lanes = pl.ds(pl.multiple_of((me ^ (step // n_core)) * part, TABLE), part)
        for other in range(n_z):
            place(piece.at[other], other, step, lanes)
    return copies


class Shares:
    def __init__(self, sizes, rows, columns):
        self.n_dp, self.n_z, self.n_core = sizes
        self.height = rows // (self.n_z * self.n_core)
        self.part = up_to(columns, TABLE * self.n_dp) // self.n_dp
        self.empty = self.part * self.n_dp - columns
        self.shape = (self.n_core, self.n_dp, self.n_z, self.height, self.part)
        self.columns = columns

    def place(self, core, share, z):
        return (core, share, z)

    def put(self, ref, low, values):
        done = 0
        while done < values.shape[1]:
            share, at = divmod(low + done, self.part)
            take = min(self.part - at, values.shape[1] - done)
            for owner in range(self.n_z * self.n_core):
                z, core = divmod(owner, self.n_core)
                ref[self.place(core, share, z) + (slice(None), slice(at, at + take))] = values[
                    owner * self.height : (owner + 1) * self.height, done : done + take
                ]
            done += take

    def close(self, refs, stage, names):
        if self.empty:
            self.put(stage, self.columns, jnp.zeros((self.height * self.n_z * self.n_core, self.empty), BF16))
        core = lax.axis_index("core")
        for source, name in ((1 - core, names[1]), (core, names[0])):
            refs.leaving.append(refs.copy(stage.at[source], refs[name]))


class Blocks(Shares):
    def __init__(self, sizes, rows, columns):
        super().__init__(sizes, rows, columns)
        self.shape = (self.n_dp, self.n_z, self.n_core, self.height, self.part)

    def place(self, core, share, z):
        return (share, z, core)

    def close(self, refs, stage, names):
        refs.leaving.append(refs.copy(stage, refs[names[0]]))


class Plain:
    def __init__(self, rows, columns):
        self.shape = (rows, columns)

    def put(self, ref, low, values):
        ref[:, low : low + values.shape[1]] = values

    def close(self, refs, stage, names):
        refs.leaving.append(refs.copy(stage, refs[names[0]]))


def input_grads(product, sums, weight, table):
    gain = table[:, VECS_AT : VECS_AT + 1].astype(F32)
    shift = table[:, VECS_AT + 1 : VECS_AT + 2].astype(F32)
    weight = weight.astype(F32)
    lane = lax.broadcasted_iota(jnp.int32, (1, TABLE), 1)
    parts = jnp.where(lane == VECS_AT, jnp.sum(product * weight, axis=-1, keepdims=True), 0.0)
    parts = jnp.where(lane == VECS_AT + 1, jnp.sum(sums * weight, axis=-1, keepdims=True), parts)
    return gain * product + shift * sums, parts


def middle(plan, shares, sizes, n_pieces, refs):
    rows, width, hidden = plan.rows, plan.width, FFN
    vec = lambda index: refs.vec[VECS_AT + index : VECS_AT + index + 1, :]
    zero = jnp.zeros((8, width), F32)
    sums = {index: zero for index in (2, 4, 5, 6, 7, 8)}
    blocks = list(tiles(0, rows, 256))
    up_at = 3 * width
    down_at = up_at + hidden
    wq, wm, wo = (refs.wb.at[:, at * width : (at + 1) * width] for at in range(3))
    wu, wd = refs.wb.at[:, up_at:down_at], refs.wb.at[:, down_at : down_at + hidden]
    refs.begin("mixed", "normed")
    arriving = gather(refs, sizes, n_pieces, "wb")
    refs.begin()
    refs.need("mixed", "normed")
    for copy in arriving:
        copy.wait()
    refs.leaving.append(refs.copy(wq, refs.wq))

    def before(block):
        modulator = dot(refs.mixed[block, :], wm[...]) + vec(4)
        queries = dot(refs.normed[block, :], wq[...]) + vec(2)
        refs.mod[block, :] = modulator.astype(BF16)
        refs.q[block, :] = queries.astype(BF16)
        refs.prod[block, :] = (queries * modulator).astype(BF16)
        yield
        refs.need("x")
        refs.resid[block, :] = dot(refs.prod[block, :], wo[...])
        yield
        for part in tiles(block.start, block.stop, 64):
            for at in tiles(part.start, part.stop, 32):
                resid = refs.resid[at, :] + refs.x[at, :].astype(F32) + vec(5)
                refs.resid[at, :] = resid
                unit, scale = unit_rows(resid)
                refs.unit[at, :] = unit
                refs.scale[at, :] = jnp.broadcast_to(scale, (scale.shape[0], TABLE))
                refs.n2[at, :] = (unit * vec(6) + vec(7)).astype(BF16)
            yield

    def mlp(block):
        refs.need("wl")
        for index, lanes in enumerate(tiles(0, hidden, 256)):
            pre, grad_act = refs.pa.at[index % 3], refs.ga.at[index % 3]
            pre[...] = dot(refs.n2[block, :], wu[:, lanes])
            grad_act[...] = dot(refs.wl[block, :], wd[:, lanes])
            bias = refs.upb[0:1, lanes]
            total = jnp.zeros((8, 256), F32) if block.start == 0 else refs.gub[:, lanes]
            for low in tiles(0, 256, 16):
                at = slice(block.start + low.start, block.start + low.stop)
                value, slope = gelu_and_slope(pre[low, :] + bias)
                grad = grad_act[low, :] * slope
                refs.act[at, lanes] = value.astype(BF16)
                refs.pre[at, lanes] = grad.astype(BF16)
                total = total + fold(grad)
            refs.gub[:, lanes] = total
            yield

    def after(block):
        refs.gn[block, :] = dot_nt(refs.pre[block, :], wu[...])
        yield
        refs.out[block, :] = (refs.resid[block, :] + dot_nt(refs.act[block, :], wd[...]) + vec(8)).astype(BF16)
        refs.send("out", block)
        yield
        for part in tiles(block.start, block.stop, 128):
            for at in tiles(part.start, part.stop, 32):
                grad = refs.gn[at, :]
                unit = refs.unit[at, :]
                weighted = refs.wl[at, :].astype(F32)
                gained = grad * vec(6)
                mean_one = jnp.mean(gained, axis=-1, keepdims=True)
                mean_two = jnp.mean(gained * unit, axis=-1, keepdims=True)
                result = weighted + refs.scale[at, 0:1] * (gained - mean_one - unit * mean_two)
                refs.gres[at, :] = result
                refs.glow[at, :] = result.astype(BF16)
                for index, new in ((6, grad * unit), (7, grad), (5, result), (8, weighted)):
                    sums[index] = sums[index] + fold(new)
            yield
        refs.send("gres", block)
        refs.gn[block, :] = dot_nt(refs.glow[block, :], wo[...])
        yield
        for at in tiles(block.start, block.stop, 32):
            grad = refs.gn[at, :]
            grad_query = grad * refs.mod[at, :].astype(F32)
            grad_mod = grad * refs.q[at, :].astype(F32)
            refs.gq[at, :] = grad_query.astype(BF16)
            refs.gmod[at, :] = grad_mod.astype(BF16)
            for index, new in ((2, grad_query), (4, grad_mod)):
                sums[index] = sums[index] + fold(new)
        refs.send("gq", block)
        refs.gmix[block, :] = dot_nt(refs.gmod[block, :], wm[...]).astype(BF16)
        refs.send("gmix", block)
        yield

    def together(*steps):
        steps = list(steps)
        while steps:
            steps = [step for step in steps if next(step, refs) is not refs]

    together(before(blocks[0]))
    for index in range(len(blocks) + 1):
        steps = []
        if index < len(blocks):
            steps.append(mlp(blocks[index]))
        if index + 1 < len(blocks):
            steps.append(before(blocks[index + 1]))
        if index:
            steps.append(after(blocks[index - 1]))
        together(*steps)
    for lanes in tiles(0, hidden, 256):
        shares.put(refs.stage, lanes.start, dot_tn(refs.n2[...], refs.pre[:, lanes]).astype(BF16))
        shares.put(refs.stage, hidden + lanes.start, dot_tn(refs.wl[...], refs.act[:, lanes]).astype(BF16))
    refs.need("unit_in", "table")
    product = dot_tn(refs.unit_in[...], refs.gq[...])
    product, refs.parts[...] = input_grads(product, column_sum(sums[2]), wq[...], refs.table[...])
    shares.put(refs.stage, 2 * hidden, product.astype(BF16))
    shares.put(refs.stage, 2 * hidden + width, dot_tn(refs.mixed[...], refs.gmod[...]).astype(BF16))
    shares.put(refs.stage, 2 * hidden + 2 * width, dot_tn(refs.prod[...], refs.glow[...]).astype(BF16))
    shares.close(refs, refs.stage, ("keep", "give"))
    refs.gv[...] = jnp.zeros(refs.gv.shape, F32)
    for index, total in sums.items():
        refs.gv[index : index + 1, :] = column_sum(total)
    ratio = hidden // width
    row = lax.broadcasted_iota(jnp.int32, (16, hidden), 0)
    lane = lax.broadcasted_iota(jnp.int32, (16, hidden), 1)
    picked = jnp.where(lax.rem(lane, ratio) == row, column_sum(refs.gub[...]), 0.0).astype(BF16)
    refs.need("lanes")
    refs.gv[16:32, :] = dot(picked, refs.lanes[...])


def kept(shares):
    if isinstance(shares, (Plain, Blocks)):
        return dict(keep=(shares.shape, BF16))
    return dict(keep=(shares.shape[1:], BF16), give=(shares.shape[1:], BF16))


def middle_pass(plan, consts, shares, x_rows, wl, first, pieces, sizes):
    rows, width, hidden = plan.rows, plan.width, FFN
    near = dict(mixed=first["mixed"], normed=first["normed"], x=x_rows, wl=wl, unit_in=first["unit"], lanes=consts["lanes"])
    apart = {"w" + str(step): piece for step, piece in enumerate(pieces)}
    inputs = dict(near, wa=first["wa"], vec=first["vec"], upb=first["upb"], **apart)
    fetched = dict({k: None for k in near}, table=("wa", slice(width, width + TABLE)))
    token, field, wide = ((rows, width), BF16), ((rows, width), F32), ((rows, hidden), BF16)
    outputs = dict(kept(shares), out=token, gq=token, gmix=token, gres=field)
    outputs.update(wq=((width, width), BF16), gv=((32, width), F32), parts=((width, TABLE), F32))
    scratch = dict(mod=token, q=token, prod=token, glow=token, gmod=token, n2=token)
    scratch.update(resid=field, unit=field, gn=field, act=wide, pre=wide)
    scratch.update(
        scale=((rows, TABLE), F32),
        pa=((3, 256, 256), F32),
        ga=((3, 256, 256), F32),
        gub=((8, hidden), F32),
        stage=(shares.shape, BF16),
        wb=((width, up_to(3 * width + 2 * hidden, TABLE * sizes[0])), BF16),
    )
    body = partial(middle, plan, shares, sizes, len(pieces))
    far = ["keep", "give", "wq"] + list(apart)
    return run(body, inputs, outputs, scratch, fetched, ("out", "gq", "gmix", "gres"), far, 26)


def backward_mix(plan, places, shares, refs):
    rows, width = plan.rows, plan.width
    refs.begin()
    refs.need("gmix", "gate")
    for at in tiles(0, rows, 32):
        refs.tmp[at, :] = (refs.gmix[at, :].astype(F32) * refs.gate[at, 3:4]).astype(BF16)
    refs.need("pick", "spread", "wa")
    table = refs.wa[:, width:]
    grad_summary = dot(refs.pick[...], refs.tmp[...]) * refs.sum[1] * image_scale(plan)
    grad_summary_low = grad_summary.astype(BF16)
    for block in tiles(0, rows, 256):
        refs.gc[block, :] = dot(refs.spread[block, :], grad_summary_low)
    summary_low = refs.sum[0].astype(BF16)
    lane = lax.broadcasted_iota(jnp.int32, (1, TABLE), 1)

    def gates(low, high):
        refs.need("c")
        for at in tiles(low, high, 32):
            grad = refs.gmix[at, :].astype(F32)
            spread = dot(refs.spread[at, :], summary_low)
            result = jnp.where(lane == 3, jnp.sum(grad * spread, axis=-1, keepdims=True), 0.0)
            for level in range(3):
                part = jnp.sum(grad * refs.c[level, at, :].astype(F32), axis=-1, keepdims=True)
                result = jnp.where(lane == level, part, result)
            refs.ggate[at, :] = result.astype(BF16)

    taps_total = jnp.zeros((TABLE, width), F32)
    refs.need("gp")
    for level in (2, 1, 0):
        for kind in "bs":
            refs.need("f" + kind + str(level), "k" + kind + str(level), "g" + kind + str(level))
            spectrum_of_taps(refs, kind + str(level), table)
        refs.need("hat" + str(level))
        hat = refs["hat" + str(level)]
        seen = set()
        for pair in pairs(plan):
            kind = pair[0][0]
            name = kind + str(level)
            count = refs["f" + name].shape[0]
            half = count // 2
            taps, cross = refs["h" + name], refs["x" + kind]
            for _, at, _ in pair:
                for into in tiles(at.start, at.stop, 16):
                    direct = refs.gmix[into, :].astype(F32) * refs.gate[into, level : level + 1]
                    grad = refs.gc[into, :] + direct
                    refs.tmp[into, :] = (grad * refs.gp[level, into, :].astype(F32)).astype(BF16)
            both = dot(refs["f" + name][...], side_by_side([refs.tmp[at, :] for _, at, _ in pair]))
            for place, (_, _, index) in enumerate(pair):
                refs.wave[index, :count, :] = both[:, place * width : (place + 1) * width]
            for re in tiles(0, half, 16):
                im = slice(half + re.start, half + re.stop)
                tap_re, tap_im = taps[re, :], taps[im, :]
                cross_re = cross_im = None
                for _, _, index in pair:
                    saved = places[level, index].start
                    wave_re = hat[saved + re.start : saved + re.stop, :].astype(F32)
                    wave_im = hat[saved + im.start : saved + im.stop, :].astype(F32)
                    grad_re, grad_im = refs.wave[index, re, :], refs.wave[index, im, :]
                    refs.wave_low[index, re, :] = (grad_re * tap_re + grad_im * tap_im).astype(BF16)
                    refs.wave_low[index, im, :] = (grad_im * tap_re - grad_re * tap_im).astype(BF16)
                    new_re = grad_re * wave_re + grad_im * wave_im
                    new_im = grad_re * wave_im - grad_im * wave_re
                    cross_re = new_re if cross_re is None else cross_re + new_re
                    cross_im = new_im if cross_im is None else cross_im + new_im
                if kind in seen:
                    cross_re = cross_re + cross[re, :]
                    cross_im = cross_im + cross[im, :]
                cross[re, :] = cross_re
                cross[im, :] = cross_im
            seen.add(kind)
            both = dot(refs["g" + name][...], side_by_side([refs.wave_low[index, :count, :] for _, _, index in pair]))
            for place, (_, at, _) in enumerate(pair):
                refs.gc[at, :] = both[:, place * width : (place + 1) * width]
        for kind in "bs":
            name = kind + str(level)
            count = refs["f" + name].shape[0]
            refs.need("t" + name)
            taps_total = taps_total + dot(refs["t" + name][...], refs["x" + kind][:count, :].astype(BF16))
        if level:
            half = rows // 64 * 32
            gates(*((0, half) if level == 2 else (half, rows)))
    refs.gtab[...] = taps_total
    if rows > plan.used:
        refs.gc[plan.used :, :] = jnp.zeros((rows - plan.used, width), F32)
    context_total = jnp.zeros((8, width), F32)
    for block in tiles(0, rows, 256):
        for at in tiles(block.start, block.stop, 32):
            grad = refs.gc[at, :]
            refs.glow[at, :] = grad.astype(BF16)
            context_total = context_total + fold(grad)
        refs.send("glow", block)
    refs.gtab[VECS_AT + 2 : VECS_AT + 3, :] = refs.gv[2:3, :]
    refs.gtab[VECS_AT + 3 : VECS_AT + 4, :] = column_sum(context_total)
    refs.gtab[VECS_AT + 4 : VECS_AT + 9, :] = refs.gv[4:9, :]
    refs.gtab[BIAS_AT : BIAS_AT + 4, :] = refs.gv[16:20, :]
    refs.need("unit", "eye")
    product = dot_tn(refs.unit[...], refs.glow[...])
    product, parts = input_grads(product, column_sum(context_total), refs.wa[:, :width], table)
    shares.put(refs.stage, 0, product.astype(BF16))
    gate_total = jnp.zeros((8, TABLE), F32)
    for at in tiles(0, rows, 64):
        gate_total = gate_total + fold(refs.ggate[at, :].astype(F32))
    small, more = input_grads(dot_tn(refs.unit[...], refs.ggate[...]), column_sum(gate_total), table, table)
    small = small + parts + more + refs.parts[...] + dot_tn(refs.gtab[...].astype(BF16), refs.eye[...])
    shares.put(refs.stage, width, small.astype(BF16))
    shares.close(refs, refs.stage, ("keep",))


def input_back(plan, refs):
    rows, width = plan.rows, plan.width
    refs.begin()
    refs.need("glow", "wa", "ggate", "wq", "gq", "x", "gres")
    gain = refs.vec[VECS_AT : VECS_AT + 1, :]
    for block in tiles(0, rows, 256):
        refs.gc[block, :] = (
            dot_nt(refs.gq[block, :], refs.wq[...])
            + dot_nt(refs.glow[block, :], refs.wa[:, :width])
            + dot_nt(refs.ggate[block, :], refs.wa[:, width:])
        )
        for at in tiles(block.start, block.stop, 32):
            unit, scale_row = unit_rows(refs.x[at, :].astype(F32))
            gained = refs.gc[at, :] * gain
            mean_one = jnp.mean(gained, axis=-1, keepdims=True)
            mean_two = jnp.mean(gained * unit, axis=-1, keepdims=True)
            result = refs.gres[at, :] + scale_row * (gained - mean_one - unit * mean_two)
            refs.gx[at, :] = result.astype(BF16)
        refs.send("gx", block)


def mix_backward(plan, consts, shares, first, mid):
    rows, width = plan.rows, plan.width
    waves, n_units = most_waves(consts), len(units(plan))
    places, _ = wave_rows(plan, consts)
    keys = [k + kind + str(level) for level in (2, 1, 0) for k in "kfgt" for kind in "bs"]
    near = dict(gmix=mid["gmix"], gate=first["gate"], pick=consts["pick"], spread=consts["spread"], wa=first["wa"])
    near["gp"] = first["gp"]
    for level in (2, 1, 0):
        near.update({name: consts[name] for name in keys if name.endswith(str(level))})
        near["hat" + str(level)] = first["hat" + str(level)]
        near["c"] = first["c"]
    near.update(unit=first["unit"], eye=consts["eye"])
    inputs = dict(near, sum=first["sum"], gv=mid["gv"], parts=mid["parts"])
    outputs = dict(kept(shares), glow=((rows, width), BF16), ggate=((rows, TABLE), BF16))
    scratch = dict(
        wave=((n_units, waves, width), F32),
        wave_low=((n_units, waves, width), BF16),
        xb=((waves, width), F32),
        xs=((waves, width), F32),
        gc=((rows, width), F32),
        tmp=((rows, width), BF16),
        gtab=((TABLE, width), F32),
        stage=(shares.shape, BF16),
        **mix_scratch(plan, consts),
    )
    body = partial(backward_mix, plan, places, shares)
    return run(body, inputs, outputs, scratch, {k: None for k in near}, ("glow",), ("keep",), 18)


def input_pass(plan, x_rows, first, mid, mix):
    rows, width = plan.rows, plan.width
    near = dict(glow=mix["glow"], wa=first["wa"], ggate=mix["ggate"], wq=mid["wq"], gq=mid["gq"], x=x_rows)
    near["gres"] = mid["gres"]
    inputs = dict(near, vec=first["vec"])
    outputs = dict(gx=((rows, width), BF16))
    scratch = dict(gc=((rows, width), F32))
    return run(partial(input_back, plan), inputs, outputs, scratch, {k: None for k in near}, ("gx",), micros=7)


def adam_rows(params, grads, first, second, scale):
    clipped = grads * scale
    first_new = BETA_ONE * first + (1.0 - BETA_ONE) * clipped
    second_new = BETA_TWO * second + (1.0 - BETA_TWO) * clipped * clipped
    first_hat = first_new * (1.0 / (1.0 - BETA_ONE**STEP))
    second_hat = second_new * (1.0 / (1.0 - BETA_TWO**STEP))
    params_new = params - LEARN_RATE * (first_hat / (jnp.sqrt(second_hat) + ADAM_EPS) + DECAY_RATE * params)
    return (params_new, first_new, second_new)


def to_rows(plan, big, small):
    tables = []
    for images, count, pix, rows in (
        (big, plan.n_big, plan.pix_big, plan.rows_big),
        (small, plan.n_groups, plan.group * plan.pix_small, plan.rows_small),
    ):
        table = jnp.pad(images.reshape(count, pix, plan.width), ((0, 0), (0, rows - pix), (0, 0)))
        tables.append(table.reshape(count * rows, plan.width))
    if plan.rows > plan.used:
        tables.append(jnp.zeros((plan.rows - plan.used, plan.width), big.dtype))
    return jnp.concatenate(tables, axis=0)


def from_rows(plan, table, big_shape, small_shape):
    big = table[: plan.small_at].reshape(plan.n_big, plan.rows_big, plan.width)[:, : plan.pix_big]
    small = table[plan.small_at : plan.used].reshape(plan.n_groups, plan.rows_small, plan.width)
    return big.reshape(big_shape), small[:, : plan.group * plan.pix_small].reshape(small_shape)


def whole_sums(plan, sizes, tail, late, early, late_columns):
    fsdp = ("z", "core")
    width, hidden = plan.width, FFN
    rows = late.shape[0]
    table = jnp.concatenate([late[:, :late_columns], early], axis=1)
    if sizes[1] * sizes[2] > 1:
        table = lax.psum_scatter(table, fsdp, scatter_dimension=0, tiled=True)
    table = lax.psum(table, "dp").astype(F32)
    ups, rest = late_columns, late_columns + 2 * hidden
    grads = jnp.concatenate(
        [
            table[:, rest : rest + width],
            table[:, : width + 4],
            table[:, rest + width :],
            table[:, ups:rest],
            table[:, width + 4 : width + 4 + tail],
        ],
        axis=1,
    )
    return grads, lax.psum(jnp.sum(grads * grads), fsdp)


def late_sums(refs):
    late = refs.both[0].astype(F32)
    for index in range(1, refs.both.shape[0]):
        late = late + refs.both[index].astype(F32)
    late = late.astype(BF16)
    refs.late[...] = late
    square = jnp.sum(jnp.square(refs.early[...].astype(F32))) + jnp.sum(jnp.square(late.astype(F32)))
    refs.wide[...] = jnp.full(refs.wide.shape, square, F32)


def optimizer(plan, sizes, parts, tail, refs):
    n_dp = sizes[0]
    refs.begin()
    part1, part3 = parts
    width, hidden = plan.width, FFN
    me = lax.axis_index("dp")
    split = part1
    for step in range(n_dp):
        at = pl.ds(me ^ step, 1)
        refs.by_dp[at, :, :split] = refs["o" + str(step)][...].astype(F32)[None]
        refs.by_dp[at, :, split:] = refs["l" + str(step)][...].astype(F32)[None]
    blocks = [refs.by_dp[index] for index in range(n_dp)]
    cut = lambda low, high: jnp.concatenate([block[:, low:high] for block in blocks], axis=1)
    early = cut(0, part1)
    lates = cut(part1, part1 + part3)
    table = lates[:, width : width + TABLE]
    mids = 2 * hidden + width
    refs.flat[:, :width] = early[:, 2 * hidden : mids]
    refs.flat[:, width : 2 * width] = lates[:, :width]
    moved = [early[:, mids : mids + 2 * width], early[:, : 2 * hidden], pltpu.roll(table, TABLE - 4, 1)]
    moved = jnp.concatenate(moved, axis=1)
    refs.flat[:, 2 * width :] = pltpu.roll(moved, 4, 1)
    total = refs.wide[0]
    for index in range(1, refs.wide.shape[0]):
        total = total + refs.wide[index]
    norm = jnp.sqrt(total)
    refs.norm[0, 0] = norm[0, 0]
    scale = jnp.minimum(1.0, CLIP_NORM / (norm[0:1, 0:1] + 1e-06))
    columns = refs.params.shape[1]
    for lanes in tiles(0, columns, 512):
        new = adam_rows(
            refs.params[:, lanes], refs.flat[:, lanes], refs.first[:, lanes], refs.second[:, lanes], scale
        )
        for name, value in zip(("new_params", "new_first", "new_second"), new):
            refs[name][:, lanes] = value


def local(sizes, x_big, x_small, cot_big, cot_small, counts, params, first, second):
    n_dp, n_z, n_core = sizes
    fsdp = ("z", "core")
    everywhere = ("dp",) + fsdp
    width = x_big.shape[-1]
    hidden = FFN
    plan = Plan(x_big.shape, x_small.shape)
    consts = constants(plan)
    height = params.shape[0]
    mod_at = 2 * width + 4
    tail_at = mod_at + 2 * width + 2 * hidden
    tail = params.shape[1] - tail_at
    power = all(size & (size - 1) == 0 for size in sizes)
    blocked = height % 16 == 0 and n_core == 2 and power and n_dp <= 4 and n_z <= 4

    def over(part, axis, step):
        return lax.ppermute(part, axis, [(index, index ^ step) for index in range(sizes[axis_of[axis]])])

    axis_of = dict(dp=0, z=1, core=2)
    def table_of_x(x_big, x_small):
        return to_rows(plan, x_big, x_small)

    def table_of_cot(cot_big, cot_small, counts):
        count_pair = counts.reshape(2)
        live_big = (jnp.arange(cot_big.shape[0]) < count_pair[0]).astype(BF16)
        live_small = (jnp.arange(cot_small.shape[0]) < count_pair[1]).astype(BF16)
        return to_rows(plan, cot_big * live_big[:, None, None, None], cot_small * live_small[:, None, None, None])

    shard = params.astype(BF16)
    empty = lambda columns: [jnp.zeros((height, columns), BF16)]
    shard_a = jnp.concatenate([shard[:, width:mod_at], shard[:, tail_at:]] + empty(TABLE - 4 - tail), axis=1)
    rest = 3 * width + 2 * hidden
    shard_b = [shard[:, :width], shard[:, mod_at:tail_at]] + empty(up_to(rest, TABLE * n_dp) - rest)
    shard_b = jnp.concatenate(shard_b, axis=1)
    if blocked:
        me, my_z = lax.axis_index("dp"), lax.axis_index("z")
        split_b = shard_b.shape[1] // n_dp
        mine_b = lax.dynamic_slice_in_dim(shard_b, me * split_b, split_b, 1)

        def over_z(part):
            return [part] + [over(part, "z", step) for step in range(1, n_z)]

        def over_dp(part):
            return [part] + [over(part, "dp", step) for step in range(1, n_dp)]

        def with_core(parts):
            return [one for part in parts for one in (part, over(part, "core", 1))]

        all_b, all_a = over_z(mine_b), over_z(shard_a)
        near = min(1, n_z - 1)
        all_b[near], x_big, x_small, cot_big, cot_small = lax.optimization_barrier(
            (all_b[near], x_big, x_small, cot_big, cot_small)
        )
        stack_b = jnp.stack(all_b)
        x_rows, wl = table_of_x(x_big, x_small), table_of_cot(cot_big, cot_small, counts)
        wl, stack_b = lax.optimization_barrier((wl, stack_b))
        pieces_b = over_dp(stack_b)
        *all_a, x_rows, stack_b = lax.optimization_barrier((*all_a, x_rows, stack_b))
        pieces_a = with_core(all_a)
    else:
        x_rows, wl = table_of_x(x_big, x_small), table_of_cot(cot_big, cot_small, counts)
        pieces_a, pieces_b = ([lax.all_gather(part, fsdp, axis=0, tiled=True)] for part in (shard_a, shard_b))
    if blocked:
        share1 = Shares(sizes, width, 3 * width + 2 * hidden)
        share3 = Blocks(sizes, width, width + TABLE)
    else:
        share1, share3 = Plain(width, 3 * width + 2 * hidden), Plain(width, width + TABLE)

    one = mix_forward(plan, consts, x_rows, pieces_a, sizes)
    if blocked:
        *pieces_b, one["mixed"] = lax.optimization_barrier((*pieces_b, one["mixed"]))
        pieces_b = with_core(pieces_b)
    mid = middle_pass(plan, consts, share1, x_rows, wl, one, pieces_b, sizes)
    if blocked:
        got = over(mid["give"], "core", 1)
        pick = lambda table, index: lax.dynamic_index_in_dim(table, index, 0, keepdims=False)
        part_of = lambda step: pick(mid["keep"], me ^ step) + pick(got, me ^ step)
        by_dp = [part_of(0)] + [over(part_of(step), "dp", step) for step in range(1, n_dp)]
    mix = mix_backward(plan, consts, share3, one, mid)
    if not blocked:
        end = input_pass(plan, x_rows, one, mid, mix)
        images = from_rows(plan, mid["out"], x_big.shape, x_small.shape)
        images += from_rows(plan, end["gx"], x_big.shape, x_small.shape)
        grads, square = whole_sums(plan, sizes, tail, mix["keep"], mid["keep"], width + TABLE)
        grad_norm = jnp.sqrt(square)
        scale = jnp.minimum(1.0, CLIP_NORM / (grad_norm + 1e-06))
        return images + adam_rows(params, grads, first, second, scale) + (grad_norm,)
    count = n_dp * n_z * n_core
    *by_dp, last = lax.optimization_barrier((*by_dp, mix["keep"]))
    summed = sum(part.astype(F32) for part in by_dp).astype(BF16)
    sent = [pick(summed, my_z ^ step) for step in range(n_z)]
    *sent, last, mix["glow"] = lax.optimization_barrier((*sent, last, mix["glow"]))
    both = lax.all_to_all(last.reshape(count, height, share3.part), everywhere, 0, 0)
    by_z = [sent[0]] + [over(sent[step], "z", step) for step in range(1, n_z)]
    end = input_pass(plan, x_rows, one, mid, mix)
    *by_z, end["gx"] = lax.optimization_barrier((*by_z, end["gx"]))
    early = sum(part.astype(F32) for part in by_z).astype(BF16)
    owned = [early] + [over(early, "dp", step) for step in range(1, n_dp)]
    grad_images = from_rows(plan, end["gx"], x_big.shape, x_small.shape)
    both, *rest = lax.optimization_barrier((both, *grad_images, *owned))
    grad_images, owned = rest[:2], rest[2:]
    sums = run(
        late_sums,
        dict(both=both, early=owned[0]),
        dict(late=((height, share3.part), BF16), wide=((count, 8, TABLE), F32)),
        {},
        micros=2,
        limit=4 * 2**20,
    )
    wide = lax.all_to_all(sums["wide"], everywhere, 0, 0)
    late = [sums["late"]] + [over(sums["late"], "dp", step) for step in range(1, n_dp)]
    wide, *outs = lax.optimization_barrier((wide, *from_rows(plan, mid["out"], x_big.shape, x_small.shape)))
    images = tuple(outs) + tuple(grad_images)
    state = ((height, params.shape[1]), F32)
    inputs = dict({"o" + str(step): part for step, part in enumerate(owned)}, wide=wide)
    inputs.update({"l" + str(step): part for step, part in enumerate(late)})
    new = run(
        partial(optimizer, plan, sizes, (share1.part, share3.part), tail),
        dict(inputs, params=params, first=first, second=second),
        dict(new_params=state, new_first=state, new_second=state, norm=((1, 1), F32)),
        dict(
            by_dp=((n_dp, height, share1.part + share3.part), F32),
            flat=((height, up_to(params.shape[1], TABLE)), F32),
        ),
        micros=3,
        limit=16 * 2**20,
    )
    return tuple(images) + (new["new_params"], new["new_first"], new["new_second"], new["norm"].reshape(()))


def solution(mesh):
    n_dp, n_fsdp = mesh.shape["dp"], mesh.shape["fsdp"]
    n_core = 2 if n_fsdp % 2 == 0 else 1
    n_z = n_fsdp // n_core
    split = jax.sharding.Mesh(mesh.devices.reshape(n_dp, n_z, n_core), ("dp", "z", "core"))
    images = P(("dp", "z", "core"), None, None, None)
    rows = P(("z", "core"), None)
    in_specs = (images,) * 4 + (P("dp", ("z", "core"), None),) + (rows,) * 3
    out_specs = (images,) * 4 + (rows,) * 3 + (P(),)
    return jax.shard_map(
        partial(local, (n_dp, n_z, n_core)), mesh=split, in_specs=in_specs, out_specs=out_specs, check_vma=False
    )
```

```python
from functools import partial

import jax
import jax.numpy as jnp
import numpy as np
from jax import lax
from jax.experimental import pallas as pl
from jax.experimental.pallas import tpu as pltpu
from jax.sharding import PartitionSpec as P

FFN = 1536
STEP = 10
CLIP_NORM = 1.0
BETA_ONE = 0.9
BETA_TWO = 0.999
LEARN_RATE = 0.05
DECAY_RATE = 0.05
ADAM_EPS = 1e-08
KERNEL_SIDES = (3, 5, 7)
F32 = jnp.float32
BF16 = jnp.bfloat16
VMEM_BYTES = 58 * 2**20

SLOT = 16


def up_to(value, step):
    return -(-value // step) * step


class Plan:
    def __init__(self, big_shape, small_shape):
        self.n_big, self.side_big = big_shape[0], big_shape[1]
        self.n_small, self.side_small = small_shape[0], small_shape[1]
        self.width = big_shape[3]
        self.pix_big = self.side_big**2
        self.pix_small = self.side_small**2
        self.rows_big = up_to(self.pix_big, SLOT)
        self.group = max(size for size in (1, 2, 3) if self.n_small % size == 0)
        self.n_groups = self.n_small // self.group
        self.rows_small = up_to(self.group * self.pix_small, SLOT)
        self.small_at = self.n_big * self.rows_big
        self.used = self.small_at + self.n_groups * self.rows_small
        self.rows = up_to(self.used, 256)
        self.n_images = self.n_big + self.n_small
        self.image_rows = up_to(self.n_images, SLOT)


def half_spectrum(size):
    reps = []
    for u in range(size):
        for v in range(size):
            other = ((-u) % size, (-v) % size)
            if (u, v) <= other:
                reps.append((u, v, 1.0 if (u, v) == other else 2.0))
    return np.array(reps)


def transform_pair(side, kernel_side, copies):
    margin = kernel_side // 2
    size = side + margin
    reps = half_spectrum(size)
    count = len(reps)
    freq = 2 * np.pi * reps[:, :2] / size
    grid = np.array([(i, j) for i in range(side) for j in range(side)], float)
    lags = np.array([(i - margin, j - margin) for i in range(kernel_side) for j in range(kernel_side)], float)
    phase = freq @ grid.T
    lag_phase = freq @ lags.T
    weight = reps[:, 2:3] / size**2
    pix = side * side
    half = up_to(copies * count, SLOT)
    rows = up_to(copies * pix, SLOT)
    forward = np.zeros((2 * half, rows))
    inverse = np.zeros((rows, 2 * half))
    taps = np.zeros((2 * half, kernel_side**2))
    back = np.zeros((kernel_side**2, 2 * half))
    for one in range(copies):
        low, col = one * count, one * pix
        forward[low : low + count, col : col + pix] = np.cos(phase)
        forward[half + low : half + low + count, col : col + pix] = -np.sin(phase)
        inverse[col : col + pix, low : low + count] = (weight * np.cos(phase)).T
        inverse[col : col + pix, half + low : half + low + count] = -(weight * np.sin(phase)).T
        taps[low : low + count] = np.cos(lag_phase)
        taps[half + low : half + low + count] = np.sin(lag_phase)
        back[:, low : low + count] = (weight * np.cos(lag_phase)).T
        back[:, half + low : half + low + count] = -(weight * np.sin(lag_phase)).T
    return forward, inverse, taps, back


TABLE = 128
LAG = 1
GATES_AT = 0
TAPS_AT = 4
VECS_AT = 87
BIAS_AT = 96


def low_np(values):
    return jnp.asarray(values, F32).astype(BF16)


def high_and_rest(values):
    high = values.astype(np.float32).astype(jnp.bfloat16)
    rest = (values - high.astype(np.float64)).astype(np.float32).astype(jnp.bfloat16)
    return jnp.asarray(high), jnp.asarray(rest)


def constants(plan):
    consts = {}
    tap_at = TAPS_AT
    for level, kernel_side in enumerate(KERNEL_SIDES):
        for kind, side, copies in (("b", plan.side_big, 1), ("s", plan.side_small, plan.group)):
            forward, inverse, taps, back = transform_pair(side, kernel_side, copies)
            wide = np.zeros((taps.shape[0], TABLE))
            wide[:, tap_at : tap_at + kernel_side**2] = taps
            tall = np.zeros((TABLE, taps.shape[0]))
            tall[tap_at : tap_at + kernel_side**2] = back
            consts["f" + kind + str(level)] = low_np(forward)
            consts["g" + kind + str(level)] = low_np(inverse)
            high, rest = high_and_rest(wide)
            consts["k" + kind + str(level)] = jnp.concatenate([high, rest], axis=1)
            consts["t" + kind + str(level)] = low_np(tall)
        tap_at += kernel_side**2
    pick = np.zeros((plan.image_rows, plan.rows))
    for one in range(plan.n_big):
        pick[one, one * plan.rows_big : one * plan.rows_big + plan.pix_big] = 1.0
    for one in range(plan.n_small):
        at = plan.small_at + one // plan.group * plan.rows_small + one % plan.group * plan.pix_small
        pick[plan.n_big + one, at : at + plan.pix_small] = 1.0
    consts["pick"] = low_np(pick)
    consts["spread"] = low_np(pick.T)
    consts["eye"] = low_np(np.eye(TABLE))
    lanes = np.zeros((FFN, plan.width))
    lanes[np.arange(FFN), np.arange(FFN) // (FFN // plan.width)] = 1.0
    consts["lanes"] = low_np(lanes)
    return consts


def dot(left, right):
    return jnp.dot(left, right, preferred_element_type=F32)


def dot_nt(left, right):
    return lax.dot_general(left, right, (((1,), (1,)), ((), ())), preferred_element_type=F32)


def dot_tn(left, right):
    return lax.dot_general(left, right, (((0,), (0,)), ((), ())), preferred_element_type=F32)


def tiles(low, high, step):
    for at in range(low, high, step):
        yield slice(at, min(at + step, high))


def gelu_and_slope(values):
    chance = 0.5 + 0.5 * lax.erf(values * 0.7071067811865476)
    bell = jnp.exp(values * values * -0.5) * 0.3989422804014327
    return values * chance, chance + values * bell


class Refs(dict):
    def __getattr__(self, name):
        return self[name]

    def setup(self, fetched, sent):
        self.used = 0
        self.open = {}
        self.leaving = []
        self.sent = sent
        self.waiting = dict(fetched)

    def plan(self, source, target):
        self.used += 1
        return pltpu.make_async_copy(source, target, self["sems"].at[self.used - 1])

    def copy(self, source, target):
        result = self.plan(source, target)
        result.start()
        return result

    def begin(self, *names):
        for name in names or tuple(self.waiting):
            source, lanes = self.waiting.pop(name)
            far = self[source] if lanes is None else self[source].at[:, lanes]
            self.open[name] = self.copy(far, self[name])

    def begin_parts(self, parts, *names):
        for part in parts:
            for name in names:
                source, _ = self.waiting[name]
                self.open[name, part.start] = self.copy(self[source].at[part], self[name].at[part])
        for name in names:
            self.waiting.pop(name)

    def need_part(self, part, *names):
        self.need(*((name, part.start) for name in names))

    def need(self, *names):
        for name in names:
            if name in self.open:
                self.open.pop(name).wait()

    def send(self, name, at=None):
        far, near = self["far_" + name], self[name]
        if at is not None:
            far, near = far.at[at], near.at[at]
        self.leaving.append(self.copy(near, far))

    def finish(self):
        self.need(*list(self.open))
        for copy in self.leaving:
            copy.wait()


COPIES = 128


def run(body, inputs, outputs, scratch, fetched=None, sent=(), far=(), micros=20, limit=VMEM_BYTES):
    fetched = {name: (name, None) if entry is None else entry for name, entry in (fetched or {}).items()}
    sources = {source for source, _ in fetched.values()}
    buffers = {}
    for name, (source, lanes) in fetched.items():
        shape = inputs[source].shape
        if lanes is not None:
            shape = (shape[0], lanes.stop - lanes.start)
        buffers["near_" + name] = (shape, inputs[source].dtype)
    for name in sent:
        buffers["near_" + name] = outputs[name]
    names = ["in_" + name for name in inputs] + ["out_" + name for name in outputs] + list(scratch) + list(buffers)

    def kernel(*args):
        given = dict(zip(names + ["sems"], args))
        refs = Refs()
        for name in inputs:
            refs[name] = given["in_" + name]
        for name in outputs:
            refs["far_" + name if name in sent else name] = given["out_" + name]
        for name in list(scratch) + ["sems"]:
            refs[name] = given[name]
        entries = {}
        for name, (source, lanes) in fetched.items():
            refs["source_" + source] = given["in_" + source]
            entries[name] = ("source_" + source, lanes)
        for name in list(fetched) + list(sent):
            refs[name] = given["near_" + name]
        refs.setup(entries, sent)
        body(refs)
        refs.finish()

    def space(name, distant):
        return pl.BlockSpec(memory_space=pl.ANY if distant else pltpu.VMEM)

    results = pl.pallas_call(
        kernel,
        in_specs=[space(name, name in sources or name in far) for name in inputs],
        out_specs=[
            pl.BlockSpec(memory_space=pltpu.SMEM) if shape == (1, 1) else space(name, name in sent or name in far)
            for name, (shape, _) in outputs.items()
        ],
        out_shape=[jax.ShapeDtypeStruct(shape, dtype) for shape, dtype in outputs.values()],
        scratch_shapes=[pltpu.VMEM(*entry) for entry in list(scratch.values()) + list(buffers.values())]
        + [pltpu.SemaphoreType.DMA((COPIES,))],
        compiler_params=pltpu.CompilerParams(vmem_limit_bytes=limit),
        cost_estimate=pl.CostEstimate(flops=micros * 10**9, bytes_accessed=micros * 10**6, transcendentals=0),
    )(*inputs.values())
    return dict(zip(outputs, results))


def units(plan):
    result = []
    for one in range(plan.n_big):
        result.append(("b", slice(one * plan.rows_big, (one + 1) * plan.rows_big), len(result)))
    for one in range(plan.n_groups):
        at = plan.small_at + one * plan.rows_small
        result.append(("s", slice(at, at + plan.rows_small), len(result)))
    return result


def pairs(plan):
    result = []
    for kind in "bs":
        same = [unit for unit in units(plan) if unit[0] == kind]
        result += [same[low : low + 2] for low in range(0, len(same), 2)]
    return result


def staggered(chains, lag):
    turn, live = 0, list(enumerate(chains))
    while live:
        left = []
        for index, chain in live:
            if turn < index * lag or next(chain, chains) is not chains:
                left.append((index, chain))
        live = left
        turn += 1


def side_by_side(values):
    return values[0] if len(values) == 1 else jnp.concatenate(values, axis=1)


def wave_rows(plan, consts):
    result, total = {}, []
    for level in range(3):
        at = 0
        for kind, _, index in units(plan):
            count = consts["f" + kind + str(level)].shape[0]
            result[level, index] = slice(at, at + count)
            at += count
        total.append(at)
    return result, total


def spectrum_of_taps(refs, name, table):
    refs["h" + name][...] = dot_nt(refs["k" + name][:, :TABLE], table) + dot_nt(refs["k" + name][:, TABLE:], table)


def image_scale(plan):
    row = lax.broadcasted_iota(jnp.int32, (plan.image_rows, 1), 0)
    return jnp.where(row < plan.n_big, 1.0 / plan.pix_big, 1.0 / plan.pix_small).astype(F32)


def unit_rows(values):
    center = values - jnp.mean(values, axis=-1, keepdims=True)
    scale = lax.rsqrt(jnp.mean(center * center, axis=-1, keepdims=True) + 1e-05)
    return center * scale, scale


def fold(values):
    total = values[0:8]
    for low in range(8, values.shape[0], 8):
        total = total + values[low : low + 8]
    return total


def column_sum(values):
    return jnp.sum(values, axis=0, keepdims=True)


def forward_mix(plan, places, sizes, n_pieces, refs):
    rows, width, hidden = plan.rows, plan.width, FFN
    arriving = sum(gather(refs, sizes, n_pieces, "wa"), [])
    start_all(arriving)
    refs.begin()
    wait_all(arriving)
    refs.send("wa")
    refs.need("eye")
    inner = width + TABLE
    table = refs.wa[:, width:inner]
    refs.vec[...] = dot_nt(refs.eye[...], table)
    refs.need("x")
    gain = refs.vec[VECS_AT : VECS_AT + 1, :]
    shift = refs.vec[VECS_AT + 1 : VECS_AT + 2, :]
    for block in tiles(0, rows, 256):
        for at in tiles(block.start, block.stop, 32):
            unit, _ = unit_rows(refs.x[at, :].astype(F32))
            refs.unit[at, :] = unit.astype(BF16)
            refs.normed[at, :] = (unit * gain + shift).astype(BF16)
        refs.send("normed", block)
        refs.send("unit", block)
        part = dot(refs.normed[block, :], refs.wa[:, :inner])
        refs.context[block, :] = (part[:, :width] + refs.vec[VECS_AT + 3 : VECS_AT + 4, :]).astype(BF16)
        refs.gate[block, :] = part[:, width:]
    refs.send("gate")
    if rows > plan.used:
        refs.c[:, plan.used :, :] = jnp.zeros((3, rows - plan.used, width), BF16)
        refs.gp[:, plan.used :, :] = jnp.zeros((3, rows - plan.used, width), BF16)
    ready, finished = set(), {level: 0 for level in range(3)}

    def chain(pair):
        for level in range(3):
            name = pair[0][0] + str(level)
            if name not in ready:
                ready.add(name)
                refs.need("f" + name, "k" + name, "g" + name)
                spectrum_of_taps(refs, name, table)
            hat = refs["hat" + str(level)]
            field_in = refs.context if level == 0 else refs.c.at[level - 1]
            count = refs["f" + name].shape[0]
            half = count // 2
            taps = refs["h" + name]
            both = dot(refs["f" + name][...], side_by_side([field_in[at, :] for _, at, _ in pair]))
            for place, (_, _, index) in enumerate(pair):
                refs.wave[index, :count, :] = both[:, place * width : (place + 1) * width]
            yield
            for _, _, index in pair:
                wave, low_wave = refs.wave.at[index], refs.wave_low.at[index]
                saved = places[level, index].start
                for re in tiles(0, half, 16):
                    im = slice(half + re.start, half + re.stop)
                    wave_re, wave_im = wave[re, :], wave[im, :]
                    tap_re, tap_im = taps[re, :], taps[im, :]
                    hat[saved + re.start : saved + re.stop, :] = wave_re.astype(BF16)
                    hat[saved + im.start : saved + im.stop, :] = wave_im.astype(BF16)
                    low_wave[re, :] = (wave_re * tap_re - wave_im * tap_im).astype(BF16)
                    low_wave[im, :] = (wave_re * tap_im + wave_im * tap_re).astype(BF16)
                yield
            both = dot(refs["g" + name][...], side_by_side([refs.wave_low[index, :count, :] for _, _, index in pair]))
            for place, (_, at, _) in enumerate(pair):
                refs.field[at, :] = both[:, place * width : (place + 1) * width]
            yield
            for _, at, _ in pair:
                for into in tiles(at.start, at.stop, 16):
                    value, slope = gelu_and_slope(refs.field[into, :])
                    refs.c[level, into, :] = value.astype(BF16)
                    refs.gp[level, into, :] = slope.astype(BF16)
                yield
            finished[level] += 1
            if finished[level] == len(pairs(plan)):
                refs.send("c", slice(level, level + 1))
                refs.send("gp", slice(level, level + 1))
                refs.send("hat" + str(level))

    staggered([chain(pair) for pair in pairs(plan)], LAG)
    refs.need("pick", "spread")
    mean = dot(refs.pick[...], refs.c[2]) * image_scale(plan)
    summary, slope = gelu_and_slope(mean)
    refs.sum[0] = summary
    refs.sum[1] = slope
    summary_low = summary.astype(BF16)
    for block in tiles(0, rows, 256):
        refs.field[block, :] = dot(refs.spread[block, :], summary_low)
        for at in tiles(block.start, block.stop, 32):
            gate = refs.gate[at, :]
            total = refs.field[at, :] * gate[:, 3:4]
            for level in range(3):
                total += refs.c[level, at, :].astype(F32) * gate[:, level : level + 1]
            refs.mixed[at, :] = total.astype(BF16)
        refs.send("mixed", block)
    refs.need("lanes")
    ratio = hidden // width
    spread = dot_nt(refs.vec[BIAS_AT : BIAS_AT + 16, :].astype(BF16), refs.lanes[...])
    row = lax.broadcasted_iota(jnp.int32, (16, hidden), 0)
    lane = lax.broadcasted_iota(jnp.int32, (16, hidden), 1)
    picked = jnp.where(lax.rem(lane, ratio) == row, spread, 0.0)
    refs.upb[...] = jnp.broadcast_to(jnp.sum(picked, axis=0, keepdims=True), (8, hidden))


def mix_scratch(plan, consts):
    scratch = {}
    for level in range(3):
        for kind in "bs":
            scratch["h" + kind + str(level)] = ((consts["f" + kind + str(level)].shape[0], plan.width), F32)
    return scratch


def most_waves(consts):
    return max(consts["f" + kind + str(level)].shape[0] for level in range(3) for kind in "bs")


def mix_forward(plan, consts, x_rows, pieces, sizes):
    rows, width = plan.rows, plan.width
    waves, n_units = most_waves(consts), len(units(plan))
    places, saved = wave_rows(plan, consts)
    keys = [k + kind + str(level) for level in range(3) for kind in "bs" for k in "fkg"]
    names = ["eye"] + keys + ["pick", "spread", "lanes"]
    inputs = dict(x=x_rows, **{k: consts[k] for k in names})
    apart = {"w" + str(step): piece for step, piece in enumerate(pieces)}
    inputs.update(apart)
    outputs = dict(
        wa=((width, width + 2 * TABLE), BF16),
        normed=((rows, width), BF16),
        unit=((rows, width), BF16),
        c=((3, rows, width), BF16),
        gp=((3, rows, width), BF16),
        **{"hat" + str(level): ((saved[level], width), BF16) for level in range(3)},
        mixed=((rows, width), BF16),
        gate=((rows, TABLE), F32),
        vec=((TABLE, width), F32),
        upb=((8, FFN), F32),
        sum=((2, plan.image_rows, width), F32),
    )
    scratch = dict(
        wave=((n_units, waves, width), F32),
        wave_low=((n_units, waves, width), BF16),
        field=((rows, width), F32),
        context=((rows, width), BF16),
        **mix_scratch(plan, consts),
    )
    sent = ("normed", "unit", "c", "gp", "hat0", "hat1", "hat2", "mixed", "gate")
    sent += ("wa",)
    body = partial(forward_mix, plan, places, sizes, len(pieces))
    return run(body, inputs, outputs, scratch, {k: None for k in ["x"] + names}, sent, list(apart), 2)


def gather(refs, sizes, n_pieces, target, base=0):
    n_dp, n_z, n_core = sizes
    if n_pieces == 1:
        return [[refs.plan(refs["w0"], refs[target].at[:, base:])]]
    me, my_z, my_core = (lax.axis_index(name) for name in ("dp", "z", "core"))

    def place(piece, z, step, lanes):
        height = piece.shape[0]
        owner = (my_z ^ z) * n_core + (my_core ^ (step % n_core))
        return refs.plan(piece, refs[target].at[pl.ds(pl.multiple_of(owner * height, 16), height), lanes])

    copies = [[] for _ in range(n_pieces // n_core)]
    for step in range(n_pieces):
        piece = refs["w" + str(step)]
        if len(piece.shape) == 2:
            copies[step // n_core].append(place(piece, step // n_core, step, slice(None)))
            continue
        part = piece.shape[2]
        lanes = pl.ds(base + pl.multiple_of((me ^ (step // n_core)) * part, TABLE), part)
        copies[step // n_core] += [place(piece.at[other], other, step, lanes) for other in range(n_z)]
    return copies


def for_quarter(copies, quarter, act):
    if len(copies) == 1:
        if quarter == 0:
            act(copies[0])
        return
    me = lax.axis_index("dp")
    for step, some in enumerate(copies):
        pl.when((me ^ step) == quarter)(partial(act, some))


def start_all(copies):
    for copy in copies:
        copy.start()


def wait_all(copies):
    for copy in copies:
        copy.wait()


class Shares:
    def __init__(self, sizes, rows, columns):
        self.n_dp, self.n_z, self.n_core = sizes
        self.height = rows // (self.n_z * self.n_core)
        self.part = up_to(columns, TABLE * self.n_dp) // self.n_dp
        self.empty = self.part * self.n_dp - columns
        self.shape = (self.n_core, self.n_dp, self.n_z, self.height, self.part)
        self.columns = columns

    def place(self, core, share, z):
        return (core, share, z)

    def put(self, ref, low, values):
        done = 0
        while done < values.shape[1]:
            share, at = divmod(low + done, self.part)
            take = min(self.part - at, values.shape[1] - done)
            for owner in range(self.n_z * self.n_core):
                z, core = divmod(owner, self.n_core)
                ref[self.place(core, share, z) + (slice(None), slice(at, at + take))] = values[
                    owner * self.height : (owner + 1) * self.height, done : done + take
                ]
            done += take

    def send(self, refs, stage, names, low, high):
        core = lax.axis_index("core")
        for share in range(self.n_dp):
            if low < (share + 1) * self.part <= high:
                for source, name in ((1 - core, names[1]), (core, names[0])):
                    refs.leaving.append(refs.copy(stage.at[source, share], refs[name].at[share]))

    def close(self, refs, stage, names):
        if self.empty:
            self.put(stage, self.columns, jnp.zeros((self.height * self.n_z * self.n_core, self.empty), BF16))
        self.send(refs, stage, names, self.columns, self.part * self.n_dp)


class Blocks(Shares):
    def __init__(self, sizes, rows, columns):
        super().__init__(sizes, rows, columns)
        self.shape = (self.n_dp, self.n_z, self.n_core, self.height, self.part)

    def place(self, core, share, z):
        return (share, z, core)

    def close(self, refs, stage, names):
        refs.leaving.append(refs.copy(stage, refs[names[0]]))


class Plain:
    def __init__(self, rows, columns):
        self.shape = (rows, columns)

    def put(self, ref, low, values):
        ref[:, low : low + values.shape[1]] = values

    def send(self, refs, stage, names, low, high):
        pass

    def close(self, refs, stage, names):
        refs.leaving.append(refs.copy(stage, refs[names[0]]))


def input_grads(product, sums, weight, table):
    gain = table[:, VECS_AT : VECS_AT + 1].astype(F32)
    shift = table[:, VECS_AT + 1 : VECS_AT + 2].astype(F32)
    weight = weight.astype(F32)
    lane = lax.broadcasted_iota(jnp.int32, (1, TABLE), 1)
    parts = jnp.where(lane == VECS_AT, jnp.sum(product * weight, axis=-1, keepdims=True), 0.0)
    parts = jnp.where(lane == VECS_AT + 1, jnp.sum(sums * weight, axis=-1, keepdims=True), parts)
    return gain * product + shift * sums, parts


def middle(plan, shares, sizes, n_pieces, refs):
    rows, width, hidden = plan.rows, plan.width, FFN
    vec = lambda index: refs.vec[VECS_AT + index : VECS_AT + index + 1, :]
    zero = jnp.zeros((8, width), F32)
    sums = {index: zero for index in (2, 4, 5, 6, 7, 8)}
    blocks = list(tiles(0, rows, 256))
    up_at = 3 * width
    down_at = up_at + hidden
    wq, wm, wo = (refs.wb.at[:, at * width : (at + 1) * width] for at in range(3))
    wu, wd = refs.wb.at[:, up_at:down_at], refs.wb.at[:, down_at : down_at + hidden]
    refs.begin("mixed", "normed")
    arriving = gather(refs, sizes, n_pieces, "wb", TABLE)
    first_tile = refs.copy(refs.wa.at[:, width + TABLE :], refs.wb.at[:, :TABLE])
    for quarter in range(sizes[0]):
        for_quarter(arriving, quarter, start_all)
    refs.begin()
    refs.need("mixed", "normed")
    first_tile.wait()
    for_quarter(arriving, 0, wait_all)

    def before(block):
        modulator = dot(refs.mixed[block, :], wm[...]) + vec(4)
        queries = dot(refs.normed[block, :], wq[...]) + vec(2)
        refs.mod[block, :] = modulator.astype(BF16)
        refs.q[block, :] = queries.astype(BF16)
        refs.prod[block, :] = (queries * modulator).astype(BF16)
        yield
        refs.need("x")
        refs.resid[block, :] = dot(refs.prod[block, :], wo[...])
        yield
        for part in tiles(block.start, block.stop, 64):
            for at in tiles(part.start, part.stop, 32):
                resid = refs.resid[at, :] + refs.x[at, :].astype(F32) + vec(5)
                refs.resid[at, :] = resid
                unit, scale = unit_rows(resid)
                refs.unit[at, :] = unit
                refs.scale[at, :] = jnp.broadcast_to(scale, (scale.shape[0], TABLE))
                refs.n2[at, :] = (unit * vec(6) + vec(7)).astype(BF16)
            yield

    def mlp(block):
        refs.need("wl")
        for index, lanes in enumerate(tiles(0, hidden, 256)):
            pre, grad_act = refs.pa.at[index % 3], refs.ga.at[index % 3]
            pre[...] = dot(refs.n2[block, :], wu[:, lanes])
            grad_act[...] = dot(refs.wl[block, :], wd[:, lanes])
            bias = refs.upb[0:1, lanes]
            total = jnp.zeros((8, 256), F32) if block.start == 0 else refs.gub[:, lanes]
            for low in tiles(0, 256, 16):
                at = slice(block.start + low.start, block.start + low.stop)
                value, slope = gelu_and_slope(pre[low, :] + bias)
                grad = grad_act[low, :] * slope
                refs.act[at, lanes] = value.astype(BF16)
                refs.pre[at, lanes] = grad.astype(BF16)
                total = total + fold(grad)
            refs.gub[:, lanes] = total
            yield

    def after(block):
        refs.gn[block, :] = dot_nt(refs.pre[block, :], wu[...])
        yield
        refs.out[block, :] = (refs.resid[block, :] + dot_nt(refs.act[block, :], wd[...]) + vec(8)).astype(BF16)
        refs.send("out", block)
        yield
        for part in tiles(block.start, block.stop, 128):
            for at in tiles(part.start, part.stop, 32):
                grad = refs.gn[at, :]
                unit = refs.unit[at, :]
                weighted = refs.wl[at, :].astype(F32)
                gained = grad * vec(6)
                mean_one = jnp.mean(gained, axis=-1, keepdims=True)
                mean_two = jnp.mean(gained * unit, axis=-1, keepdims=True)
                result = weighted + refs.scale[at, 0:1] * (gained - mean_one - unit * mean_two)
                refs.gres[at, :] = result
                refs.glow[at, :] = result.astype(BF16)
                for index, new in ((6, grad * unit), (7, grad), (5, result), (8, weighted)):
                    sums[index] = sums[index] + fold(new)
            yield
        refs.send("gres", block)
        refs.gn[block, :] = dot_nt(refs.glow[block, :], wo[...])
        yield
        for at in tiles(block.start, block.stop, 32):
            grad = refs.gn[at, :]
            grad_query = grad * refs.mod[at, :].astype(F32)
            grad_mod = grad * refs.q[at, :].astype(F32)
            refs.gq[at, :] = grad_query.astype(BF16)
            refs.gmod[at, :] = grad_mod.astype(BF16)
            for index, new in ((2, grad_query), (4, grad_mod)):
                sums[index] = sums[index] + fold(new)
        refs.send("gq", block)
        refs.gmix[block, :] = dot_nt(refs.gmod[block, :], wm[...]).astype(BF16)
        refs.send("gmix", block)
        yield

    def together(*steps):
        steps = list(steps)
        while steps:
            steps = [step for step in steps if next(step, refs) is not refs]

    together(before(blocks[0]))
    for quarter in range(1, sizes[0]):
        for_quarter(arriving, quarter, wait_all)
    refs.leaving.append(refs.copy(wq, refs.wq))
    for index in range(len(blocks) + 1):
        steps = []
        if index < len(blocks):
            steps.append(mlp(blocks[index]))
        if index + 1 < len(blocks):
            steps.append(before(blocks[index + 1]))
        if index:
            steps.append(after(blocks[index - 1]))
        together(*steps)
    names = ("keep", "give")

    def put(low, values):
        shares.put(refs.stage, low, values.astype(BF16))
        shares.send(refs, refs.stage, names, low, low + values.shape[1])

    for lanes in tiles(0, hidden, 256):
        put(lanes.start, dot_tn(refs.n2[...], refs.pre[:, lanes]))
    for lanes in tiles(0, hidden, 256):
        put(hidden + lanes.start, dot_tn(refs.wl[...], refs.act[:, lanes]))
    refs.need("unit_in", "table")
    product = dot_tn(refs.unit_in[...], refs.gq[...])
    product, refs.parts[...] = input_grads(product, column_sum(sums[2]), wq[...], refs.table[...])
    put(2 * hidden, product)
    put(2 * hidden + width, dot_tn(refs.mixed[...], refs.gmod[...]))
    put(2 * hidden + 2 * width, dot_tn(refs.prod[...], refs.glow[...]))
    shares.close(refs, refs.stage, names)
    refs.gv[...] = jnp.zeros(refs.gv.shape, F32)
    for index, total in sums.items():
        refs.gv[index : index + 1, :] = column_sum(total)
    ratio = hidden // width
    row = lax.broadcasted_iota(jnp.int32, (16, hidden), 0)
    lane = lax.broadcasted_iota(jnp.int32, (16, hidden), 1)
    picked = jnp.where(lax.rem(lane, ratio) == row, column_sum(refs.gub[...]), 0.0).astype(BF16)
    refs.need("lanes")
    refs.gv[16:32, :] = dot(picked, refs.lanes[...])


def kept(shares):
    if isinstance(shares, (Plain, Blocks)):
        return dict(keep=(shares.shape, BF16))
    return dict(keep=(shares.shape[1:], BF16), give=(shares.shape[1:], BF16))


def middle_pass(plan, consts, shares, x_rows, wl, first, pieces, sizes):
    rows, width, hidden = plan.rows, plan.width, FFN
    near = dict(mixed=first["mixed"], normed=first["normed"], x=x_rows, wl=wl, unit_in=first["unit"], lanes=consts["lanes"])
    apart = {"w" + str(step): piece for step, piece in enumerate(pieces)}
    inputs = dict(near, wa=first["wa"], vec=first["vec"], upb=first["upb"], **apart)
    fetched = dict({k: None for k in near}, table=("wa", slice(width, width + TABLE)))
    token, field, wide = ((rows, width), BF16), ((rows, width), F32), ((rows, hidden), BF16)
    outputs = dict(kept(shares), out=token, gq=token, gmix=token, gres=field)
    outputs.update(wq=((width, width), BF16), gv=((32, width), F32), parts=((width, TABLE), F32))
    scratch = dict(mod=token, q=token, prod=token, glow=token, gmod=token, n2=token)
    scratch.update(resid=field, unit=field, gn=field, act=wide, pre=wide)
    scratch.update(
        scale=((rows, TABLE), F32),
        pa=((3, 256, 256), F32),
        ga=((3, 256, 256), F32),
        gub=((8, hidden), F32),
        stage=(shares.shape, BF16),
        wb=((width, TABLE + up_to(3 * width + 2 * hidden - TABLE, TABLE * sizes[0])), BF16),
    )
    body = partial(middle, plan, shares, sizes, len(pieces))
    far = ["keep", "give", "wq", "wa"] + list(apart)
    return run(body, inputs, outputs, scratch, fetched, ("out", "gq", "gmix", "gres"), far, 26)


def backward_mix(plan, places, shares, refs):
    rows, width = plan.rows, plan.width
    refs.begin("gmix", "gate", "pick", "spread", "wa")
    refs.begin_parts([slice(level, level + 1) for level in (2, 1, 0)], "gp")
    refs.begin()
    refs.need("gmix", "gate")
    for at in tiles(0, rows, 32):
        refs.tmp[at, :] = (refs.gmix[at, :].astype(F32) * refs.gate[at, 3:4]).astype(BF16)
    refs.need("pick", "spread", "wa")
    table = refs.wa[:, width : width + TABLE]
    grad_summary = dot(refs.pick[...], refs.tmp[...]) * refs.sum[1] * image_scale(plan)
    grad_summary_low = grad_summary.astype(BF16)
    for block in tiles(0, rows, 256):
        refs.gc[block, :] = dot(refs.spread[block, :], grad_summary_low)
    summary_low = refs.sum[0].astype(BF16)
    lane = lax.broadcasted_iota(jnp.int32, (1, TABLE), 1)

    def gates(low, high):
        refs.need("c")
        for at in tiles(low, high, 32):
            grad = refs.gmix[at, :].astype(F32)
            spread = dot(refs.spread[at, :], summary_low)
            result = jnp.where(lane == 3, jnp.sum(grad * spread, axis=-1, keepdims=True), 0.0)
            for level in range(3):
                part = jnp.sum(grad * refs.c[level, at, :].astype(F32), axis=-1, keepdims=True)
                result = jnp.where(lane == level, part, result)
            refs.ggate[at, :] = result.astype(BF16)

    ready, seen = set(), set()

    def chain(pair):
        for level in (2, 1, 0):
            kind = pair[0][0]
            name = kind + str(level)
            if name not in ready:
                ready.add(name)
                refs.need("f" + name, "k" + name, "g" + name, "hat" + str(level))
                spectrum_of_taps(refs, name, table)
            refs.need_part(slice(level, level + 1), "gp")
            hat = refs["hat" + str(level)]
            count = refs["f" + name].shape[0]
            half = count // 2
            taps, cross = refs["h" + name], refs["x" + name]
            for _, at, _ in pair:
                for into in tiles(at.start, at.stop, 16):
                    direct = refs.gmix[into, :].astype(F32) * refs.gate[into, level : level + 1]
                    grad = refs.gc[into, :] + direct
                    refs.tmp[into, :] = (grad * refs.gp[level, into, :].astype(F32)).astype(BF16)
            yield
            both = dot(refs["f" + name][...], side_by_side([refs.tmp[at, :] for _, at, _ in pair]))
            for place, (_, _, index) in enumerate(pair):
                refs.wave[index, :count, :] = both[:, place * width : (place + 1) * width]
            yield
            for re in tiles(0, half, 16):
                im = slice(half + re.start, half + re.stop)
                tap_re, tap_im = taps[re, :], taps[im, :]
                cross_re = cross_im = None
                for _, _, index in pair:
                    saved = places[level, index].start
                    wave_re = hat[saved + re.start : saved + re.stop, :].astype(F32)
                    wave_im = hat[saved + im.start : saved + im.stop, :].astype(F32)
                    grad_re, grad_im = refs.wave[index, re, :], refs.wave[index, im, :]
                    refs.wave_low[index, re, :] = (grad_re * tap_re + grad_im * tap_im).astype(BF16)
                    refs.wave_low[index, im, :] = (grad_im * tap_re - grad_re * tap_im).astype(BF16)
                    new_re = grad_re * wave_re + grad_im * wave_im
                    new_im = grad_re * wave_im - grad_im * wave_re
                    cross_re = new_re if cross_re is None else cross_re + new_re
                    cross_im = new_im if cross_im is None else cross_im + new_im
                if name in seen:
                    cross_re = cross_re + cross[re, :]
                    cross_im = cross_im + cross[im, :]
                cross[re, :] = cross_re
                cross[im, :] = cross_im
                if re.start == half // 32 * 16:
                    yield
            seen.add(name)
            yield
            both = dot(refs["g" + name][...], side_by_side([refs.wave_low[index, :count, :] for _, _, index in pair]))
            for place, (_, at, _) in enumerate(pair):
                refs.gc[at, :] = both[:, place * width : (place + 1) * width]
            yield

    def gate_chain():
        for block in tiles(0, rows, 128):
            gates(block.start, block.stop)
            yield

    chains = [chain(pair) for pair in pairs(plan)]
    staggered(chains[:1] + [gate_chain()] + chains[1:], LAG)
    taps_total = jnp.zeros((TABLE, width), F32)
    for level in range(3):
        for kind in "bs":
            name = kind + str(level)
            refs.need("t" + name)
            taps_total = taps_total + dot(refs["t" + name][...], refs["x" + name][...].astype(BF16))
    refs.gtab[...] = taps_total
    if rows > plan.used:
        refs.gc[plan.used :, :] = jnp.zeros((rows - plan.used, width), F32)
    context_total = jnp.zeros((8, width), F32)
    for block in tiles(0, rows, 256):
        for at in tiles(block.start, block.stop, 32):
            grad = refs.gc[at, :]
            refs.glow[at, :] = grad.astype(BF16)
            context_total = context_total + fold(grad)
        refs.send("glow", block)
    refs.gtab[VECS_AT + 2 : VECS_AT + 3, :] = refs.gv[2:3, :]
    refs.gtab[VECS_AT + 3 : VECS_AT + 4, :] = column_sum(context_total)
    refs.gtab[VECS_AT + 4 : VECS_AT + 9, :] = refs.gv[4:9, :]
    refs.gtab[BIAS_AT : BIAS_AT + 4, :] = refs.gv[16:20, :]
    refs.need("unit", "eye")
    product = dot_tn(refs.unit[...], refs.glow[...])
    product, parts = input_grads(product, column_sum(context_total), refs.wa[:, :width], table)
    shares.put(refs.stage, 0, product.astype(BF16))
    gate_total = jnp.zeros((8, TABLE), F32)
    for at in tiles(0, rows, 64):
        gate_total = gate_total + fold(refs.ggate[at, :].astype(F32))
    small, more = input_grads(dot_tn(refs.unit[...], refs.ggate[...]), column_sum(gate_total), table, table)
    small = small + parts + more + refs.parts[...] + dot_tn(refs.gtab[...].astype(BF16), refs.eye[...])
    shares.put(refs.stage, width, small.astype(BF16))
    shares.close(refs, refs.stage, ("keep",))


def input_back(plan, refs):
    rows, width = plan.rows, plan.width
    blocks = list(tiles(0, rows, 256))
    refs.begin("wq", "wa")
    refs.begin_parts(blocks, "gq", "glow", "ggate", "x", "gres")
    refs.need("wq", "wa")
    gain = refs.vec[VECS_AT : VECS_AT + 1, :]
    for block in blocks:
        refs.need_part(block, "gq", "glow", "ggate", "x", "gres")
        refs.gc[block, :] = (
            dot_nt(refs.gq[block, :], refs.wq[...])
            + dot_nt(refs.glow[block, :], refs.wa[:, :width])
            + dot_nt(refs.ggate[block, :], refs.wa[:, width : width + TABLE])
        )
        for at in tiles(block.start, block.stop, 32):
            unit, scale_row = unit_rows(refs.x[at, :].astype(F32))
            gained = refs.gc[at, :] * gain
            mean_one = jnp.mean(gained, axis=-1, keepdims=True)
            mean_two = jnp.mean(gained * unit, axis=-1, keepdims=True)
            result = refs.gres[at, :] + scale_row * (gained - mean_one - unit * mean_two)
            refs.gx[at, :] = result.astype(BF16)
        refs.send("gx", block)


def mix_backward(plan, consts, shares, first, mid):
    rows, width = plan.rows, plan.width
    waves, n_units = most_waves(consts), len(units(plan))
    places, _ = wave_rows(plan, consts)
    keys = [k + kind + str(level) for level in (2, 1, 0) for k in "kfgt" for kind in "bs"]
    near = dict(gmix=mid["gmix"], gate=first["gate"], pick=consts["pick"], spread=consts["spread"], wa=first["wa"])
    near["gp"] = first["gp"]
    for level in (2, 1, 0):
        near.update({name: consts[name] for name in keys if name.endswith(str(level))})
        near["hat" + str(level)] = first["hat" + str(level)]
        near["c"] = first["c"]
    near.update(unit=first["unit"], eye=consts["eye"])
    inputs = dict(near, sum=first["sum"], gv=mid["gv"], parts=mid["parts"])
    outputs = dict(kept(shares), glow=((rows, width), BF16), ggate=((rows, TABLE), BF16))
    scratch = dict(
        wave=((n_units, waves, width), F32),
        wave_low=((n_units, waves, width), BF16),
        **{k.replace("f", "x"): ((consts[k].shape[0], width), F32) for k in keys if k[0] == "f"},
        gc=((rows, width), F32),
        tmp=((rows, width), BF16),
        gtab=((TABLE, width), F32),
        stage=(shares.shape, BF16),
        **mix_scratch(plan, consts),
    )
    body = partial(backward_mix, plan, places, shares)
    return run(body, inputs, outputs, scratch, {k: None for k in near}, ("glow",), ("keep",), 18)


def input_pass(plan, x_rows, first, mid, mix):
    rows, width = plan.rows, plan.width
    near = dict(glow=mix["glow"], wa=first["wa"], ggate=mix["ggate"], wq=mid["wq"], gq=mid["gq"], x=x_rows)
    near["gres"] = mid["gres"]
    inputs = dict(near, vec=first["vec"])
    outputs = dict(gx=((rows, width), BF16))
    scratch = dict(gc=((rows, width), F32))
    return run(partial(input_back, plan), inputs, outputs, scratch, {k: None for k in near}, ("gx",), micros=7)


def adam_rows(params, grads, first, second, scale):
    clipped = grads * scale
    first_new = BETA_ONE * first + (1.0 - BETA_ONE) * clipped
    second_new = BETA_TWO * second + (1.0 - BETA_TWO) * clipped * clipped
    first_hat = first_new * (1.0 / (1.0 - BETA_ONE**STEP))
    second_hat = second_new * (1.0 / (1.0 - BETA_TWO**STEP))
    params_new = params - LEARN_RATE * (first_hat / (jnp.sqrt(second_hat) + ADAM_EPS) + DECAY_RATE * params)
    return (params_new, first_new, second_new)


def to_rows(plan, big, small):
    tables = []
    for images, count, pix, rows in (
        (big, plan.n_big, plan.pix_big, plan.rows_big),
        (small, plan.n_groups, plan.group * plan.pix_small, plan.rows_small),
    ):
        table = jnp.pad(images.reshape(count, pix, plan.width), ((0, 0), (0, rows - pix), (0, 0)))
        tables.append(table.reshape(count * rows, plan.width))
    if plan.rows > plan.used:
        tables.append(jnp.zeros((plan.rows - plan.used, plan.width), big.dtype))
    return jnp.concatenate(tables, axis=0)


def from_rows(plan, table, big_shape, small_shape):
    big = table[: plan.small_at].reshape(plan.n_big, plan.rows_big, plan.width)[:, : plan.pix_big]
    small = table[plan.small_at : plan.used].reshape(plan.n_groups, plan.rows_small, plan.width)
    return big.reshape(big_shape), small[:, : plan.group * plan.pix_small].reshape(small_shape)


def whole_sums(plan, sizes, tail, late, early, late_columns):
    fsdp = ("z", "core")
    width, hidden = plan.width, FFN
    rows = late.shape[0]
    table = jnp.concatenate([late[:, :late_columns], early], axis=1)
    if sizes[1] * sizes[2] > 1:
        table = lax.psum_scatter(table, fsdp, scatter_dimension=0, tiled=True)
    table = lax.psum(table, "dp").astype(F32)
    ups, rest = late_columns, late_columns + 2 * hidden
    grads = jnp.concatenate(
        [
            table[:, rest : rest + width],
            table[:, : width + 4],
            table[:, rest + width :],
            table[:, ups:rest],
            table[:, width + 4 : width + 4 + tail],
        ],
        axis=1,
    )
    return grads, lax.psum(jnp.sum(grads * grads), fsdp)


def late_sums(refs):
    late = refs.both[0].astype(F32)
    for index in range(1, refs.both.shape[0]):
        late = late + refs.both[index].astype(F32)
    late = late.astype(BF16)
    refs.late[...] = late
    square = jnp.sum(jnp.square(refs.early[...].astype(F32))) + jnp.sum(jnp.square(late.astype(F32)))
    refs.wide[...] = jnp.full(refs.wide.shape, square, F32)


def optimizer(plan, sizes, parts, tail, refs):
    n_dp = sizes[0]
    refs.begin()
    part1, part3 = parts
    width, hidden = plan.width, FFN
    me = lax.axis_index("dp")
    split = part1
    for step in range(n_dp):
        at = pl.ds(me ^ step, 1)
        refs.by_dp[at, :, :split] = refs["o" + str(step)][...].astype(F32)[None]
        refs.by_dp[at, :, split:] = refs["l" + str(step)][...].astype(F32)[None]
    blocks = [refs.by_dp[index] for index in range(n_dp)]
    cut = lambda low, high: jnp.concatenate([block[:, low:high] for block in blocks], axis=1)
    early = cut(0, part1)
    lates = cut(part1, part1 + part3)
    table = lates[:, width : width + TABLE]
    mids = 2 * hidden + width
    refs.flat[:, :width] = early[:, 2 * hidden : mids]
    refs.flat[:, width : 2 * width] = lates[:, :width]
    moved = [early[:, mids : mids + 2 * width], early[:, : 2 * hidden], pltpu.roll(table, TABLE - 4, 1)]
    moved = jnp.concatenate(moved, axis=1)
    refs.flat[:, 2 * width :] = pltpu.roll(moved, 4, 1)
    total = refs.wide[0]
    for index in range(1, refs.wide.shape[0]):
        total = total + refs.wide[index]
    norm = jnp.sqrt(total)
    refs.norm[0, 0] = norm[0, 0]
    scale = jnp.minimum(1.0, CLIP_NORM / (norm[0:1, 0:1] + 1e-06))
    columns = refs.params.shape[1]
    for lanes in tiles(0, columns, 512):
        new = adam_rows(
            refs.params[:, lanes], refs.flat[:, lanes], refs.first[:, lanes], refs.second[:, lanes], scale
        )
        for name, value in zip(("new_params", "new_first", "new_second"), new):
            refs[name][:, lanes] = value


def local(sizes, x_big, x_small, cot_big, cot_small, counts, params, first, second):
    n_dp, n_z, n_core = sizes
    fsdp = ("z", "core")
    everywhere = ("dp",) + fsdp
    width = x_big.shape[-1]
    hidden = FFN
    plan = Plan(x_big.shape, x_small.shape)
    consts = constants(plan)
    height = params.shape[0]
    mod_at = 2 * width + 4
    tail_at = mod_at + 2 * width + 2 * hidden
    tail = params.shape[1] - tail_at
    power = all(size & (size - 1) == 0 for size in sizes)
    blocked = height % 16 == 0 and n_core == 2 and power and n_dp <= 4 and n_z <= 4

    def over(part, axis, step):
        return lax.ppermute(part, axis, [(index, index ^ step) for index in range(sizes[axis_of[axis]])])

    axis_of = dict(dp=0, z=1, core=2)
    def table_of_x(x_big, x_small):
        return to_rows(plan, x_big, x_small)

    def table_of_cot(cot_big, cot_small, counts):
        count_pair = counts.reshape(2)
        live_big = (jnp.arange(cot_big.shape[0]) < count_pair[0]).astype(BF16)
        live_small = (jnp.arange(cot_small.shape[0]) < count_pair[1]).astype(BF16)
        return to_rows(plan, cot_big * live_big[:, None, None, None], cot_small * live_small[:, None, None, None])

    shard = params.astype(BF16)
    empty = lambda columns: [jnp.zeros((height, columns), BF16)]
    shard_a = [shard[:, width:mod_at], shard[:, tail_at:]] + empty(TABLE - 4 - tail) + [shard[:, :TABLE]]
    shard_a = jnp.concatenate(shard_a, axis=1)
    rest = 3 * width + 2 * hidden - TABLE
    shard_b = [shard[:, TABLE:width], shard[:, mod_at:tail_at]] + empty(up_to(rest, TABLE * n_dp) - rest)
    shard_b = jnp.concatenate(shard_b, axis=1)
    if blocked:
        me, my_z = lax.axis_index("dp"), lax.axis_index("z")
        split_b = shard_b.shape[1] // n_dp
        mine_b = lax.dynamic_slice_in_dim(shard_b, me * split_b, split_b, 1)

        def over_z(part):
            return [part] + [over(part, "z", step) for step in range(1, n_z)]

        def over_dp(part):
            return [part] + [over(part, "dp", step) for step in range(1, n_dp)]

        def with_core(parts):
            return [one for part in parts for one in (part, over(part, "core", 1))]

        all_b, all_a = over_z(mine_b), over_z(shard_a)
        near = min(1, n_z - 1)
        all_b[near], x_big, x_small, cot_big, cot_small = lax.optimization_barrier(
            (all_b[near], x_big, x_small, cot_big, cot_small)
        )
        stack_b = jnp.stack(all_b)
        x_rows, wl = table_of_x(x_big, x_small), table_of_cot(cot_big, cot_small, counts)
        wl, stack_b = lax.optimization_barrier((wl, stack_b))
        pieces_b = over_dp(stack_b)
        *all_a, x_rows, stack_b = lax.optimization_barrier((*all_a, x_rows, stack_b))
        pieces_a = with_core(all_a)
    else:
        x_rows, wl = table_of_x(x_big, x_small), table_of_cot(cot_big, cot_small, counts)
        pieces_a, pieces_b = ([lax.all_gather(part, fsdp, axis=0, tiled=True)] for part in (shard_a, shard_b))
    if blocked:
        share1 = Shares(sizes, width, 3 * width + 2 * hidden)
        share3 = Blocks(sizes, width, width + TABLE)
    else:
        share1, share3 = Plain(width, 3 * width + 2 * hidden), Plain(width, width + TABLE)

    one = mix_forward(plan, consts, x_rows, pieces_a, sizes)
    if blocked:
        *rest_b, one["mixed"] = lax.optimization_barrier((*pieces_b[1:], one["mixed"]))
        pieces_b = with_core(pieces_b[:1]) + with_core(rest_b)
    mid = middle_pass(plan, consts, share1, x_rows, wl, one, pieces_b, sizes)
    if blocked:
        got = over(mid["give"], "core", 1)
        pick = lambda table, index: lax.dynamic_index_in_dim(table, index, 0, keepdims=False)
        part_of = lambda step: pick(mid["keep"], me ^ step) + pick(got, me ^ step)
        by_dp = [part_of(0)] + [over(part_of(step), "dp", step) for step in range(1, n_dp)]
    mix = mix_backward(plan, consts, share3, one, mid)
    if not blocked:
        end = input_pass(plan, x_rows, one, mid, mix)
        images = from_rows(plan, mid["out"], x_big.shape, x_small.shape)
        images += from_rows(plan, end["gx"], x_big.shape, x_small.shape)
        grads, square = whole_sums(plan, sizes, tail, mix["keep"], mid["keep"], width + TABLE)
        grad_norm = jnp.sqrt(square)
        scale = jnp.minimum(1.0, CLIP_NORM / (grad_norm + 1e-06))
        return images + adam_rows(params, grads, first, second, scale) + (grad_norm,)
    count = n_dp * n_z * n_core
    *by_dp, last = lax.optimization_barrier((*by_dp, mix["keep"]))
    summed = sum(part.astype(F32) for part in by_dp).astype(BF16)
    sent = [pick(summed, my_z ^ step) for step in range(n_z)]
    *sent, last, mix["glow"] = lax.optimization_barrier((*sent, last, mix["glow"]))
    both = lax.all_to_all(last.reshape(count, height, share3.part), everywhere, 0, 0)
    by_z = [sent[0]] + [over(sent[step], "z", step) for step in range(1, n_z)]
    end = input_pass(plan, x_rows, one, mid, mix)
    *by_z, end["gx"] = lax.optimization_barrier((*by_z, end["gx"]))
    early = sum(part.astype(F32) for part in by_z).astype(BF16)
    owned = [early] + [over(early, "dp", step) for step in range(1, n_dp)]
    grad_images = from_rows(plan, end["gx"], x_big.shape, x_small.shape)
    near = min(1, n_dp - 1)
    outs = from_rows(plan, mid["out"], x_big.shape, x_small.shape)
    both, owned[near], *rest = lax.optimization_barrier((both, owned[near], *outs, *grad_images))
    outs, grad_images = rest[:2], rest[2:]
    sums = run(
        late_sums,
        dict(both=both, early=owned[0]),
        dict(late=((height, share3.part), BF16), wide=((count, 8, TABLE), F32)),
        {},
        micros=2,
        limit=4 * 2**20,
    )
    wide = lax.all_to_all(sums["wide"], everywhere, 0, 0)
    late = [sums["late"]] + [over(sums["late"], "dp", step) for step in range(1, n_dp)]
    images = tuple(outs) + tuple(grad_images)
    state = ((height, params.shape[1]), F32)
    inputs = dict({"o" + str(step): part for step, part in enumerate(owned)}, wide=wide)
    inputs.update({"l" + str(step): part for step, part in enumerate(late)})
    new = run(
        partial(optimizer, plan, sizes, (share1.part, share3.part), tail),
        dict(inputs, params=params, first=first, second=second),
        dict(new_params=state, new_first=state, new_second=state, norm=((1, 1), F32)),
        dict(
            by_dp=((n_dp, height, share1.part + share3.part), F32),
            flat=((height, up_to(params.shape[1], TABLE)), F32),
        ),
        micros=3,
        limit=16 * 2**20,
    )
    return tuple(images) + (new["new_params"], new["new_first"], new["new_second"], new["norm"].reshape(()))


def solution(mesh):
    n_dp, n_fsdp = mesh.shape["dp"], mesh.shape["fsdp"]
    n_core = 2 if n_fsdp % 2 == 0 else 1
    n_z = n_fsdp // n_core
    split = jax.sharding.Mesh(mesh.devices.reshape(n_dp, n_z, n_core), ("dp", "z", "core"))
    images = P(("dp", "z", "core"), None, None, None)
    rows = P(("z", "core"), None)
    in_specs = (images,) * 4 + (P("dp", ("z", "core"), None),) + (rows,) * 3
    out_specs = (images,) * 4 + (rows,) * 3 + (P(),)
    return jax.shard_map(
        partial(local, (n_dp, n_z, n_core)), mesh=split, in_specs=in_specs, out_specs=out_specs, check_vma=False
    )
```

```python
from functools import partial

import jax
import jax.numpy as jnp
import numpy as np
from jax import lax
from jax.experimental import pallas as pl
from jax.experimental.pallas import tpu as pltpu
from jax.sharding import PartitionSpec as P

FFN = 1536
STEP = 10
CLIP_NORM = 1.0
BETA_ONE = 0.9
BETA_TWO = 0.999
LEARN_RATE = 0.05
DECAY_RATE = 0.05
ADAM_EPS = 1e-08
KERNEL_SIDES = (3, 5, 7)
F32 = jnp.float32
BF16 = jnp.bfloat16
VMEM_BYTES = 58 * 2**20

SLOT = 16


def up_to(value, step):
    return -(-value // step) * step


class Plan:
    def __init__(self, big_shape, small_shape):
        self.n_big, self.side_big = big_shape[0], big_shape[1]
        self.n_small, self.side_small = small_shape[0], small_shape[1]
        self.width = big_shape[3]
        self.pix_big = self.side_big**2
        self.pix_small = self.side_small**2
        self.rows_big = up_to(self.pix_big, SLOT)
        self.group = max(size for size in (1, 2, 3) if self.n_small % size == 0)
        self.n_groups = self.n_small // self.group
        self.rows_small = up_to(self.group * self.pix_small, SLOT)
        self.small_at = self.n_big * self.rows_big
        self.used = self.small_at + self.n_groups * self.rows_small
        self.rows = up_to(self.used, 256)
        self.n_images = self.n_big + self.n_small
        self.image_rows = up_to(self.n_images, SLOT)


def half_spectrum(size):
    reps = []
    for u in range(size):
        for v in range(size):
            other = ((-u) % size, (-v) % size)
            if (u, v) <= other:
                reps.append((u, v, 1.0 if (u, v) == other else 2.0))
    return np.array(reps)


def transform_pair(side, kernel_side, copies):
    margin = kernel_side // 2
    size = side + margin
    reps = half_spectrum(size)
    count = len(reps)
    freq = 2 * np.pi * reps[:, :2] / size
    grid = np.array([(i, j) for i in range(side) for j in range(side)], float)
    lags = np.array([(i - margin, j - margin) for i in range(kernel_side) for j in range(kernel_side)], float)
    phase = freq @ grid.T
    lag_phase = freq @ lags.T
    weight = reps[:, 2:3] / size**2
    pix = side * side
    half = up_to(copies * count, SLOT)
    rows = up_to(copies * pix, SLOT)
    forward = np.zeros((2 * half, rows))
    inverse = np.zeros((rows, 2 * half))
    taps = np.zeros((2 * half, kernel_side**2))
    back = np.zeros((kernel_side**2, 2 * half))
    for one in range(copies):
        low, col = one * count, one * pix
        forward[low : low + count, col : col + pix] = np.cos(phase)
        forward[half + low : half + low + count, col : col + pix] = -np.sin(phase)
        inverse[col : col + pix, low : low + count] = (weight * np.cos(phase)).T
        inverse[col : col + pix, half + low : half + low + count] = -(weight * np.sin(phase)).T
        taps[low : low + count] = np.cos(lag_phase)
        taps[half + low : half + low + count] = np.sin(lag_phase)
        back[:, low : low + count] = (weight * np.cos(lag_phase)).T
        back[:, half + low : half + low + count] = -(weight * np.sin(lag_phase)).T
    return forward, inverse, taps, back


TABLE = 128
LAG = 1
GATES_AT = 0
TAPS_AT = 4
VECS_AT = 87
BIAS_AT = 96


def low_np(values):
    return jnp.asarray(values, F32).astype(BF16)


def high_and_rest(values):
    high = values.astype(np.float32).astype(jnp.bfloat16)
    rest = (values - high.astype(np.float64)).astype(np.float32).astype(jnp.bfloat16)
    return jnp.asarray(high), jnp.asarray(rest)


def constants(plan):
    consts = {}
    tap_at = TAPS_AT
    for level, kernel_side in enumerate(KERNEL_SIDES):
        for kind, side, copies in (("b", plan.side_big, 1), ("s", plan.side_small, plan.group)):
            forward, inverse, taps, back = transform_pair(side, kernel_side, copies)
            wide = np.zeros((taps.shape[0], TABLE))
            wide[:, tap_at : tap_at + kernel_side**2] = taps
            tall = np.zeros((TABLE, taps.shape[0]))
            tall[tap_at : tap_at + kernel_side**2] = back
            consts["f" + kind + str(level)] = low_np(forward)
            consts["g" + kind + str(level)] = low_np(inverse)
            high, rest = high_and_rest(wide)
            consts["k" + kind + str(level)] = jnp.concatenate([high, rest], axis=1)
            consts["t" + kind + str(level)] = low_np(tall)
        tap_at += kernel_side**2
    pick = np.zeros((plan.image_rows, plan.rows))
    for one in range(plan.n_big):
        pick[one, one * plan.rows_big : one * plan.rows_big + plan.pix_big] = 1.0
    for one in range(plan.n_small):
        at = plan.small_at + one // plan.group * plan.rows_small + one % plan.group * plan.pix_small
        pick[plan.n_big + one, at : at + plan.pix_small] = 1.0
    consts["pick"] = low_np(pick)
    consts["spread"] = low_np(pick.T)
    consts["eye"] = low_np(np.eye(TABLE))
    lanes = np.zeros((FFN, plan.width))
    lanes[np.arange(FFN), np.arange(FFN) // (FFN // plan.width)] = 1.0
    consts["lanes"] = low_np(lanes)
    return consts


def dot(left, right):
    return jnp.dot(left, right, preferred_element_type=F32)


def dot_nt(left, right):
    return lax.dot_general(left, right, (((1,), (1,)), ((), ())), preferred_element_type=F32)


def dot_tn(left, right):
    return lax.dot_general(left, right, (((0,), (0,)), ((), ())), preferred_element_type=F32)


def tiles(low, high, step):
    for at in range(low, high, step):
        yield slice(at, min(at + step, high))


def gelu_and_slope(values):
    chance = 0.5 + 0.5 * lax.erf(values * 0.7071067811865476)
    bell = jnp.exp(values * values * -0.5) * 0.3989422804014327
    return values * chance, chance + values * bell


class Refs(dict):
    def __getattr__(self, name):
        return self[name]

    def setup(self, fetched, sent):
        self.used = 0
        self.open = {}
        self.leaving = []
        self.sent = sent
        self.waiting = dict(fetched)

    def plan(self, source, target):
        self.used += 1
        return pltpu.make_async_copy(source, target, self["sems"].at[self.used - 1])

    def copy(self, source, target):
        result = self.plan(source, target)
        result.start()
        return result

    def begin(self, *names):
        for name in names or tuple(self.waiting):
            source, lanes = self.waiting.pop(name)
            far = self[source] if lanes is None else self[source].at[:, lanes]
            self.open[name] = self.copy(far, self[name])

    def begin_parts(self, parts, *names, last=True):
        for part in parts:
            for name in names:
                source, _ = self.waiting[name]
                self.open[name, part.start] = self.copy(self[source].at[part], self[name].at[part])
        for name in names if last else ():
            self.waiting.pop(name)

    def need_part(self, part, *names):
        self.need(*((name, part.start) for name in names))

    def need(self, *names):
        for name in names:
            if name in self.open:
                self.open.pop(name).wait()

    def send(self, name, at=None):
        far, near = self["far_" + name], self[name]
        if at is not None:
            far, near = far.at[at], near.at[at]
        self.leaving.append(self.copy(near, far))

    def finish(self):
        self.need(*list(self.open))
        for copy in self.leaving:
            copy.wait()


COPIES = 128


def run(body, inputs, outputs, scratch, fetched=None, sent=(), far=(), micros=20, limit=VMEM_BYTES):
    fetched = {name: (name, None) if entry is None else entry for name, entry in (fetched or {}).items()}
    sources = {source for source, _ in fetched.values()}
    buffers = {}
    for name, (source, lanes) in fetched.items():
        shape = inputs[source].shape
        if lanes is not None:
            shape = (shape[0], lanes.stop - lanes.start)
        buffers["near_" + name] = (shape, inputs[source].dtype)
    for name in sent:
        buffers["near_" + name] = outputs[name]
    names = ["in_" + name for name in inputs] + ["out_" + name for name in outputs] + list(scratch) + list(buffers)

    def kernel(*args):
        given = dict(zip(names + ["sems"], args))
        refs = Refs()
        for name in inputs:
            refs[name] = given["in_" + name]
        for name in outputs:
            refs["far_" + name if name in sent else name] = given["out_" + name]
        for name in list(scratch) + ["sems"]:
            refs[name] = given[name]
        entries = {}
        for name, (source, lanes) in fetched.items():
            refs["source_" + source] = given["in_" + source]
            entries[name] = ("source_" + source, lanes)
        for name in list(fetched) + list(sent):
            refs[name] = given["near_" + name]
        refs.setup(entries, sent)
        body(refs)
        refs.finish()

    def space(name, distant):
        return pl.BlockSpec(memory_space=pl.ANY if distant else pltpu.VMEM)

    results = pl.pallas_call(
        kernel,
        in_specs=[space(name, name in sources or name in far) for name in inputs],
        out_specs=[
            pl.BlockSpec(memory_space=pltpu.SMEM) if shape == (1, 1) else space(name, name in sent or name in far)
            for name, (shape, _) in outputs.items()
        ],
        out_shape=[jax.ShapeDtypeStruct(shape, dtype) for shape, dtype in outputs.values()],
        scratch_shapes=[pltpu.VMEM(*entry) for entry in list(scratch.values()) + list(buffers.values())]
        + [pltpu.SemaphoreType.DMA((COPIES,))],
        compiler_params=pltpu.CompilerParams(vmem_limit_bytes=limit),
        cost_estimate=pl.CostEstimate(flops=micros * 10**9, bytes_accessed=micros * 10**6, transcendentals=0),
    )(*inputs.values())
    return dict(zip(outputs, results))


def units(plan):
    result = []
    for one in range(plan.n_big):
        result.append(("b", slice(one * plan.rows_big, (one + 1) * plan.rows_big), len(result)))
    for one in range(plan.n_groups):
        at = plan.small_at + one * plan.rows_small
        result.append(("s", slice(at, at + plan.rows_small), len(result)))
    return result


def pairs(plan):
    result = []
    for kind in "bs":
        same = [unit for unit in units(plan) if unit[0] == kind]
        result += [same[low : low + 2] for low in range(0, len(same), 2)]
    return result


def staggered(chains, lag):
    turn, live = 0, list(enumerate(chains))
    while live:
        left = []
        for index, chain in live:
            if turn < index * lag or next(chain, chains) is not chains:
                left.append((index, chain))
        live = left
        turn += 1


def side_by_side(values):
    return values[0] if len(values) == 1 else jnp.concatenate(values, axis=1)


def wave_rows(plan, consts):
    result, total = {}, []
    for level in range(3):
        at = 0
        for kind, _, index in units(plan):
            count = consts["f" + kind + str(level)].shape[0]
            result[level, index] = slice(at, at + count)
            at += count
        total.append(at)
    return result, total


def spectrum_of_taps(refs, name, table):
    refs["h" + name][...] = dot_nt(refs["k" + name][:, :TABLE], table) + dot_nt(refs["k" + name][:, TABLE:], table)


def image_scale(plan):
    row = lax.broadcasted_iota(jnp.int32, (plan.image_rows, 1), 0)
    return jnp.where(row < plan.n_big, 1.0 / plan.pix_big, 1.0 / plan.pix_small).astype(F32)


def unit_rows(values):
    center = values - jnp.mean(values, axis=-1, keepdims=True)
    scale = lax.rsqrt(jnp.mean(center * center, axis=-1, keepdims=True) + 1e-05)
    return center * scale, scale


def fold(values):
    total = values[0:8]
    for low in range(8, values.shape[0], 8):
        total = total + values[low : low + 8]
    return total


def column_sum(values):
    return jnp.sum(values, axis=0, keepdims=True)


def forward_mix(plan, places, sizes, n_pieces, refs):
    rows, width, hidden = plan.rows, plan.width, FFN
    arriving = sum(gather(refs, sizes, n_pieces, "wa"), [])
    start_all(arriving)
    refs.begin()
    wait_all(arriving)
    refs.send("wa")
    refs.need("eye")
    inner = width + TABLE
    table = refs.wa[:, width:inner]
    refs.vec[...] = dot_nt(refs.eye[...], table)
    refs.need("x")
    gain = refs.vec[VECS_AT : VECS_AT + 1, :]
    shift = refs.vec[VECS_AT + 1 : VECS_AT + 2, :]
    for block in tiles(0, rows, 256):
        for at in tiles(block.start, block.stop, 32):
            unit, _ = unit_rows(refs.x[at, :].astype(F32))
            refs.unit[at, :] = unit.astype(BF16)
            refs.normed[at, :] = (unit * gain + shift).astype(BF16)
        refs.send("normed", block)
        refs.send("unit", block)
        part = dot(refs.normed[block, :], refs.wa[:, :inner])
        refs.context[block, :] = (part[:, :width] + refs.vec[VECS_AT + 3 : VECS_AT + 4, :]).astype(BF16)
        refs.gate[block, :] = part[:, width:]
    refs.send("gate")
    if rows > plan.used:
        refs.c[:, plan.used :, :] = jnp.zeros((3, rows - plan.used, width), BF16)
        refs.gp[:, plan.used :, :] = jnp.zeros((3, rows - plan.used, width), BF16)
    ready, finished = set(), {level: 0 for level in range(3)}

    def chain(pair):
        for level in range(3):
            name = pair[0][0] + str(level)
            if name not in ready:
                ready.add(name)
                refs.need("f" + name, "k" + name, "g" + name)
                spectrum_of_taps(refs, name, table)
            hat = refs["hat" + str(level)]
            field_in = refs.context if level == 0 else refs.c.at[level - 1]
            count = refs["f" + name].shape[0]
            half = count // 2
            taps = refs["h" + name]
            both = dot(refs["f" + name][...], side_by_side([field_in[at, :] for _, at, _ in pair]))
            for place, (_, _, index) in enumerate(pair):
                refs.wave[index, :count, :] = both[:, place * width : (place + 1) * width]
            yield
            for _, _, index in pair:
                wave, low_wave = refs.wave.at[index], refs.wave_low.at[index]
                saved = places[level, index].start
                for re in tiles(0, half, 16):
                    im = slice(half + re.start, half + re.stop)
                    wave_re, wave_im = wave[re, :], wave[im, :]
                    tap_re, tap_im = taps[re, :], taps[im, :]
                    hat[saved + re.start : saved + re.stop, :] = wave_re.astype(BF16)
                    hat[saved + im.start : saved + im.stop, :] = wave_im.astype(BF16)
                    low_wave[re, :] = (wave_re * tap_re - wave_im * tap_im).astype(BF16)
                    low_wave[im, :] = (wave_re * tap_im + wave_im * tap_re).astype(BF16)
                yield
            both = dot(refs["g" + name][...], side_by_side([refs.wave_low[index, :count, :] for _, _, index in pair]))
            for place, (_, at, _) in enumerate(pair):
                refs.field[at, :] = both[:, place * width : (place + 1) * width]
            yield
            for _, at, _ in pair:
                for into in tiles(at.start, at.stop, 16):
                    value, slope = gelu_and_slope(refs.field[into, :])
                    refs.c[level, into, :] = value.astype(BF16)
                    refs.gp[level, into, :] = slope.astype(BF16)
                yield
            finished[level] += 1
            if finished[level] == len(pairs(plan)):
                refs.send("c", slice(level, level + 1))
                refs.send("gp", slice(level, level + 1))
                refs.send("hat" + str(level))

    staggered([chain(pair) for pair in pairs(plan)], LAG)
    refs.need("pick", "spread")
    mean = dot(refs.pick[...], refs.c[2]) * image_scale(plan)
    summary, slope = gelu_and_slope(mean)
    refs.sum[0] = summary
    refs.sum[1] = slope
    summary_low = summary.astype(BF16)
    for block in tiles(0, rows, 256):
        refs.field[block, :] = dot(refs.spread[block, :], summary_low)
        for at in tiles(block.start, block.stop, 32):
            gate = refs.gate[at, :]
            total = refs.field[at, :] * gate[:, 3:4]
            for level in range(3):
                total += refs.c[level, at, :].astype(F32) * gate[:, level : level + 1]
            refs.mixed[at, :] = total.astype(BF16)
        refs.send("mixed", block)
    refs.need("lanes")
    ratio = hidden // width
    spread = dot_nt(refs.vec[BIAS_AT : BIAS_AT + 16, :].astype(BF16), refs.lanes[...])
    row = lax.broadcasted_iota(jnp.int32, (16, hidden), 0)
    lane = lax.broadcasted_iota(jnp.int32, (16, hidden), 1)
    picked = jnp.where(lax.rem(lane, ratio) == row, spread, 0.0)
    refs.upb[...] = jnp.broadcast_to(jnp.sum(picked, axis=0, keepdims=True), (8, hidden))


def mix_scratch(plan, consts):
    scratch = {}
    for level in range(3):
        for kind in "bs":
            scratch["h" + kind + str(level)] = ((consts["f" + kind + str(level)].shape[0], plan.width), F32)
    return scratch


def most_waves(consts):
    return max(consts["f" + kind + str(level)].shape[0] for level in range(3) for kind in "bs")


def mix_forward(plan, consts, x_rows, pieces, sizes):
    rows, width = plan.rows, plan.width
    waves, n_units = most_waves(consts), len(units(plan))
    places, saved = wave_rows(plan, consts)
    keys = [k + kind + str(level) for level in range(3) for kind in "bs" for k in "fkg"]
    names = ["eye"] + keys + ["pick", "spread", "lanes"]
    inputs = dict(x=x_rows, **{k: consts[k] for k in names})
    apart = {"w" + str(step): piece for step, piece in enumerate(pieces)}
    inputs.update(apart)
    outputs = dict(
        wa=((width, width + 2 * TABLE), BF16),
        normed=((rows, width), BF16),
        unit=((rows, width), BF16),
        c=((3, rows, width), BF16),
        gp=((3, rows, width), BF16),
        **{"hat" + str(level): ((saved[level], width), BF16) for level in range(3)},
        mixed=((rows, width), BF16),
        gate=((rows, TABLE), F32),
        vec=((TABLE, width), F32),
        upb=((8, FFN), F32),
        sum=((2, plan.image_rows, width), F32),
    )
    scratch = dict(
        wave=((n_units, waves, width), F32),
        wave_low=((n_units, waves, width), BF16),
        field=((rows, width), F32),
        context=((rows, width), BF16),
        **mix_scratch(plan, consts),
    )
    sent = ("normed", "unit", "c", "gp", "hat0", "hat1", "hat2", "mixed", "gate")
    sent += ("wa",)
    body = partial(forward_mix, plan, places, sizes, len(pieces))
    return run(body, inputs, outputs, scratch, {k: None for k in ["x"] + names}, sent, list(apart), 2)


def gather(refs, sizes, n_pieces, target, base=0):
    n_dp, n_z, n_core = sizes
    if n_pieces == 1:
        return [[refs.plan(refs["w0"], refs[target].at[:, base:])]]
    me, my_z, my_core = (lax.axis_index(name) for name in ("dp", "z", "core"))

    def place(piece, z, step, lanes):
        height = piece.shape[0]
        owner = (my_z ^ z) * n_core + (my_core ^ (step % n_core))
        return refs.plan(piece, refs[target].at[pl.ds(pl.multiple_of(owner * height, 16), height), lanes])

    copies = [[] for _ in range(n_pieces // n_core)]
    for step in range(n_pieces):
        piece = refs["w" + str(step)]
        if len(piece.shape) == 2:
            copies[step // n_core].append(place(piece, step // n_core, step, slice(None)))
            continue
        part = piece.shape[2]
        lanes = pl.ds(base + pl.multiple_of((me ^ (step // n_core)) * part, TABLE), part)
        copies[step // n_core] += [place(piece.at[other], other, step, lanes) for other in range(n_z)]
    return copies


def for_quarter(copies, quarter, act):
    if len(copies) == 1:
        if quarter == 0:
            act(copies[0])
        return
    me = lax.axis_index("dp")
    for step, some in enumerate(copies):
        pl.when((me ^ step) == quarter)(partial(act, some))


def start_all(copies):
    for copy in copies:
        copy.start()


def wait_all(copies):
    for copy in copies:
        copy.wait()


class Shares:
    def __init__(self, sizes, rows, columns):
        self.n_dp, self.n_z, self.n_core = sizes
        self.height = rows // (self.n_z * self.n_core)
        self.part = up_to(columns, TABLE * self.n_dp) // self.n_dp
        self.empty = self.part * self.n_dp - columns
        self.shape = (self.n_core, self.n_dp, self.n_z, self.height, self.part)
        self.columns = columns

    def place(self, core, share, z):
        return (core, share, z)

    def put(self, ref, low, values):
        done = 0
        while done < values.shape[1]:
            share, at = divmod(low + done, self.part)
            take = min(self.part - at, values.shape[1] - done)
            for owner in range(self.n_z * self.n_core):
                z, core = divmod(owner, self.n_core)
                ref[self.place(core, share, z) + (slice(None), slice(at, at + take))] = values[
                    owner * self.height : (owner + 1) * self.height, done : done + take
                ]
            done += take

    def send(self, refs, stage, names, low, high):
        core = lax.axis_index("core")
        for share in range(self.n_dp):
            if low < (share + 1) * self.part <= high:
                for source, name in ((1 - core, names[1]), (core, names[0])):
                    refs.leaving.append(refs.copy(stage.at[source, share], refs[name].at[share]))

    def close(self, refs, stage, names):
        if self.empty:
            self.put(stage, self.columns, jnp.zeros((self.height * self.n_z * self.n_core, self.empty), BF16))
        self.send(refs, stage, names, self.columns, self.part * self.n_dp)


class Blocks(Shares):
    def __init__(self, sizes, rows, columns):
        super().__init__(sizes, rows, columns)
        self.shape = (self.n_dp, self.n_z, self.n_core, self.height, self.part)

    def place(self, core, share, z):
        return (share, z, core)

    def close(self, refs, stage, names):
        refs.leaving.append(refs.copy(stage, refs[names[0]]))


class Plain:
    def __init__(self, rows, columns):
        self.shape = (rows, columns)

    def put(self, ref, low, values):
        ref[:, low : low + values.shape[1]] = values

    def send(self, refs, stage, names, low, high):
        pass

    def close(self, refs, stage, names):
        refs.leaving.append(refs.copy(stage, refs[names[0]]))


def input_grads(product, sums, weight, table):
    gain = table[:, VECS_AT : VECS_AT + 1].astype(F32)
    shift = table[:, VECS_AT + 1 : VECS_AT + 2].astype(F32)
    weight = weight.astype(F32)
    lane = lax.broadcasted_iota(jnp.int32, (1, TABLE), 1)
    parts = jnp.where(lane == VECS_AT, jnp.sum(product * weight, axis=-1, keepdims=True), 0.0)
    parts = jnp.where(lane == VECS_AT + 1, jnp.sum(sums * weight, axis=-1, keepdims=True), parts)
    return gain * product + shift * sums, parts


def middle(plan, shares, sizes, n_pieces, refs):
    rows, width, hidden = plan.rows, plan.width, FFN
    vec = lambda index: refs.vec[VECS_AT + index : VECS_AT + index + 1, :]
    zero = jnp.zeros((8, width), F32)
    sums = {index: zero for index in (2, 4, 5, 6, 7, 8)}
    blocks = list(tiles(0, rows, 256))
    up_at = 3 * width
    down_at = up_at + hidden
    wq, wm, wo = (refs.wb.at[:, at * width : (at + 1) * width] for at in range(3))
    wu, wd = refs.wb.at[:, up_at:down_at], refs.wb.at[:, down_at : down_at + hidden]
    refs.begin("mixed", "normed")
    arriving = gather(refs, sizes, n_pieces, "wb", TABLE)
    first_tile = refs.copy(refs.wa.at[:, width + TABLE :], refs.wb.at[:, :TABLE])
    for quarter in range(sizes[0]):
        for_quarter(arriving, quarter, start_all)
    refs.begin()
    refs.need("mixed", "normed")
    first_tile.wait()
    for_quarter(arriving, 0, wait_all)

    def before(block):
        modulator = dot(refs.mixed[block, :], wm[...]) + vec(4)
        queries = dot(refs.normed[block, :], wq[...]) + vec(2)
        refs.mod[block, :] = modulator.astype(BF16)
        refs.q[block, :] = queries.astype(BF16)
        refs.prod[block, :] = (queries * modulator).astype(BF16)
        yield
        refs.need("x")
        refs.resid[block, :] = dot(refs.prod[block, :], wo[...])
        yield
        for part in tiles(block.start, block.stop, 64):
            for at in tiles(part.start, part.stop, 32):
                resid = refs.resid[at, :] + refs.x[at, :].astype(F32) + vec(5)
                refs.resid[at, :] = resid
                unit, scale = unit_rows(resid)
                refs.unit[at, :] = unit
                refs.scale[at, :] = jnp.broadcast_to(scale, (scale.shape[0], TABLE))
                refs.n2[at, :] = (unit * vec(6) + vec(7)).astype(BF16)
            yield

    def mlp(block):
        refs.need("wl")
        for index, lanes in enumerate(tiles(0, hidden, 256)):
            pre, grad_act = refs.pa.at[index % 3], refs.ga.at[index % 3]
            pre[...] = dot(refs.n2[block, :], wu[:, lanes])
            grad_act[...] = dot(refs.wl[block, :], wd[:, lanes])
            bias = refs.upb[0:1, lanes]
            total = jnp.zeros((8, 256), F32) if block.start == 0 else refs.gub[:, lanes]
            for low in tiles(0, 256, 16):
                at = slice(block.start + low.start, block.start + low.stop)
                value, slope = gelu_and_slope(pre[low, :] + bias)
                grad = grad_act[low, :] * slope
                refs.act[at, lanes] = value.astype(BF16)
                refs.pre[at, lanes] = grad.astype(BF16)
                total = total + fold(grad)
            refs.gub[:, lanes] = total
            yield

    def after(block):
        refs.gn[block, :] = dot_nt(refs.pre[block, :], wu[...])
        yield
        refs.out[block, :] = (refs.resid[block, :] + dot_nt(refs.act[block, :], wd[...]) + vec(8)).astype(BF16)
        refs.send("out", block)
        yield
        for part in tiles(block.start, block.stop, 128):
            for at in tiles(part.start, part.stop, 32):
                grad = refs.gn[at, :]
                unit = refs.unit[at, :]
                weighted = refs.wl[at, :].astype(F32)
                gained = grad * vec(6)
                mean_one = jnp.mean(gained, axis=-1, keepdims=True)
                mean_two = jnp.mean(gained * unit, axis=-1, keepdims=True)
                result = weighted + refs.scale[at, 0:1] * (gained - mean_one - unit * mean_two)
                refs.gres[at, :] = result
                refs.glow[at, :] = result.astype(BF16)
                for index, new in ((6, grad * unit), (7, grad), (5, result), (8, weighted)):
                    sums[index] = sums[index] + fold(new)
            yield
        refs.send("gres", block)
        refs.gn[block, :] = dot_nt(refs.glow[block, :], wo[...])
        yield
        for at in tiles(block.start, block.stop, 32):
            grad = refs.gn[at, :]
            grad_query = grad * refs.mod[at, :].astype(F32)
            grad_mod = grad * refs.q[at, :].astype(F32)
            refs.gq[at, :] = grad_query.astype(BF16)
            refs.gmod[at, :] = grad_mod.astype(BF16)
            for index, new in ((2, grad_query), (4, grad_mod)):
                sums[index] = sums[index] + fold(new)
        refs.send("gq", block)
        refs.gmix[block, :] = dot_nt(refs.gmod[block, :], wm[...]).astype(BF16)
        refs.send("gmix", block)
        yield

    def together(*steps):
        steps = list(steps)
        while steps:
            steps = [step for step in steps if next(step, refs) is not refs]

    together(before(blocks[0]))
    for quarter in range(1, sizes[0]):
        for_quarter(arriving, quarter, wait_all)
    refs.leaving.append(refs.copy(wq, refs.wq))
    for index in range(len(blocks) + 1):
        steps = []
        if index < len(blocks):
            steps.append(mlp(blocks[index]))
        if index + 1 < len(blocks):
            steps.append(before(blocks[index + 1]))
        if index:
            steps.append(after(blocks[index - 1]))
        together(*steps)
    names = ("keep", "give")

    def put(low, values):
        shares.put(refs.stage, low, values.astype(BF16))
        shares.send(refs, refs.stage, names, low, low + values.shape[1])

    for lanes in tiles(0, hidden, 256):
        put(lanes.start, dot_tn(refs.n2[...], refs.pre[:, lanes]))
    for lanes in tiles(0, hidden, 256):
        put(hidden + lanes.start, dot_tn(refs.wl[...], refs.act[:, lanes]))
    refs.need("unit_in", "table")
    product = dot_tn(refs.unit_in[...], refs.gq[...])
    product, refs.parts[...] = input_grads(product, column_sum(sums[2]), wq[...], refs.table[...])
    put(2 * hidden, product)
    put(2 * hidden + width, dot_tn(refs.mixed[...], refs.gmod[...]))
    put(2 * hidden + 2 * width, dot_tn(refs.prod[...], refs.glow[...]))
    shares.close(refs, refs.stage, names)
    refs.gv[...] = jnp.zeros(refs.gv.shape, F32)
    for index, total in sums.items():
        refs.gv[index : index + 1, :] = column_sum(total)
    ratio = hidden // width
    row = lax.broadcasted_iota(jnp.int32, (16, hidden), 0)
    lane = lax.broadcasted_iota(jnp.int32, (16, hidden), 1)
    picked = jnp.where(lax.rem(lane, ratio) == row, column_sum(refs.gub[...]), 0.0).astype(BF16)
    refs.need("lanes")
    refs.gv[16:32, :] = dot(picked, refs.lanes[...])


def kept(shares):
    if isinstance(shares, (Plain, Blocks)):
        return dict(keep=(shares.shape, BF16))
    return dict(keep=(shares.shape[1:], BF16), give=(shares.shape[1:], BF16))


def middle_pass(plan, consts, shares, x_rows, wl, first, pieces, sizes):
    rows, width, hidden = plan.rows, plan.width, FFN
    near = dict(mixed=first["mixed"], normed=first["normed"], x=x_rows, wl=wl, unit_in=first["unit"], lanes=consts["lanes"])
    apart = {"w" + str(step): piece for step, piece in enumerate(pieces)}
    inputs = dict(near, wa=first["wa"], vec=first["vec"], upb=first["upb"], **apart)
    fetched = dict({k: None for k in near}, table=("wa", slice(width, width + TABLE)))
    token, field, wide = ((rows, width), BF16), ((rows, width), F32), ((rows, hidden), BF16)
    outputs = dict(kept(shares), out=token, gq=token, gmix=token, gres=field)
    outputs.update(wq=((width, width), BF16), gv=((32, width), F32), parts=((width, TABLE), F32))
    scratch = dict(mod=token, q=token, prod=token, glow=token, gmod=token, n2=token)
    scratch.update(resid=field, unit=field, gn=field, act=wide, pre=wide)
    scratch.update(
        scale=((rows, TABLE), F32),
        pa=((3, 256, 256), F32),
        ga=((3, 256, 256), F32),
        gub=((8, hidden), F32),
        stage=(shares.shape, BF16),
        wb=((width, TABLE + up_to(3 * width + 2 * hidden - TABLE, TABLE * sizes[0])), BF16),
    )
    body = partial(middle, plan, shares, sizes, len(pieces))
    far = ["keep", "give", "wq", "wa"] + list(apart)
    return run(body, inputs, outputs, scratch, fetched, ("out", "gq", "gmix", "gres"), far, 26)


def backward_mix(plan, places, shares, refs):
    rows, width = plan.rows, plan.width
    refs.begin("gmix", "gate", "pick", "spread", "wa")
    for level in (2, 1, 0):
        refs.begin_parts([slice(level, level + 1)], "gp", last=level == 0)
        refs.begin(*(name for name in tuple(refs.waiting) if name.endswith(str(level))))
    refs.begin()
    refs.need("gmix", "gate")
    for at in tiles(0, rows, 32):
        refs.tmp[at, :] = (refs.gmix[at, :].astype(F32) * refs.gate[at, 3:4]).astype(BF16)
    refs.need("pick", "spread", "wa")
    table = refs.wa[:, width : width + TABLE]
    grad_summary = dot(refs.pick[...], refs.tmp[...]) * refs.sum[1] * image_scale(plan)
    grad_summary_low = grad_summary.astype(BF16)
    for block in tiles(0, rows, 256):
        refs.gc[block, :] = dot(refs.spread[block, :], grad_summary_low)
    summary_low = refs.sum[0].astype(BF16)
    lane = lax.broadcasted_iota(jnp.int32, (1, TABLE), 1)

    def gates(low, high):
        refs.need("c")
        refs.held[low:high, :] = dot(refs.spread[low:high, :], summary_low)
        for at in tiles(low, high, 32):
            grad = refs.gmix[at, :].astype(F32)
            result = jnp.where(lane == 3, jnp.sum(grad * refs.held[at, :], axis=-1, keepdims=True), 0.0)
            for level in range(3):
                part = jnp.sum(grad * refs.c[level, at, :].astype(F32), axis=-1, keepdims=True)
                result = jnp.where(lane == level, part, result)
            refs.ggate[at, :] = result.astype(BF16)

    ready, seen = set(), set()

    def chain(pair):
        for level in (2, 1, 0):
            kind = pair[0][0]
            name = kind + str(level)
            if name not in ready:
                ready.add(name)
                refs.need("f" + name, "k" + name, "g" + name, "hat" + str(level))
                spectrum_of_taps(refs, name, table)
            refs.need_part(slice(level, level + 1), "gp")
            hat = refs["hat" + str(level)]
            count = refs["f" + name].shape[0]
            half = count // 2
            taps, cross = refs["h" + name], refs["x" + name]
            for _, at, _ in pair:
                for into in tiles(at.start, at.stop, 16):
                    direct = refs.gmix[into, :].astype(F32) * refs.gate[into, level : level + 1]
                    grad = refs.gc[into, :] + direct
                    refs.tmp[into, :] = (grad * refs.gp[level, into, :].astype(F32)).astype(BF16)
            yield
            both = dot(refs["f" + name][...], side_by_side([refs.tmp[at, :] for _, at, _ in pair]))
            for place, (_, _, index) in enumerate(pair):
                refs.wave[index, :count, :] = both[:, place * width : (place + 1) * width]
            yield
            for re in tiles(0, half, 16):
                im = slice(half + re.start, half + re.stop)
                tap_re, tap_im = taps[re, :], taps[im, :]
                cross_re = cross_im = None
                for _, _, index in pair:
                    saved = places[level, index].start
                    wave_re = hat[saved + re.start : saved + re.stop, :].astype(F32)
                    wave_im = hat[saved + im.start : saved + im.stop, :].astype(F32)
                    grad_re, grad_im = refs.wave[index, re, :], refs.wave[index, im, :]
                    refs.wave_low[index, re, :] = (grad_re * tap_re + grad_im * tap_im).astype(BF16)
                    refs.wave_low[index, im, :] = (grad_im * tap_re - grad_re * tap_im).astype(BF16)
                    new_re = grad_re * wave_re + grad_im * wave_im
                    new_im = grad_re * wave_im - grad_im * wave_re
                    cross_re = new_re if cross_re is None else cross_re + new_re
                    cross_im = new_im if cross_im is None else cross_im + new_im
                if name in seen:
                    cross_re = cross_re + cross[re, :]
                    cross_im = cross_im + cross[im, :]
                cross[re, :] = cross_re
                cross[im, :] = cross_im
                if re.start == half // 32 * 16:
                    yield
            seen.add(name)
            yield
            both = dot(refs["g" + name][...], side_by_side([refs.wave_low[index, :count, :] for _, _, index in pair]))
            for place, (_, at, _) in enumerate(pair):
                refs.gc[at, :] = both[:, place * width : (place + 1) * width]
            yield

    def gate_chain():
        for block in tiles(0, rows, 256):
            gates(block.start, block.stop)
            yield

    chains = [chain(pair) for pair in pairs(plan)]
    staggered(chains + [gate_chain()], LAG)
    taps_total = jnp.zeros((TABLE, width), F32)
    for level in range(3):
        for kind in "bs":
            name = kind + str(level)
            refs.need("t" + name)
            taps_total = taps_total + dot(refs["t" + name][...], refs["x" + name][...].astype(BF16))
    refs.gtab[...] = taps_total
    if rows > plan.used:
        refs.gc[plan.used :, :] = jnp.zeros((rows - plan.used, width), F32)
    context_total = jnp.zeros((8, width), F32)
    for block in tiles(0, rows, 256):
        for at in tiles(block.start, block.stop, 32):
            grad = refs.gc[at, :]
            refs.glow[at, :] = grad.astype(BF16)
            context_total = context_total + fold(grad)
        refs.send("glow", block)
    refs.gtab[VECS_AT + 2 : VECS_AT + 3, :] = refs.gv[2:3, :]
    refs.gtab[VECS_AT + 3 : VECS_AT + 4, :] = column_sum(context_total)
    refs.gtab[VECS_AT + 4 : VECS_AT + 9, :] = refs.gv[4:9, :]
    refs.gtab[BIAS_AT : BIAS_AT + 4, :] = refs.gv[16:20, :]
    refs.need("unit", "eye")
    product = dot_tn(refs.unit[...], refs.glow[...])
    product, parts = input_grads(product, column_sum(context_total), refs.wa[:, :width], table)
    shares.put(refs.stage, 0, product.astype(BF16))
    gate_total = jnp.zeros((8, TABLE), F32)
    for at in tiles(0, rows, 64):
        gate_total = gate_total + fold(refs.ggate[at, :].astype(F32))
    small, more = input_grads(dot_tn(refs.unit[...], refs.ggate[...]), column_sum(gate_total), table, table)
    small = small + parts + more + refs.parts[...] + dot_tn(refs.gtab[...].astype(BF16), refs.eye[...])
    shares.put(refs.stage, width, small.astype(BF16))
    shares.close(refs, refs.stage, ("keep",))


def input_back(plan, refs):
    rows, width = plan.rows, plan.width
    blocks = list(tiles(0, rows, 256))
    refs.begin("wq", "wa")
    refs.begin_parts(blocks, "gq", "glow", "ggate", "x", "gres")
    refs.need("wq", "wa")
    gain = refs.vec[VECS_AT : VECS_AT + 1, :]
    for block in blocks:
        refs.need_part(block, "gq", "glow", "ggate", "x", "gres")
        refs.gc[block, :] = (
            dot_nt(refs.gq[block, :], refs.wq[...])
            + dot_nt(refs.glow[block, :], refs.wa[:, :width])
            + dot_nt(refs.ggate[block, :], refs.wa[:, width : width + TABLE])
        )
        for at in tiles(block.start, block.stop, 32):
            unit, scale_row = unit_rows(refs.x[at, :].astype(F32))
            gained = refs.gc[at, :] * gain
            mean_one = jnp.mean(gained, axis=-1, keepdims=True)
            mean_two = jnp.mean(gained * unit, axis=-1, keepdims=True)
            result = refs.gres[at, :] + scale_row * (gained - mean_one - unit * mean_two)
            refs.gx[at, :] = result.astype(BF16)
        refs.send("gx", block)


def mix_backward(plan, consts, shares, first, mid):
    rows, width = plan.rows, plan.width
    waves, n_units = most_waves(consts), len(units(plan))
    places, _ = wave_rows(plan, consts)
    keys = [k + kind + str(level) for level in (2, 1, 0) for k in "kfgt" for kind in "bs"]
    near = dict(gmix=mid["gmix"], gate=first["gate"], pick=consts["pick"], spread=consts["spread"], wa=first["wa"])
    near["gp"] = first["gp"]
    for level in (2, 1, 0):
        near.update({name: consts[name] for name in keys if name.endswith(str(level))})
        near["hat" + str(level)] = first["hat" + str(level)]
        near["c"] = first["c"]
    near.update(unit=first["unit"], eye=consts["eye"])
    inputs = dict(near, sum=first["sum"], gv=mid["gv"], parts=mid["parts"])
    outputs = dict(kept(shares), glow=((rows, width), BF16), ggate=((rows, TABLE), BF16))
    scratch = dict(
        wave=((n_units, waves, width), F32),
        wave_low=((n_units, waves, width), BF16),
        **{k.replace("f", "x"): ((consts[k].shape[0], width), F32) for k in keys if k[0] == "f"},
        gc=((rows, width), F32),
        held=((rows, width), F32),
        tmp=((rows, width), BF16),
        gtab=((TABLE, width), F32),
        stage=(shares.shape, BF16),
        **mix_scratch(plan, consts),
    )
    body = partial(backward_mix, plan, places, shares)
    return run(body, inputs, outputs, scratch, {k: None for k in near}, ("glow",), ("keep",), 18)


def input_pass(plan, x_rows, first, mid, mix):
    rows, width = plan.rows, plan.width
    near = dict(glow=mix["glow"], wa=first["wa"], ggate=mix["ggate"], wq=mid["wq"], gq=mid["gq"], x=x_rows)
    near["gres"] = mid["gres"]
    inputs = dict(near, vec=first["vec"])
    outputs = dict(gx=((rows, width), BF16))
    scratch = dict(gc=((rows, width), F32))
    return run(partial(input_back, plan), inputs, outputs, scratch, {k: None for k in near}, ("gx",), micros=7)


def adam_rows(params, grads, first, second, scale):
    clipped = grads * scale
    first_new = BETA_ONE * first + (1.0 - BETA_ONE) * clipped
    second_new = BETA_TWO * second + (1.0 - BETA_TWO) * clipped * clipped
    first_hat = first_new * (1.0 / (1.0 - BETA_ONE**STEP))
    second_hat = second_new * (1.0 / (1.0 - BETA_TWO**STEP))
    params_new = params - LEARN_RATE * (first_hat / (jnp.sqrt(second_hat) + ADAM_EPS) + DECAY_RATE * params)
    return (params_new, first_new, second_new)


def to_rows(plan, big, small):
    tables = []
    for images, count, pix, rows in (
        (big, plan.n_big, plan.pix_big, plan.rows_big),
        (small, plan.n_groups, plan.group * plan.pix_small, plan.rows_small),
    ):
        table = jnp.pad(images.reshape(count, pix, plan.width), ((0, 0), (0, rows - pix), (0, 0)))
        tables.append(table.reshape(count * rows, plan.width))
    if plan.rows > plan.used:
        tables.append(jnp.zeros((plan.rows - plan.used, plan.width), big.dtype))
    return jnp.concatenate(tables, axis=0)


def from_rows(plan, table, big_shape, small_shape):
    big = table[: plan.small_at].reshape(plan.n_big, plan.rows_big, plan.width)[:, : plan.pix_big]
    small = table[plan.small_at : plan.used].reshape(plan.n_groups, plan.rows_small, plan.width)
    return big.reshape(big_shape), small[:, : plan.group * plan.pix_small].reshape(small_shape)


def whole_sums(plan, sizes, tail, late, early, late_columns):
    fsdp = ("z", "core")
    width, hidden = plan.width, FFN
    rows = late.shape[0]
    table = jnp.concatenate([late[:, :late_columns], early], axis=1)
    if sizes[1] * sizes[2] > 1:
        table = lax.psum_scatter(table, fsdp, scatter_dimension=0, tiled=True)
    table = lax.psum(table, "dp").astype(F32)
    ups, rest = late_columns, late_columns + 2 * hidden
    grads = jnp.concatenate(
        [
            table[:, rest : rest + width],
            table[:, : width + 4],
            table[:, rest + width :],
            table[:, ups:rest],
            table[:, width + 4 : width + 4 + tail],
        ],
        axis=1,
    )
    return grads, lax.psum(jnp.sum(grads * grads), fsdp)


def late_sums(refs):
    late = refs.both[0].astype(F32)
    for index in range(1, refs.both.shape[0]):
        late = late + refs.both[index].astype(F32)
    late = late.astype(BF16)
    refs.late[...] = late
    square = jnp.sum(jnp.square(refs.early[...].astype(F32))) + jnp.sum(jnp.square(late.astype(F32)))
    refs.wide[...] = jnp.full(refs.wide.shape, square, F32)


def optimizer(plan, sizes, parts, tail, refs):
    n_dp = sizes[0]
    row_blocks = list(tiles(0, refs.params.shape[0], 16))
    part1, part3 = parts
    width, hidden = plan.width, FFN
    me = lax.axis_index("dp")
    split = part1
    for step in range(n_dp):
        at = pl.ds(me ^ step, 1)
        refs.by_dp[at, :, :split] = refs["o" + str(step)][...].astype(F32)[None]
        refs.by_dp[at, :, split:] = refs["l" + str(step)][...].astype(F32)[None]
    blocks = [refs.by_dp[index] for index in range(n_dp)]
    cut = lambda low, high: jnp.concatenate([block[:, low:high] for block in blocks], axis=1)
    early = cut(0, part1)
    lates = cut(part1, part1 + part3)
    table = lates[:, width : width + TABLE]
    mids = 2 * hidden + width
    refs.flat[:, :width] = early[:, 2 * hidden : mids]
    refs.flat[:, width : 2 * width] = lates[:, :width]
    moved = [early[:, mids : mids + 2 * width], early[:, : 2 * hidden], pltpu.roll(table, TABLE - 4, 1)]
    moved = jnp.concatenate(moved, axis=1)
    refs.flat[:, 2 * width :] = pltpu.roll(moved, 4, 1)
    total = refs.wide[0]
    for index in range(1, refs.wide.shape[0]):
        total = total + refs.wide[index]
    norm = jnp.sqrt(total)
    refs.norm[0, 0] = norm[0, 0]
    scale = jnp.minimum(1.0, CLIP_NORM / (norm[0:1, 0:1] + 1e-06))
    columns = refs.params.shape[1]
    for block in row_blocks:
        for lanes in tiles(0, columns, 512):
            state = (refs.flat[block, lanes], refs.first[block, lanes], refs.second[block, lanes])
            new = adam_rows(refs.params[block, lanes], *state, scale)
            refs.new_params[block, lanes], refs.new_first[block, lanes], refs.new_second[block, lanes] = new
        for name in ("new_params", "new_first", "new_second"):
            refs.send(name, block)


def local(sizes, x_big, x_small, cot_big, cot_small, counts, params, first, second):
    n_dp, n_z, n_core = sizes
    fsdp = ("z", "core")
    everywhere = ("dp",) + fsdp
    width = x_big.shape[-1]
    hidden = FFN
    plan = Plan(x_big.shape, x_small.shape)
    consts = constants(plan)
    height = params.shape[0]
    mod_at = 2 * width + 4
    tail_at = mod_at + 2 * width + 2 * hidden
    tail = params.shape[1] - tail_at
    power = all(size & (size - 1) == 0 for size in sizes)
    blocked = height % 16 == 0 and n_core == 2 and power and n_dp <= 4 and n_z <= 4

    def over(part, axis, step):
        return lax.ppermute(part, axis, [(index, index ^ step) for index in range(sizes[axis_of[axis]])])

    axis_of = dict(dp=0, z=1, core=2)
    def table_of_x(x_big, x_small):
        return to_rows(plan, x_big, x_small)

    def table_of_cot(cot_big, cot_small, counts):
        count_pair = counts.reshape(2)
        live_big = (jnp.arange(cot_big.shape[0]) < count_pair[0]).astype(BF16)
        live_small = (jnp.arange(cot_small.shape[0]) < count_pair[1]).astype(BF16)
        return to_rows(plan, cot_big * live_big[:, None, None, None], cot_small * live_small[:, None, None, None])

    shard = params.astype(BF16)
    empty = lambda columns: [jnp.zeros((height, columns), BF16)]
    shard_a = [shard[:, width:mod_at], shard[:, tail_at:]] + empty(TABLE - 4 - tail) + [shard[:, :TABLE]]
    shard_a = jnp.concatenate(shard_a, axis=1)
    rest = 3 * width + 2 * hidden - TABLE
    shard_b = [shard[:, TABLE:width], shard[:, mod_at:tail_at]] + empty(up_to(rest, TABLE * n_dp) - rest)
    shard_b = jnp.concatenate(shard_b, axis=1)
    if blocked:
        me, my_z = lax.axis_index("dp"), lax.axis_index("z")
        split_b = shard_b.shape[1] // n_dp
        mine_b = lax.dynamic_slice_in_dim(shard_b, me * split_b, split_b, 1)

        def over_z(part):
            return [part] + [over(part, "z", step) for step in range(1, n_z)]

        def over_dp(part):
            return [part] + [over(part, "dp", step) for step in range(1, n_dp)]

        def with_core(parts):
            return [one for part in parts for one in (part, over(part, "core", 1))]

        all_b, all_a = over_z(mine_b), over_z(shard_a)
        near = min(1, n_z - 1)
        all_b[near], x_big, x_small, cot_big, cot_small = lax.optimization_barrier(
            (all_b[near], x_big, x_small, cot_big, cot_small)
        )
        stack_b = jnp.stack(all_b)
        x_rows, wl = table_of_x(x_big, x_small), table_of_cot(cot_big, cot_small, counts)
        wl, stack_b = lax.optimization_barrier((wl, stack_b))
        pieces_b = over_dp(stack_b)
        *all_a, x_rows, stack_b = lax.optimization_barrier((*all_a, x_rows, stack_b))
        pieces_a = with_core(all_a)
    else:
        x_rows, wl = table_of_x(x_big, x_small), table_of_cot(cot_big, cot_small, counts)
        pieces_a, pieces_b = ([lax.all_gather(part, fsdp, axis=0, tiled=True)] for part in (shard_a, shard_b))
    if blocked:
        share1 = Shares(sizes, width, 3 * width + 2 * hidden)
        share3 = Blocks(sizes, width, width + TABLE)
    else:
        share1, share3 = Plain(width, 3 * width + 2 * hidden), Plain(width, width + TABLE)

    one = mix_forward(plan, consts, x_rows, pieces_a, sizes)
    if blocked:
        *rest_b, one["mixed"] = lax.optimization_barrier((*pieces_b[1:], one["mixed"]))
        pieces_b = with_core(pieces_b[:1]) + with_core(rest_b)
    mid = middle_pass(plan, consts, share1, x_rows, wl, one, pieces_b, sizes)
    if blocked:
        got = over(mid["give"], "core", 1)
        pick = lambda table, index: lax.dynamic_index_in_dim(table, index, 0, keepdims=False)
        part_of = lambda step: pick(mid["keep"], me ^ step) + pick(got, me ^ step)
        by_dp = [part_of(0)] + [over(part_of(step), "dp", step) for step in range(1, n_dp)]
    mix = mix_backward(plan, consts, share3, one, mid)
    if not blocked:
        end = input_pass(plan, x_rows, one, mid, mix)
        images = from_rows(plan, mid["out"], x_big.shape, x_small.shape)
        images += from_rows(plan, end["gx"], x_big.shape, x_small.shape)
        grads, square = whole_sums(plan, sizes, tail, mix["keep"], mid["keep"], width + TABLE)
        grad_norm = jnp.sqrt(square)
        scale = jnp.minimum(1.0, CLIP_NORM / (grad_norm + 1e-06))
        return images + adam_rows(params, grads, first, second, scale) + (grad_norm,)
    count = n_dp * n_z * n_core
    *by_dp, last = lax.optimization_barrier((*by_dp, mix["keep"]))
    summed = sum(part.astype(F32) for part in by_dp).astype(BF16)
    sent = [pick(summed, my_z ^ step) for step in range(n_z)]
    *sent, last, mix["glow"] = lax.optimization_barrier((*sent, last, mix["glow"]))
    both = lax.all_to_all(last.reshape(count, height, share3.part), everywhere, 0, 0)
    by_z = [sent[0]] + [over(sent[step], "z", step) for step in range(1, n_z)]
    end = input_pass(plan, x_rows, one, mid, mix)
    *by_z, end["gx"] = lax.optimization_barrier((*by_z, end["gx"]))
    early = sum(part.astype(F32) for part in by_z).astype(BF16)
    owned = [early] + [over(early, "dp", step) for step in range(1, n_dp)]
    grad_images = from_rows(plan, end["gx"], x_big.shape, x_small.shape)
    near = min(1, n_dp - 1)
    outs = from_rows(plan, mid["out"], x_big.shape, x_small.shape)
    both, owned[near], *rest = lax.optimization_barrier((both, owned[near], *outs, *grad_images))
    outs, grad_images = rest[:2], rest[2:]
    sums = run(
        late_sums,
        dict(both=both, early=owned[0]),
        dict(late=((height, share3.part), BF16), wide=((count, 8, TABLE), F32)),
        {},
        micros=2,
        limit=4 * 2**20,
    )
    wide = lax.all_to_all(sums["wide"], everywhere, 0, 0)
    late = [sums["late"]] + [over(sums["late"], "dp", step) for step in range(1, n_dp)]
    images = tuple(outs) + tuple(grad_images)
    state = ((height, params.shape[1]), F32)
    inputs = dict({"o" + str(step): part for step, part in enumerate(owned)}, wide=wide)
    inputs.update({"l" + str(step): part for step, part in enumerate(late)})
    new = run(
        partial(optimizer, plan, sizes, (share1.part, share3.part), tail),
        dict(inputs, params=params, first=first, second=second),
        dict(new_params=state, new_first=state, new_second=state, norm=((1, 1), F32)),
        dict(
            by_dp=((n_dp, height, share1.part + share3.part), F32),
            flat=((height, up_to(params.shape[1], TABLE)), F32),
        ),
        sent=("new_params", "new_first", "new_second"),
        micros=3,
        limit=16 * 2**20,
    )
    return tuple(images) + (new["new_params"], new["new_first"], new["new_second"], new["norm"].reshape(()))


def solution(mesh):
    n_dp, n_fsdp = mesh.shape["dp"], mesh.shape["fsdp"]
    n_core = 2 if n_fsdp % 2 == 0 else 1
    n_z = n_fsdp // n_core
    split = jax.sharding.Mesh(mesh.devices.reshape(n_dp, n_z, n_core), ("dp", "z", "core"))
    images = P(("dp", "z", "core"), None, None, None)
    rows = P(("z", "core"), None)
    in_specs = (images,) * 4 + (P("dp", ("z", "core"), None),) + (rows,) * 3
    out_specs = (images,) * 4 + (rows,) * 3 + (P(),)
    return jax.shard_map(
        partial(local, (n_dp, n_z, n_core)), mesh=split, in_specs=in_specs, out_specs=out_specs, check_vma=False
    )
```
